32 devices in a mesh: dp: 4 (over y, x), exp: 2 (over core), col: 4 (over z).
Axes of the slice: x: 2, y: 2, z: 4, core: 2. Of those that a mesh axis runs over, the one named last changes fastest.
Arguments:
- inputs: bfloat16 [8192, 2048], P(('dp', 'exp', 'col')), may hold values from -6 to 6
- expert_ids: int32 [8192, 8], P(('dp', 'exp', 'col')), may hold values from 0 to 31, all different within a row; in each aligned block of 256 rows (0 to 255, 256 to 511, ...) at most 80 rows name the same one
- positions: int32 [8192], P(('dp', 'exp')), may hold values from 0 to 3069, as said below
- cotangent: bfloat16 [8192, 2048], P(('dp', 'exp', 'col')), may hold values from -6 to 6
- attn_gain: float32 [2048], replicated, may hold values from 0.5 to 1.5
- query_proj: bfloat16 [2048, 4096], P('exp', 'col'), may hold values from -0.125 to 0.125
- key_projection: bfloat16 [2048, 512], P('exp', 'col'), may hold values from -0.125 to 0.125
- value_projection: bfloat16 [2048, 512], P('exp', 'col'), may hold values from -0.125 to 0.125
- query_norm_gain: float32 [128], replicated, may hold values from 1 to 2
- key_norm_gain: float32 [128], replicated, may hold values from 1 to 2
- out_proj: bfloat16 [2048, 4096], P('exp', 'col'), may hold values from -0.5 to 0.5
- moe_gain: float32 [2048], replicated, may hold values from 0.5 to 1.5
- router: bfloat16 [2048, 32], replicated, may hold values from -0.0625 to 0.0625
- gate_proj: bfloat16 [32, 2048, 768], P(('dp', 'exp', 'col')), may hold values from -0.125 to 0.125
- up_proj: bfloat16 [32, 2048, 768], P(('dp', 'exp', 'col')), may hold values from -0.125 to 0.125
- down_proj: bfloat16 [32, 768, 2048], P(('dp', 'exp', 'col')), may hold values from -0.875 to 0.875
Outputs:
- outputs: bfloat16 [8192, 2048], P(('dp', 'exp', 'col'))
- grad_inputs: bfloat16 [8192, 2048], P(('dp', 'exp', 'col'))
- grad_attn_gain: float32 [2048], replicated
- grad_query_proj: float32 [2048, 4096], P(('dp', 'exp'), 'col')
- grad_key_proj: float32 [2048, 512], P(('dp', 'exp'), 'col')
- grad_value_proj: float32 [2048, 512], P(('dp', 'exp'), 'col')
- grad_query_gain: float32 [128], replicated
- grad_key_gain: float32 [128], replicated
- grad_out_proj: float32 [2048, 4096], P(('dp', 'exp'), 'col')
- grad_moe_gain: float32 [2048], replicated
- grad_router: float32 [2048, 32], replicated
- grad_gate_proj: float32 [32, 2048, 768], P(('dp', 'exp', 'col'))
- grad_up_proj: float32 [32, 2048, 768], P(('dp', 'exp', 'col'))
- grad_down_proj: float32 [32, 768, 2048], P(('dp', 'exp', 'col'))
The draws below stay inside these ranges and needn't reach their ends.
Inputs may be any that keep to these rules, and one draw needn't show every extreme that they name: `expert_ids`: each row names 8 different experts. Among the rows of one device no expert is named by more than 80 rows, a bound that some block reaches of them. Within each sequence of 1024 tokens the positions start at 0 and rise by 1 to 3 from one token to the next; in one sequence every rise is 3.
All inputs are finite; a program needn't handle non-finite values.
Results may differ from the reference program's by a relative error of at most 0.025.
Values may be sent and summed in bfloat16 or wider, within the bound.
No kernel may reach another device: no remote copies, remote signals or barrier semaphores. Data moves between devices by JAX's collectives and lax.ppermute only.
A program may use at most 256 MiB of HBM per device.

```python
import math
import jax
import jax.numpy as jnp
import numpy as np
from jax import lax

MODEL_DIMENSION = 2048
QUERY_HEAD_COUNT = 32
KEY_VALUE_HEADS = 4
HEAD_DIMENSION = 128
FF = 768
TOPK = 8
TOK_DEV = 256
EXPERTS = 32
MOST = 80
SEQUENCE_LENGTH = 1024
TOKENS = 8192


def draw_positions(key, part):
    key = jax.random.fold_in(key, 7)
    sequence_count = TOKENS // SEQUENCE_LENGTH
    step_key = jax.random.fold_in(key, 1)
    pick_key = jax.random.fold_in(key, 2)
    steps_up = jax.random.randint(step_key, (sequence_count, SEQUENCE_LENGTH), 1, 4, dtype=jnp.int32)
    steady = jax.random.randint(pick_key, (), 0, sequence_count, dtype=jnp.int32)
    steps_up = jnp.where(jnp.arange(sequence_count, dtype=jnp.int32)[:, None] == steady, jnp.int32(3), steps_up)
    steps_up = jnp.concatenate([jnp.zeros((sequence_count, 1), jnp.int32), steps_up[:, 1:]], axis=1)
    return jnp.cumsum(steps_up, axis=1).reshape(TOKENS).astype(jnp.int32)


def block_levels(stream_key, extent, shards, low, largest):
    level, own = 1.0, jax.random.fold_in(stream_key, 6)
    for axis_at, blocks in shards:
        steps = jnp.exp(jax.random.uniform(jax.random.fold_in(own, axis_at), (blocks,), jnp.float32, low / len(shards), largest / len(shards)))
        level = level * jnp.repeat(steps, extent[axis_at] // blocks).reshape([-1 if axis == axis_at else 1 for axis in range(len(extent))])
    return level


def routed_block(stream_key, own, number, rows, amount, top, most, skew):
    sequence = jax.random.permutation(stream_key, amount)
    crowded, ordinary = portions_of(amount, rows * top, most, skew, True), portions_of(amount, rows * top, most, skew, False)
    places = jnp.arange(amount)

    def named(lengths, offset_by):
        used = int((lengths > 0).sum())
        fixed = max(1, used // 4)
        passed = fixed + (places - fixed + offset_by * (used - fixed)) % max(1, amount - fixed)
        return jnp.zeros((amount,), jnp.int32).at[sequence[jnp.where(places < fixed, places, passed)]].set(jnp.asarray(lengths, jnp.int32))

    lengths = jnp.where(number % 4 == 0, named(crowded, number // 4), named(ordinary, number - number // 4 - 1))
    mixed = jax.random.permutation(jax.random.fold_in(own, 3), amount)
    source_of, taker = mixed[0:amount // 2 * 2:2], mixed[1:amount // 2 * 2:2]
    slack = jnp.minimum(lengths[source_of] - 1, most - lengths[taker]) // 2
    slack = jnp.where((source_of == sequence[0]) | (taker == sequence[0]) | (lengths[taker] == 0), 0, jnp.maximum(slack, 0))
    passed = jax.random.randint(jax.random.fold_in(own, 4), (amount // 2,), 0, 1 << 20) % (slack + 1)
    lengths = lengths.at[source_of].add(-passed).at[taker].add(passed)
    items = jnp.searchsorted(jnp.cumsum(lengths), jnp.arange(rows * top), side="right").astype(jnp.int32)
    table = items.reshape(top, rows).T
    table = table[jax.random.permutation(jax.random.fold_in(own, 1), rows)]
    offset_by = jax.random.randint(jax.random.fold_in(own, 2), (rows, 1), 0, top)
    return jnp.take_along_axis(table, (jnp.arange(top)[None, :] + offset_by) % top, axis=1)


def portions_of(amount, total, reach, slope, full):
    portions = [(1 << 20) // math.isqrt(grade ** slope) + 1 for grade in range(1, amount + 1)]
    largest = reach if full else min(reach, max(-(-total // amount), total * portions[0] // sum(portions)))
    least = 1 if total - largest >= amount - 1 else 0
    given, rest = [largest] + [least] * (amount - 1), total - largest - least * (amount - 1)
    while rest > 0:
        candidates = [i for i in range(1, amount) if given[i] < largest] or [i for i in range(1, amount) if given[i] < reach]
        pool, budget = sum([portions[i] for i in candidates]), rest
        for i in candidates:
            extra = min(reach - given[i], max(1, budget * portions[i] // pool), rest)
            given[i] = given[i] + extra
            rest = rest - extra
    return np.array(given)


def gaussian(key, extent, width, most, cuts=(), held_as=jnp.bfloat16):
    drawn = width * jax.random.normal(key, extent, jnp.float32)
    if cuts:
        drawn = drawn * block_levels(key, extent, cuts, -0.22, 0.18)
    return jnp.clip(drawn, -most, most).astype(held_as)


def setup_inputs(seed: int = 0) -> dict:
    arg_keys = jax.random.split(jax.random.key(seed), 17)
    inputs = gaussian(arg_keys[0], (TOKENS, MODEL_DIMENSION), 1.0, 6.0, ((0, 32),))
    expert_ids_keys = jax.random.split(jax.random.fold_in(arg_keys[1], 1), TOKENS // TOK_DEV)
    expert_ids_turns = jax.random.permutation(jax.random.fold_in(arg_keys[1], 3), TOKENS // TOK_DEV)
    expert_ids = jax.vmap(lambda own, number: routed_block(jax.random.fold_in(arg_keys[1], 2), own, number, TOK_DEV, EXPERTS, TOPK, MOST, 2))(expert_ids_keys, expert_ids_turns).reshape((TOKENS, TOPK))
    positions = draw_positions(jax.random.fold_in(arg_keys[16], 71), 0)
    cotangent = gaussian(arg_keys[3], (TOKENS, MODEL_DIMENSION), 1.0, 6.0, ((0, 32),))
    attn_gain = jnp.clip(1.0 + 0.1 * jax.random.normal(arg_keys[4], (MODEL_DIMENSION,), jnp.float32), 0.5, 1.5)
    query_proj = gaussian(arg_keys[5], (MODEL_DIMENSION, QUERY_HEAD_COUNT * HEAD_DIMENSION), MODEL_DIMENSION ** -0.5, 0.125, ((0, 2), (1, 4)))
    key_projection = gaussian(arg_keys[6], (MODEL_DIMENSION, KEY_VALUE_HEADS * HEAD_DIMENSION), MODEL_DIMENSION ** -0.5, 0.125, ((0, 2), (1, 4)))
    value_projection = gaussian(arg_keys[7], (MODEL_DIMENSION, KEY_VALUE_HEADS * HEAD_DIMENSION), MODEL_DIMENSION ** -0.5, 0.125, ((0, 2), (1, 4)))
    query_norm_gain = jnp.clip(jnp.exp(jax.random.uniform(arg_keys[8], (HEAD_DIMENSION,), jnp.float32, math.log(1.0), math.log(2.0))), 1.0, 2.0)
    key_norm_gain = jnp.clip(jnp.exp(jax.random.uniform(arg_keys[9], (HEAD_DIMENSION,), jnp.float32, math.log(1.0), math.log(2.0))), 1.0, 2.0)
    out_proj = gaussian(arg_keys[10], (MODEL_DIMENSION, QUERY_HEAD_COUNT * HEAD_DIMENSION), (QUERY_HEAD_COUNT * HEAD_DIMENSION // 32) ** -0.5, 0.5, ((0, 2), (1, 4)))
    moe_gain = jnp.clip(1.0 + 0.1 * jax.random.normal(arg_keys[11], (MODEL_DIMENSION,), jnp.float32), 0.5, 1.5)
    router = gaussian(arg_keys[12], (MODEL_DIMENSION, EXPERTS), (4 * MODEL_DIMENSION) ** -0.5, 0.0625)
    gate_proj = gaussian(arg_keys[13], (EXPERTS, MODEL_DIMENSION, FF), MODEL_DIMENSION ** -0.5, 0.125, ((0, 32),))
    up_proj = gaussian(arg_keys[14], (EXPERTS, MODEL_DIMENSION, FF), MODEL_DIMENSION ** -0.5, 0.125, ((0, 32),))
    down_proj = gaussian(arg_keys[15], (EXPERTS, FF, MODEL_DIMENSION), (FF // 16) ** -0.5, 0.875, ((0, 32),))
    return dict(inputs=inputs, expert_ids=expert_ids, positions=positions, cotangent=cotangent, attn_gain=attn_gain, query_proj=query_proj, key_projection=key_projection, value_projection=value_projection, query_norm_gain=query_norm_gain, key_norm_gain=key_norm_gain, out_proj=out_proj, moe_gain=moe_gain, router=router, gate_proj=gate_proj, up_proj=up_proj, down_proj=down_proj)


@jax.custom_vjp
def low(v):
    return lax.optimization_barrier(v.astype(jnp.bfloat16)).astype(jnp.float32)

@jax.custom_vjp
def low_back(v):
    return v

def low_keep(v):
    return (low(v), None)

def low_pass(kept, grad):
    return (grad,)

def back_keep(v):
    return (v, None)

def back_low(kept, grad):
    return (low(grad),)
low.defvjp(low_keep, low_pass)
low_back.defvjp(back_keep, back_low)
epsilon = 1e-06
rotary_base = 1000000.0
highest = lax.Precision.HIGHEST

def rms_scale(values, gain):
    return values * lax.rsqrt(lax.optimization_barrier(jnp.mean(values * values, axis=-1, keepdims=True)) + epsilon) * gain

def rotary_tables(positions, head_width):
    halves = head_width // 2
    frequency = rotary_base ** (-2.0 * jnp.arange(halves, dtype=jnp.float32) / head_width)
    angles = positions.astype(jnp.float32)[:, None] * frequency[None, :]
    return (jnp.cos(angles), jnp.sin(angles))

def rotary(values, cosine, sine_part):
    halves = values.shape[-1] // 2
    former = values[..., :halves]
    latter = values[..., halves:]
    cos_rows = cosine[:, None, :]
    sin_rows = sine_part[:, None, :]
    return jnp.concatenate([former * cos_rows - latter * sin_rows, latter * cos_rows + former * sin_rows], axis=-1)

def build_attention(query_norm_gain, key_norm_gain):

    def attend(entries):
        query_rows, key_row_block, value_row_block, seq_positions = entries
        cosine, sine_part = rotary_tables(seq_positions, HEAD_DIMENSION)
        query_rows = low(rotary(rms_scale(query_rows, query_norm_gain), cosine, sine_part))
        key_row_block = low(rotary(rms_scale(key_row_block, key_norm_gain), cosine, sine_part))
        value_row_block = low(value_row_block)
        grouped_heads = query_rows.reshape(SEQUENCE_LENGTH, KEY_VALUE_HEADS, QUERY_HEAD_COUNT // KEY_VALUE_HEADS, HEAD_DIMENSION)
        scores = jnp.einsum('bkgd,tkd->kgbt', grouped_heads, key_row_block, precision=highest) * HEAD_DIMENSION ** (-0.5)
        scores = low_back(scores)
        allowed = jnp.arange(SEQUENCE_LENGTH)[:, None] >= jnp.arange(SEQUENCE_LENGTH)[None, :]
        scores = jnp.where(allowed, scores, -1e+30)
        weights_low = low(jax.nn.softmax(scores, axis=-1))
        expert_mixture = jnp.einsum('kgbt,tkd->bkgd', weights_low, value_row_block, precision=highest)
        return expert_mixture.reshape(SEQUENCE_LENGTH, QUERY_HEAD_COUNT * HEAD_DIMENSION)
    return jax.checkpoint(attend)

def layer_forward(inputs, attn_gain, query_proj, key_projection, value_projection, query_norm_gain, key_norm_gain, out_proj, moe_gain, router, gate_proj, up_proj, down_proj, expert_ids, positions):
    sequence_count = TOKENS // SEQUENCE_LENGTH
    normed = low(rms_scale(inputs, attn_gain))
    query_rows = low_back(jnp.dot(normed, query_proj, precision=highest))
    key_row_block = low_back(jnp.dot(normed, key_projection, precision=highest))
    value_row_block = low_back(jnp.dot(normed, value_projection, precision=highest))
    expert_mixture = lax.map(build_attention(query_norm_gain, key_norm_gain), (query_rows.reshape(sequence_count, SEQUENCE_LENGTH, QUERY_HEAD_COUNT, HEAD_DIMENSION), key_row_block.reshape(sequence_count, SEQUENCE_LENGTH, KEY_VALUE_HEADS, HEAD_DIMENSION), value_row_block.reshape(sequence_count, SEQUENCE_LENGTH, KEY_VALUE_HEADS, HEAD_DIMENSION), positions.reshape(sequence_count, SEQUENCE_LENGTH)))
    attended = low_back(low(expert_mixture.reshape(TOKENS, QUERY_HEAD_COUNT * HEAD_DIMENSION)))
    branch = low_back(jnp.dot(attended, out_proj.T, precision=highest))
    hidden = inputs + branch
    routed = low(rms_scale(hidden, moe_gain))
    logits = low_back(jnp.dot(routed, router, precision=highest))
    gate_weights = jax.nn.softmax(jnp.take_along_axis(logits, expert_ids, axis=1), axis=-1)
    capacity = EXPERTS * MOST
    assigned = TOKENS * TOPK
    flat_ids = expert_ids.reshape(assigned).astype(jnp.int32)
    matches = (flat_ids[:, None] == jnp.arange(EXPERTS, dtype=jnp.int32)[None, :]).astype(jnp.int32)
    slot_rank = lax.optimization_barrier(jnp.sum((jnp.cumsum(matches, axis=0) - 1) * matches, axis=1)).astype(jnp.int32)
    slot_table = jnp.full((EXPERTS, capacity), assigned, jnp.int32).at[flat_ids, slot_rank].set(jnp.arange(assigned, dtype=jnp.int32))
    token_of = jnp.minimum(slot_table // TOPK, TOKENS - 1).astype(jnp.int32)

    def expert_apply(entries):
        rows_index, gate_weight, up_weight, down_weight = entries
        rows_in = low_back(routed[rows_index])
        gate_part = low_back(jnp.dot(rows_in, gate_weight, precision=highest))
        up_part = low_back(jnp.dot(rows_in, up_weight, precision=highest))
        acted = low(jax.nn.silu(gate_part) * up_part)
        return low_back(low(jnp.dot(acted, down_weight, precision=highest)))
    results = lax.map(jax.checkpoint(expert_apply), (token_of, gate_proj, up_proj, down_proj))
    picked = results[expert_ids, slot_rank.reshape(TOKENS, TOPK)]
    combined = lax.optimization_barrier(jnp.sum(picked * gate_weights[:, :, None], axis=1))
    return hidden + combined

def reference(inputs, expert_ids, positions, cotangent, attn_gain, query_proj, key_projection, value_projection, query_norm_gain, key_norm_gain, out_proj, moe_gain, router, gate_proj, up_proj, down_proj):
    floats = [value.astype(jnp.float32) for value in (inputs, attn_gain, query_proj, key_projection, value_projection, query_norm_gain, key_norm_gain, out_proj, moe_gain, router, gate_proj, up_proj, down_proj)]

    def applied(*values):
        return layer_forward(*values, expert_ids, positions)
    output, pullback = jax.vjp(applied, *floats)
    gradients = pullback(cotangent.astype(jnp.float32))
    return (output.astype(jnp.bfloat16), gradients[0].astype(jnp.bfloat16), gradients[1], gradients[2], gradients[3], gradients[4], gradients[5], gradients[6], gradients[7], gradients[8], gradients[9], gradients[10], gradients[11], gradients[12])
```

```python
import functools

import jax
import jax.numpy as jnp
from jax import lax
from jax.experimental import pallas as pl
from jax.experimental.pallas import tpu as pltpu
from jax.sharding import PartitionSpec as P

epsilon = 1e-06
rotary_base = 1000000.0
plane = ("dp", "exp")
everyone = ("dp", "exp", "col")
f32 = jnp.float32
bf16 = jnp.bfloat16


def dot_nn(a, b):
    return lax.dot_general(a, b, (((1,), (0,)), ((), ())), preferred_element_type=f32)


def dot_nt(a, b):
    return lax.dot_general(a, b, (((1,), (1,)), ((), ())), preferred_element_type=f32)


def dot_tn(a, b):
    return lax.dot_general(a, b, (((0,), (0,)), ((), ())), preferred_element_type=f32)


def inverse_rms(rows):
    return lax.rsqrt(jnp.mean(rows * rows, axis=-1, keepdims=True) + epsilon)


def rotary_tables(positions, head_size):
    halves = head_size // 2
    frequency = rotary_base ** (-2.0 * jnp.arange(halves, dtype=f32) / head_size)
    angles = positions.astype(f32)[:, None] * frequency[None, :]
    cosine, sine = jnp.cos(angles), jnp.sin(angles)
    return (
        jnp.concatenate([cosine, cosine], axis=1),
        jnp.concatenate([-sine, sine], axis=1),
    )


def turn(rows, cosine, sine):
    return rows * cosine + pltpu.roll(rows, rows.shape[-1] // 2, 1) * sine


def turn_back(rows, cosine, sine):
    return rows * cosine - pltpu.roll(rows, rows.shape[-1] // 2, 1) * sine


def place_of(col_ref, blocks, tokens, true_block):
    return pl.multiple_of(lax.rem(col_ref[0] - true_block + blocks, blocks) * tokens, tokens)


def softmax_rows(query, keys_ref, first, tokens, scale):
    diagonal = dot_nt(query, keys_ref[pl.ds(first, tokens), :])
    row = lax.broadcasted_iota(jnp.int32, diagonal.shape, 0)
    column = lax.broadcasted_iota(jnp.int32, diagonal.shape, 1)
    diagonal = jnp.where(row >= column, diagonal * scale, -1e30)
    peak = jnp.max(diagonal, axis=1, keepdims=True)
    if first:
        former = dot_nt(query, keys_ref[pl.ds(0, first), :]) * scale
        peak = jnp.maximum(peak, jnp.max(former, axis=1, keepdims=True))
        former = jnp.exp(former - peak)
        diagonal = jnp.exp(diagonal - peak)
        inverse = 1.0 / (
            jnp.sum(former, axis=1, keepdims=True) + jnp.sum(diagonal, axis=1, keepdims=True)
        )
        return former * inverse, diagonal * inverse
    diagonal = jnp.exp(diagonal - peak)
    return None, diagonal / jnp.sum(diagonal, axis=1, keepdims=True)


def forward_kernel(
    blocks, tokens, scale, col_ref, q_ref, k_ref, v_ref, cos_ref, sin_ref, qg_ref, kg_ref, out_ref, keys, values
):
    @pl.when(pl.program_id(0) == 0)
    def _():
        for block in range(blocks):
            here = pl.ds(place_of(col_ref, blocks, tokens, block), tokens)
            there = pl.ds(block * tokens, tokens)
            raw = k_ref[here, :]
            rows = raw * inverse_rms(raw) * kg_ref[...]
            keys[there, :] = turn(rows, cos_ref[there, :], sin_ref[there, :]).astype(bf16)
            values[there, :] = v_ref[here, :].astype(bf16)

    for block in range(blocks):
        here = pl.ds(place_of(col_ref, blocks, tokens, block), tokens)
        first = block * tokens
        there = pl.ds(first, tokens)
        raw = q_ref[here, :]
        rows = raw * inverse_rms(raw) * qg_ref[...]
        query = turn(rows, cos_ref[there, :], sin_ref[there, :]).astype(bf16)
        former, diagonal = softmax_rows(query, keys, first, tokens, scale)
        mixed = dot_nn(diagonal.astype(bf16), values[there, :])
        if first:
            mixed = mixed + dot_nn(former.astype(bf16), values[pl.ds(0, first), :])
        out_ref[here, :] = mixed.astype(bf16)


def attention_forward(col, qkv, cosine, sine, query_gain, key_gain, heads, tokens):
    seq_len, head_size = qkv.shape[0], query_gain.shape[-1]
    column = lambda index: pl.BlockSpec((seq_len, head_size), index)
    whole = pl.BlockSpec((seq_len, head_size), lambda h, c: (0, 0))
    gain = pl.BlockSpec((1, head_size), lambda h, c: (0, 0))
    return pl.pallas_call(
        functools.partial(forward_kernel, seq_len // tokens, tokens, head_size ** (-0.5)),
        out_shape=jax.ShapeDtypeStruct((seq_len, heads * head_size), bf16),
        grid_spec=pltpu.PrefetchScalarGridSpec(
            num_scalar_prefetch=1,
            grid=(heads,),
            in_specs=[
                column(lambda h, c: (0, h)),
                column(lambda h, c: (0, heads)),
                column(lambda h, c: (0, heads + 1)),
                whole,
                whole,
                gain,
                gain,
            ],
            out_specs=column(lambda h, c: (0, h)),
            scratch_shapes=[
                pltpu.VMEM((seq_len, head_size), bf16),
                pltpu.VMEM((seq_len, head_size), bf16),
            ],
        ),
        compiler_params=pltpu.CompilerParams(vmem_limit_bytes=40 * 2**20),
        cost_estimate=pl.CostEstimate(
            flops=3 * heads * seq_len * seq_len * head_size,
            bytes_accessed=6 * seq_len * heads * head_size,
            transcendentals=heads * seq_len * seq_len // 2,
        ),
        name="attention_forward",
    )(col, qkv, qkv, qkv, cosine, sine, query_gain, key_gain)


def backward_kernel(
    blocks, tokens, scale, heads,
    col_ref, q_ref, k_ref, v_ref, g_ref, cos_ref, sin_ref, qg_ref, kg_ref,
    grad_ref, qgain_ref, kgain_ref,
    keys, values, grad_keys, grad_values,
):
    step = pl.program_id(0)

    @pl.when(step == 0)
    def _():
        for block in range(blocks):
            here = pl.ds(place_of(col_ref, blocks, tokens, block), tokens)
            there = pl.ds(block * tokens, tokens)
            raw = k_ref[here, :]
            rows = raw * inverse_rms(raw) * kg_ref[...]
            keys[there, :] = turn(rows, cos_ref[there, :], sin_ref[there, :]).astype(bf16)
            values[there, :] = v_ref[here, :].astype(bf16)
        grad_keys[...] = jnp.zeros_like(grad_keys)
        grad_values[...] = jnp.zeros_like(grad_values)
        qgain_ref[...] = jnp.zeros_like(qgain_ref)
        kgain_ref[...] = jnp.zeros_like(kgain_ref)

    def through_norm(grad_rot, unit, inverse, there, gain_ref, gain_grad_ref):
        grad_scaled = turn_back(grad_rot, cos_ref[there, :], sin_ref[there, :])
        gain_grad_ref[0:1, :] += jnp.sum(grad_scaled * unit, axis=0, keepdims=True)
        grad_unit = grad_scaled * gain_ref[...]
        return inverse * (grad_unit - unit * jnp.mean(grad_unit * unit, axis=1, keepdims=True))

    @pl.when(step < heads)
    def _():
        for block in range(blocks):
            here = pl.ds(place_of(col_ref, blocks, tokens, block), tokens)
            first = block * tokens
            there = pl.ds(first, tokens)
            raw = q_ref[here, :]
            inverse = inverse_rms(raw)
            unit = raw * inverse
            query = turn(unit * qg_ref[...], cos_ref[there, :], sin_ref[there, :]).astype(bf16)
            grad_mixed = g_ref[here, :]
            former, diagonal = softmax_rows(query, keys, first, tokens, scale)
            grad_diagonal = dot_nt(grad_mixed, values[there, :])
            inner = jnp.sum(diagonal * grad_diagonal, axis=1, keepdims=True)
            if first:
                before = pl.ds(0, first)
                grad_former = dot_nt(grad_mixed, values[before, :])
                inner = inner + jnp.sum(former * grad_former, axis=1, keepdims=True)
                score_former = (former * (grad_former - inner)).astype(bf16)
                grad_keys[before, :] += dot_tn(score_former, query)
                grad_values[before, :] += dot_tn(former.astype(bf16), grad_mixed)
            score_diagonal = (diagonal * (grad_diagonal - inner)).astype(bf16)
            grad_keys[there, :] += dot_tn(score_diagonal, query)
            grad_values[there, :] += dot_tn(diagonal.astype(bf16), grad_mixed)
            grad_query = dot_nn(score_diagonal, keys[there, :])
            if first:
                grad_query = grad_query + dot_nn(score_former, keys[before, :])
            grad_ref[here, :] = through_norm(
                grad_query * scale, unit, inverse, there, qg_ref, qgain_ref
            ).astype(bf16)

    @pl.when(step == heads)
    def _():
        for block in range(blocks):
            here = pl.ds(place_of(col_ref, blocks, tokens, block), tokens)
            there = pl.ds(block * tokens, tokens)
            raw = k_ref[here, :]
            inverse = inverse_rms(raw)
            grad_ref[here, :] = through_norm(
                grad_keys[there, :] * scale, raw * inverse, inverse, there, kg_ref, kgain_ref
            ).astype(bf16)

    @pl.when(step == heads + 1)
    def _():
        for block in range(blocks):
            here = pl.ds(place_of(col_ref, blocks, tokens, block), tokens)
            grad_ref[here, :] = grad_values[pl.ds(block * tokens, tokens), :].astype(bf16)


def attention_backward(col, qkv, grad_attended, cosine, sine, query_gain, key_gain, heads, tokens):
    seq_len, head_size = qkv.shape[0], query_gain.shape[-1]
    column = lambda index: pl.BlockSpec((seq_len, head_size), index)
    whole = pl.BlockSpec((seq_len, head_size), lambda h, c: (0, 0))
    gain = pl.BlockSpec((1, head_size), lambda h, c: (0, 0))
    gain_out = pl.BlockSpec((8, head_size), lambda h, c: (0, 0))
    last = heads - 1
    return pl.pallas_call(
        functools.partial(backward_kernel, seq_len // tokens, tokens, head_size ** (-0.5), heads),
        out_shape=(
            jax.ShapeDtypeStruct(qkv.shape, bf16),
            jax.ShapeDtypeStruct((8, head_size), f32),
            jax.ShapeDtypeStruct((8, head_size), f32),
        ),
        grid_spec=pltpu.PrefetchScalarGridSpec(
            num_scalar_prefetch=1,
            grid=(heads + 2,),
            in_specs=[
                column(lambda h, c: (0, jnp.minimum(h, last))),
                column(lambda h, c: (0, heads)),
                column(lambda h, c: (0, heads + 1)),
                column(lambda h, c: (0, jnp.minimum(h, last))),
                whole,
                whole,
                gain,
                gain,
            ],
            out_specs=(column(lambda h, c: (0, h)), gain_out, gain_out),
            scratch_shapes=[
                pltpu.VMEM((seq_len, head_size), bf16),
                pltpu.VMEM((seq_len, head_size), bf16),
                pltpu.VMEM((seq_len, head_size), f32),
                pltpu.VMEM((seq_len, head_size), f32),
            ],
        ),
        compiler_params=pltpu.CompilerParams(vmem_limit_bytes=48 * 2**20),
        cost_estimate=pl.CostEstimate(
            flops=7 * heads * seq_len * seq_len * head_size,
            bytes_accessed=8 * seq_len * heads * head_size,
            transcendentals=heads * seq_len * seq_len // 2,
        ),
        name="attention_backward",
    )(col, qkv, qkv, qkv, grad_attended, cosine, sine, query_gain, key_gain)


def local(
    inputs,
    expert_ids,
    positions,
    cotangent,
    attn_gain,
    query_proj,
    key_projection,
    value_projection,
    query_norm_gain,
    key_norm_gain,
    out_proj,
    moe_gain,
    router,
    gate_proj,
    up_proj,
    down_proj,
):
    tokens, width = inputs.shape
    head_size = query_norm_gain.shape[0]
    choices = expert_ids.shape[1]
    experts = router.shape[1]
    capacity = tokens * choices * 5 // (4 * experts)
    columns = lax.axis_size("col")
    peers = lax.axis_size("dp") * lax.axis_size("exp")
    col = lax.axis_index("col")
    col_array = jnp.reshape(col, (1,)).astype(jnp.int32)
    heads = query_proj.shape[1] // head_size
    assert key_projection.shape[1] == head_size and experts == peers * columns
    around = [(i, (i + 1) % columns) for i in range(columns)]

    def shift(block):
        return lax.ppermute(block, "col", around)

    def ring_gather(block):
        blocks = [block]
        for _ in range(columns - 1):
            blocks.append(shift(blocks[-1]))
        return blocks

    def ring_sum(part_of):
        running = part_of(1)
        for step in range(2, columns + 1):
            running = shift(running.astype(bf16)).astype(f32) + part_of(step % columns)
        return running

    def swap(rows):
        return lax.all_to_all(
            rows.reshape(peers, rows.shape[0] // peers, *rows.shape[1:]), plane, 0, 0, tiled=True
        ).reshape(rows.shape)

    def true_block(step):
        return lax.rem(col - step + columns, columns)

    local_qkv = jnp.concatenate([query_proj, key_projection, value_projection], axis=1)
    full_qkv = lax.all_gather(local_qkv, "exp", axis=0, tiled=True)
    full_out = lax.all_gather(out_proj, "exp", axis=0, tiled=True)

    input_blocks = ring_gather(inputs)
    sequence_in = jnp.concatenate(input_blocks, axis=0).astype(f32)
    inverse_in = inverse_rms(sequence_in)
    sequence = (sequence_in * inverse_in * attn_gain).astype(bf16)
    qkv = dot_nn(sequence, full_qkv)
    cosine, sine = rotary_tables(positions, head_size)
    query_gain, key_gain = query_norm_gain[None, :], key_norm_gain[None, :]
    attended = attention_forward(
        col_array, qkv, cosine, sine, query_gain, key_gain, heads, tokens
    )

    def rows_of(array, step):
        return lax.slice_in_dim(array, step * tokens, (step + 1) * tokens, axis=0)

    branch = ring_sum(lambda step: dot_nt(rows_of(attended, step), full_out))
    hidden = inputs.astype(f32) + branch
    inverse_hidden = inverse_rms(hidden)
    routed = (hidden * inverse_hidden * moe_gain).astype(bf16)

    gathered_ids = lax.all_gather(expert_ids, "col", axis=0)
    earlier = (
        lax.broadcasted_iota(jnp.int32, (tokens, tokens), 0)
        < lax.broadcasted_iota(jnp.int32, (tokens, tokens), 1)
    ).astype(bf16)

    def slots_of(ids, named):
        chosen = jnp.any(ids.T[None, :, :] == named[:, None, None], axis=1)
        rank = dot_nn(chosen.astype(bf16), earlier)
        code = jnp.where(chosen, rank, -1.0)
        place = lax.broadcasted_iota(jnp.int32, (1, capacity, 1), 1).astype(f32)
        return chosen, code[:, None, :] == place

    plane_experts = jnp.arange(peers, dtype=jnp.int32) * columns + col
    slot_mats = []
    for step in range(columns):
        ids = lax.dynamic_index_in_dim(gathered_ids, true_block(step), 0, keepdims=False)
        _, slots = slots_of(ids, plane_experts)
        slot_mats.append(slots.astype(bf16).reshape(peers * capacity, tokens))
    chosen_all, slots_all = slots_of(expert_ids, jnp.arange(experts, dtype=jnp.int32))

    def dispatch(step, block):
        return swap(dot_nn(slot_mats[step], block).astype(bf16))

    gate_weight, up_weight, down_weight = gate_proj[0], up_proj[0], down_proj[0]
    cotangent_rows = [dispatch(s, b) for s, b in enumerate(ring_gather(cotangent))]
    drive = [dot_nt(rows, down_weight) for rows in cotangent_rows]

    logits = dot_general_t(router, routed)
    logits = jnp.where(chosen_all, logits, -1e30)
    exponent = jnp.exp(logits - jnp.max(logits, axis=0, keepdims=True))
    exponent = jnp.where(chosen_all, exponent, 0.0)
    gates = exponent / jnp.sum(exponent, axis=0, keepdims=True)

    def swap_all(values):
        return lax.all_to_all(values, everyone, 0, 0, tiled=True)

    gate_slots = swap_all(jnp.sum(jnp.where(slots_all, gates[:, None, :], 0.0), axis=2))
    gate_slots = gate_slots.reshape(peers, columns, capacity)

    def ring_slots(values, step):
        return lax.dynamic_index_in_dim(values, true_block(step), 1, keepdims=False)

    arrived = [dispatch(s, b) for s, b in enumerate(ring_gather(routed))]
    acted_rows, gate_grads, up_grads, weighted_rows, row_grads, gate_dots = [], [], [], [], [], []
    for step in range(columns):
        gate_part = dot_nn(arrived[step], gate_weight)
        up_part = dot_nn(arrived[step], up_weight)
        sigmoid = jax.nn.sigmoid(gate_part)
        silu = gate_part * sigmoid
        acted = silu * up_part
        weight = ring_slots(gate_slots, step).reshape(peers * capacity, 1)
        grad_acted = drive[step] * weight
        gate_dots.append(jnp.sum(acted * drive[step], axis=1).reshape(peers, capacity))
        gate_grad = (grad_acted * up_part * sigmoid * (1.0 + gate_part * (1.0 - sigmoid))).astype(bf16)
        up_grad = (grad_acted * silu).astype(bf16)
        weighted_rows.append((acted * weight).astype(bf16))
        gate_grads.append(gate_grad)
        up_grads.append(up_grad)
        row_grads.append((dot_nt(gate_grad, gate_weight) + dot_nt(up_grad, up_weight)).astype(bf16))

    dots = jnp.stack(gate_dots, axis=1)
    order = lax.rem(col - jnp.arange(columns, dtype=jnp.int32) + columns, columns)
    dots = jnp.take(dots, order, axis=1).reshape(experts, capacity)
    dots = swap_all(dots)
    grad_gates = jnp.sum(jnp.where(slots_all, dots[:, :, None], 0.0), axis=1)
    grad_logits = (
        gates * (grad_gates - jnp.sum(gates * grad_gates, axis=0, keepdims=True))
    ).astype(bf16)

    def collect(rows):
        back = {s: swap(rows[s]) for s in [*range(1, columns), 0]}
        return ring_sum(lambda step: dot_tn(slot_mats[step], back[step]))

    grad_routed = collect(row_grads) + lax.dot_general(grad_logits, router, (((0,), (1,)), ((), ())), preferred_element_type=f32)
    upstream = cotangent.astype(f32)
    scaled = grad_routed * moe_gain
    grad_hidden = (
        upstream
        + scaled * inverse_hidden
        - hidden * (jnp.mean(hidden * scaled, axis=-1, keepdims=True) * inverse_hidden**3)
    )
    grad_moe_gain = jnp.sum(grad_routed * hidden * inverse_hidden, axis=0)
    grad_router = dot_general_t(routed, grad_logits)

    grad_sequence = jnp.concatenate(ring_gather(grad_hidden.astype(bf16)), axis=0)
    grad_attended = dot_nn(grad_sequence, full_out).astype(bf16)
    grad_qkv, grad_query_gain, grad_key_gain = attention_backward(
        col_array, qkv, grad_attended, cosine, sine, query_gain, key_gain, heads, tokens
    )
    grad_out_weight = dot_tn(grad_sequence, attended)
    partial_normed = dot_nt(grad_qkv, full_qkv)
    grad_attn_gain = jnp.sum(partial_normed * sequence_in * inverse_in, axis=0)
    grad_normed = ring_sum(lambda step: rows_of(partial_normed, step))
    input_rows = inputs.astype(f32)
    inverse_own = inverse_rms(input_rows)
    scaled_in = grad_normed * attn_gain
    grad_inputs = (
        grad_hidden
        + scaled_in * inverse_own
        - input_rows * (jnp.mean(input_rows * scaled_in, axis=-1, keepdims=True) * inverse_own**3)
    ).astype(bf16)
    grad_qkv_weight = dot_tn(sequence, grad_qkv)

    returned = [dot_nn(rows, down_weight).astype(bf16) for rows in weighted_rows]
    outputs = (hidden + collect(returned)).astype(bf16)

    arrived_all = jnp.concatenate(arrived, axis=0)
    grad_gate_weight = dot_tn(arrived_all, jnp.concatenate(gate_grads, axis=0))
    grad_up_weight = dot_tn(arrived_all, jnp.concatenate(up_grads, axis=0))
    grad_down = dot_tn(
        jnp.concatenate(weighted_rows, axis=0), jnp.concatenate(cotangent_rows, axis=0)
    )

    reduced_qkv = lax.psum_scatter(
        grad_qkv_weight.astype(bf16), plane, scatter_dimension=0, tiled=True
    ).astype(f32)
    reduced_out = lax.psum_scatter(
        grad_out_weight.astype(bf16), plane, scatter_dimension=0, tiled=True
    ).astype(f32)
    shared = lax.psum(
        (grad_attn_gain, grad_query_gain[0], grad_key_gain[0], grad_moe_gain, grad_router),
        everyone,
    )
    split = heads * head_size
    return (
        outputs,
        grad_inputs,
        shared[0],
        reduced_qkv[:, :split],
        reduced_qkv[:, split : split + head_size],
        reduced_qkv[:, split + head_size :],
        shared[1],
        shared[2],
        reduced_out,
        shared[3],
        shared[4],
        grad_gate_weight[None],
        grad_up_weight[None],
        grad_down[None],
    )


def dot_general_t(a, b):
    contract = (((0,), (1,)), ((), ()))
    return lax.dot_general(a, b, contract, preferred_element_type=f32)


def solution(mesh):
    return jax.shard_map(
        local,
        mesh=mesh,
        in_specs=(
            P(("dp", "exp", "col"), None),
            P(("dp", "exp", "col"), None),
            P(("dp", "exp")),
            P(("dp", "exp", "col"), None),
            P(),
            P("exp", "col"),
            P("exp", "col"),
            P("exp", "col"),
            P(),
            P(),
            P("exp", "col"),
            P(),
            P(),
            P(("dp", "exp", "col"), None, None),
            P(("dp", "exp", "col"), None, None),
            P(("dp", "exp", "col"), None, None),
        ),
        out_specs=(
            P(("dp", "exp", "col"), None),
            P(("dp", "exp", "col"), None),
            P(),
            P(("dp", "exp"), "col"),
            P(("dp", "exp"), "col"),
            P(("dp", "exp"), "col"),
            P(),
            P(),
            P(("dp", "exp"), "col"),
            P(),
            P(),
            P(("dp", "exp", "col"), None, None),
            P(("dp", "exp", "col"), None, None),
            P(("dp", "exp", "col"), None, None),
        ),
        check_vma=False,
    )
```

```python
import functools

import jax
import jax.numpy as jnp
from jax import lax
from jax.experimental import pallas as pl
from jax.experimental.pallas import tpu as pltpu
from jax.sharding import PartitionSpec as P

epsilon = 1e-06
rotary_base = 1000000.0
plane = ("dp", "exp")
everyone = ("dp", "exp", "col")
f32 = jnp.float32
bf16 = jnp.bfloat16


def dot_nn(a, b):
    return lax.dot_general(a, b, (((1,), (0,)), ((), ())), preferred_element_type=f32)


def dot_nt(a, b):
    return lax.dot_general(a, b, (((1,), (1,)), ((), ())), preferred_element_type=f32)


def dot_tn(a, b):
    return lax.dot_general(a, b, (((0,), (0,)), ((), ())), preferred_element_type=f32)


def inverse_rms(rows):
    return lax.rsqrt(jnp.mean(rows * rows, axis=-1, keepdims=True) + epsilon)


def rotary_tables(positions, head_size):
    halves = head_size // 2
    frequency = rotary_base ** (-2.0 * jnp.arange(halves, dtype=f32) / head_size)
    angles = positions.astype(f32)[:, None] * frequency[None, :]
    cosine, sine = jnp.cos(angles), jnp.sin(angles)
    return (
        jnp.concatenate([cosine, cosine], axis=1),
        jnp.concatenate([-sine, sine], axis=1),
    )


def turn(rows, cosine, sine):
    return rows * cosine + pltpu.roll(rows, rows.shape[-1] // 2, 1) * sine


def turn_back(rows, cosine, sine):
    return rows * cosine - pltpu.roll(rows, rows.shape[-1] // 2, 1) * sine


def place_of(col_ref, blocks, tokens, step):
    return pl.multiple_of(lax.rem(col_ref[0] - step + blocks, blocks) * tokens, tokens)


def in_order(col_ref, refs, held):
    tokens = refs[0].shape[0]
    for step, ref in enumerate(refs):
        held[pl.ds(place_of(col_ref, len(refs), tokens, step), tokens), :] = ref[...].astype(held.dtype)


def out_of_order(col_ref, held, refs):
    tokens = refs[0].shape[0]
    for step, ref in enumerate(refs):
        ref[...] = held[pl.ds(place_of(col_ref, len(refs), tokens, step), tokens), :].astype(ref.dtype)


def softmax_rows(query, keys_ref, first, tokens, scale):
    diagonal = dot_nt(query, keys_ref[pl.ds(first, tokens), :])
    row = lax.broadcasted_iota(jnp.int32, diagonal.shape, 0)
    column = lax.broadcasted_iota(jnp.int32, diagonal.shape, 1)
    diagonal = jnp.where(row >= column, diagonal * scale, -1e30)
    peak = jnp.max(diagonal, axis=1, keepdims=True)
    if first:
        former = dot_nt(query, keys_ref[pl.ds(0, first), :]) * scale
        peak = jnp.maximum(peak, jnp.max(former, axis=1, keepdims=True))
        former = jnp.exp(former - peak)
        diagonal = jnp.exp(diagonal - peak)
        inverse = 1.0 / (
            jnp.sum(former, axis=1, keepdims=True) + jnp.sum(diagonal, axis=1, keepdims=True)
        )
        return former * inverse, diagonal * inverse
    diagonal = jnp.exp(diagonal - peak)
    return None, diagonal / jnp.sum(diagonal, axis=1, keepdims=True)


def prepare_keys(col_ref, k_refs, v_refs, cos_ref, sin_ref, kg_ref, raw_rows, keys, values):
    in_order(col_ref, k_refs, raw_rows)
    in_order(col_ref, v_refs, values)
    tokens = k_refs[0].shape[0]
    for block in range(len(k_refs)):
        there = pl.ds(block * tokens, tokens)
        raw = raw_rows[there, :]
        rows = raw * inverse_rms(raw) * kg_ref[...]
        keys[there, :] = turn(rows, cos_ref[there, :], sin_ref[there, :]).astype(bf16)


def forward_kernel(blocks, scale, col_ref, *refs):
    q_refs, k_refs, v_refs = refs[:blocks], refs[blocks : 2 * blocks], refs[2 * blocks : 3 * blocks]
    cos_ref, sin_ref, qg_ref, kg_ref = refs[3 * blocks : 3 * blocks + 4]
    out_refs = refs[3 * blocks + 4 : 4 * blocks + 4]
    raw_rows, keys, values, mixed_rows = refs[4 * blocks + 4 :]
    tokens = q_refs[0].shape[0]

    @pl.when(pl.program_id(0) == 0)
    def _():
        prepare_keys(col_ref, k_refs, v_refs, cos_ref, sin_ref, kg_ref, raw_rows, keys, values)

    in_order(col_ref, q_refs, raw_rows)
    for block in range(blocks):
        first = block * tokens
        there = pl.ds(first, tokens)
        raw = raw_rows[there, :]
        rows = raw * inverse_rms(raw) * qg_ref[...]
        query = turn(rows, cos_ref[there, :], sin_ref[there, :]).astype(bf16)
        former, diagonal = softmax_rows(query, keys, first, tokens, scale)
        mixed = dot_nn(diagonal.astype(bf16), values[there, :])
        if first:
            mixed = mixed + dot_nn(former.astype(bf16), values[pl.ds(0, first), :])
        mixed_rows[there, :] = mixed.astype(bf16)
    out_of_order(col_ref, mixed_rows, out_refs)


def attention_forward(col, qkv, cosine, sine, query_gain, key_gain, heads):
    blocks, tokens, head_size = len(qkv), qkv[0].shape[0], query_gain.shape[-1]
    seq_len = blocks * tokens
    column = lambda index: [pl.BlockSpec((tokens, head_size), index)] * blocks
    whole = pl.BlockSpec((seq_len, head_size), lambda h, c: (0, 0))
    gain = pl.BlockSpec((1, head_size), lambda h, c: (0, 0))
    return pl.pallas_call(
        functools.partial(forward_kernel, blocks, head_size ** (-0.5)),
        out_shape=[jax.ShapeDtypeStruct((tokens, heads * head_size), bf16)] * blocks,
        grid_spec=pltpu.PrefetchScalarGridSpec(
            num_scalar_prefetch=1,
            grid=(heads,),
            in_specs=[
                *column(lambda h, c: (0, h)),
                *column(lambda h, c: (0, heads)),
                *column(lambda h, c: (0, heads + 1)),
                whole,
                whole,
                gain,
                gain,
            ],
            out_specs=column(lambda h, c: (0, h)),
            scratch_shapes=[
                pltpu.VMEM((seq_len, head_size), f32),
                pltpu.VMEM((seq_len, head_size), bf16),
                pltpu.VMEM((seq_len, head_size), bf16),
                pltpu.VMEM((seq_len, head_size), bf16),
            ],
        ),
        compiler_params=pltpu.CompilerParams(vmem_limit_bytes=60 * 2**20),
        cost_estimate=pl.CostEstimate(flops=1000, bytes_accessed=1000, transcendentals=0),
        name="attention_forward",
    )(col, *qkv, *qkv, *qkv, cosine, sine, query_gain, key_gain)


def backward_kernel(blocks, scale, first_head, heads, final, col_ref, *refs):
    q_refs, k_refs, v_refs, g_refs = (refs[i * blocks : (i + 1) * blocks] for i in range(4))
    cos_ref, sin_ref, qg_ref, kg_ref = refs[4 * blocks : 4 * blocks + 4]
    refs = refs[4 * blocks + 4 :]
    if first_head:
        refs = refs[blocks:]
        held_refs, refs = refs[:4], refs[4:]
    grad_refs, refs = refs[:blocks], refs[blocks:]
    qgain_ref, kgain_ref, out_keys, out_values = refs[:4]
    raw_rows, mixed_rows, keys, values, grad_rows, grad_keys, grad_values = refs[4:]
    tokens = q_refs[0].shape[0]
    step = pl.program_id(0)

    @pl.when(step == 0)
    def _():
        prepare_keys(col_ref, k_refs, v_refs, cos_ref, sin_ref, kg_ref, raw_rows, keys, values)
        if first_head:
            qgain_ref[...] = held_refs[0][...]
            kgain_ref[...] = held_refs[1][...]
            grad_keys[...] = held_refs[2][...]
            grad_values[...] = held_refs[3][...]
        else:
            grad_keys[...] = jnp.zeros_like(grad_keys)
            grad_values[...] = jnp.zeros_like(grad_values)
            qgain_ref[...] = jnp.zeros_like(qgain_ref)
            kgain_ref[...] = jnp.zeros_like(kgain_ref)

    def through_norm(grad_rot, unit, inverse, there, gain_ref, gain_grad_ref):
        grad_scaled = turn_back(grad_rot, cos_ref[there, :], sin_ref[there, :])
        gain_grad_ref[0:1, :] += jnp.sum(grad_scaled * unit, axis=0, keepdims=True)
        grad_unit = grad_scaled * gain_ref[...]
        return inverse * (grad_unit - unit * jnp.mean(grad_unit * unit, axis=1, keepdims=True))

    @pl.when(step < heads)
    def _():
        in_order(col_ref, q_refs, raw_rows)
        in_order(col_ref, g_refs, mixed_rows)
        for block in range(blocks):
            first = block * tokens
            there = pl.ds(first, tokens)
            raw = raw_rows[there, :]
            inverse = inverse_rms(raw)
            unit = raw * inverse
            query = turn(unit * qg_ref[...], cos_ref[there, :], sin_ref[there, :]).astype(bf16)
            grad_mixed = mixed_rows[there, :]
            former, diagonal = softmax_rows(query, keys, first, tokens, scale)
            grad_diagonal = dot_nt(grad_mixed, values[there, :])
            inner = jnp.sum(diagonal * grad_diagonal, axis=1, keepdims=True)
            if first:
                before = pl.ds(0, first)
                grad_former = dot_nt(grad_mixed, values[before, :])
                inner = inner + jnp.sum(former * grad_former, axis=1, keepdims=True)
                score_former = (former * (grad_former - inner)).astype(bf16)
                grad_keys[before, :] += dot_tn(score_former, query)
                grad_values[before, :] += dot_tn(former.astype(bf16), grad_mixed)
            score_diagonal = (diagonal * (grad_diagonal - inner)).astype(bf16)
            grad_keys[there, :] += dot_tn(score_diagonal, query)
            grad_values[there, :] += dot_tn(diagonal.astype(bf16), grad_mixed)
            grad_query = dot_nn(score_diagonal, keys[there, :])
            if first:
                grad_query = grad_query + dot_nn(score_former, keys[before, :])
            grad_rows[there, :] = through_norm(
                grad_query * scale, unit, inverse, there, qg_ref, qgain_ref
            ).astype(bf16)

    if not final:

        @pl.when(step == heads - 1)
        def _():
            out_keys[...] = grad_keys[...]
            out_values[...] = grad_values[...]

    @pl.when(step == heads)
    def _():
        in_order(col_ref, k_refs, raw_rows)
        for block in range(blocks):
            there = pl.ds(block * tokens, tokens)
            raw = raw_rows[there, :]
            inverse = inverse_rms(raw)
            grad_rows[there, :] = through_norm(
                grad_keys[there, :] * scale, raw * inverse, inverse, there, kg_ref, kgain_ref
            ).astype(bf16)

    @pl.when(step == heads + 1)
    def _():
        grad_rows[...] = grad_values[...].astype(bf16)

    out_of_order(col_ref, grad_rows, grad_refs)


def attention_backward(
    col, qkv, grad_attended, cosine, sine, query_gain, key_gain, all_heads, first, heads, former=None
):
    blocks, tokens, head_size = len(qkv), qkv[0].shape[0], query_gain.shape[-1]
    seq_len = blocks * tokens
    final = first + heads == all_heads
    column = lambda index: [pl.BlockSpec((tokens, head_size), index)] * blocks
    whole = pl.BlockSpec((seq_len, head_size), lambda h, c: (0, 0))
    gain = pl.BlockSpec((1, head_size), lambda h, c: (0, 0))
    gain_out = pl.BlockSpec((8, head_size), lambda h, c: (0, 0))
    last = all_heads - 1
    held = [] if former is None else former
    return pl.pallas_call(
        functools.partial(backward_kernel, blocks, head_size ** (-0.5), first, heads, final),
        out_shape=[
            *[jax.ShapeDtypeStruct(qkv[0].shape, bf16)] * blocks,
            jax.ShapeDtypeStruct((8, head_size), f32),
            jax.ShapeDtypeStruct((8, head_size), f32),
            jax.ShapeDtypeStruct((seq_len, head_size), f32),
            jax.ShapeDtypeStruct((seq_len, head_size), f32),
        ],
        grid_spec=pltpu.PrefetchScalarGridSpec(
            num_scalar_prefetch=1,
            grid=(heads + 2 if final else heads,),
            in_specs=[
                *column(lambda h, c: (0, jnp.minimum(h + first, last))),
                *column(lambda h, c: (0, all_heads)),
                *column(lambda h, c: (0, all_heads + 1)),
                *column(lambda h, c: (0, jnp.minimum(h + first, last))),
                whole,
                whole,
                gain,
                gain,
                *([] if former is None else [pl.BlockSpec(memory_space=pl.ANY)] * blocks),
                *([] if former is None else [gain_out, gain_out, whole, whole]),
            ],
            out_specs=[*column(lambda h, c: (0, h + first)), gain_out, gain_out, whole, whole],
            scratch_shapes=[
                pltpu.VMEM((seq_len, head_size), f32),
                pltpu.VMEM((seq_len, head_size), bf16),
                pltpu.VMEM((seq_len, head_size), bf16),
                pltpu.VMEM((seq_len, head_size), bf16),
                pltpu.VMEM((seq_len, head_size), bf16),
                pltpu.VMEM((seq_len, head_size), f32),
                pltpu.VMEM((seq_len, head_size), f32),
            ],
        ),
        input_output_aliases={} if former is None else {1 + 4 * blocks + 4 + i: i for i in range(blocks)},
        compiler_params=pltpu.CompilerParams(vmem_limit_bytes=60 * 2**20),
        cost_estimate=pl.CostEstimate(flops=1000, bytes_accessed=1000, transcendentals=0),
        name="attention_backward",
    )(col, *qkv, *qkv, *qkv, *grad_attended, cosine, sine, query_gain, key_gain, *held)


def weight_kernel(blocks, rights, weighted, *refs):
    left_refs, refs = refs[:blocks], refs[blocks:]
    right_refs, refs = refs[: blocks * rights], refs[blocks * rights :]
    if weighted:
        weight_refs, refs = refs[:blocks], refs[blocks:]
        out_refs, held = refs[:rights], refs[rights:]

        @pl.when(pl.program_id(0) == 0)
        def _():
            for index, ref in enumerate(right_refs):
                scaled = ref[...].astype(f32) * weight_refs[index % blocks][...]
                held[index][...] = scaled.astype(bf16)

        right_refs = held
    else:
        out_refs = refs
    for index, out_ref in enumerate(out_refs):
        total = dot_tn(left_refs[0][...], right_refs[index * blocks][...])
        for block in range(1, blocks):
            total = total + dot_tn(left_refs[block][...], right_refs[index * blocks + block][...])
        out_ref[...] = total.astype(out_ref.dtype)


def weight_gradients(lefts, rights, out_type, weights=None, tile=256, order=None):
    order = order or (lambda i: i)
    blocks, rows, tall = len(lefts), lefts[0].shape[0], lefts[0].shape[1]
    flat = [block for right in rights for block in right]
    fixed = lambda array: pl.BlockSpec(array.shape, lambda i: (0, 0))
    return pl.pallas_call(
        functools.partial(weight_kernel, blocks, len(rights), weights is not None),
        out_shape=[jax.ShapeDtypeStruct((tall, right[0].shape[1]), out_type) for right in rights],
        grid=(tall // tile,),
        in_specs=[
            *[pl.BlockSpec((rows, tile), lambda i: (0, i))] * blocks,
            *[fixed(block) for block in flat],
            *([] if weights is None else [fixed(weight) for weight in weights]),
        ],
        out_specs=[
            pl.BlockSpec((tile, right[0].shape[1]), lambda i: (order(i), 0)) for right in rights
        ],
        scratch_shapes=[] if weights is None else [pltpu.VMEM(block.shape, bf16) for block in flat],
        compiler_params=pltpu.CompilerParams(vmem_limit_bytes=60 * 2**20),
        cost_estimate=pl.CostEstimate(flops=1000, bytes_accessed=1000, transcendentals=0),
        name="weight_gradients",
    )(*lefts, *flat, *([] if weights is None else weights))


def spread_kernel(with_units, *refs):
    block_refs, weight_ref, refs = refs[:4], refs[4], refs[5:]
    if with_units:
        unit_refs, refs = refs[:4], refs[4:]
    up_ref, down_ref, up_rest, down_rest, own_ref = refs[:5]
    weight = weight_ref[...]
    middle = own_ref.shape[0] // 2
    shares = {}
    for step in (2, 3, 1, 0):
        shares[step] = dot_nt(block_refs[step][...], weight)
    up_ref[:middle, :] = shares[2][:middle].astype(bf16)
    up_ref[middle:, :] = shares[3][middle:].astype(bf16)
    down_ref[:middle, :] = shares[1][:middle].astype(bf16)
    down_ref[middle:, :] = shares[2][middle:].astype(bf16)
    up_rest[...] = shares[3][:middle]
    down_rest[...] = shares[1][middle:]
    own_ref[...] = shares[0]
    if with_units:
        total = sum(
            jnp.sum(shares[step] * unit_refs[step][...], axis=0, keepdims=True) for step in range(4)
        )
        refs[5][...] = jnp.broadcast_to(total, refs[5].shape)


def spread(blocks, weight, units=None, tile=512):
    tokens, depth = blocks[0].shape
    width = weight.shape[0]
    part = lambda rows: pl.BlockSpec((rows, tile), lambda i: (0, i))
    shape = jax.ShapeDtypeStruct
    return pl.pallas_call(
        functools.partial(spread_kernel, units is not None),
        out_shape=[
            shape((tokens, width), bf16),
            shape((tokens, width), bf16),
            shape((tokens // 2, width), f32),
            shape((tokens // 2, width), f32),
            shape((tokens, width), f32),
            *([] if units is None else [shape((8, width), f32)]),
        ],
        grid=(width // tile,),
        in_specs=[
            *[pl.BlockSpec((tokens, depth), lambda i: (0, 0))] * 4,
            pl.BlockSpec((tile, depth), lambda i: (i, 0)),
            *([] if units is None else [part(tokens)] * 4),
        ],
        out_specs=[
            part(tokens),
            part(tokens),
            part(tokens // 2),
            part(tokens // 2),
            part(tokens),
            *([] if units is None else [part(8)]),
        ],
        compiler_params=pltpu.CompilerParams(vmem_limit_bytes=60 * 2**20),
        cost_estimate=pl.CostEstimate(flops=1000, bytes_accessed=1000, transcendentals=0),
        name="spread",
    )(*blocks, weight, *([] if units is None else units))


def product_kernel(transposed, left_ref, right_ref, *refs):
    result = (dot_tn if transposed else dot_nn)(left_ref[...], right_ref[...])
    if len(refs) > 1:
        result = result + refs[0][...].astype(f32)
    refs[-1][...] = result.astype(refs[-1].dtype)


def product(left, right, addend=None, out_type=bf16, transposed=False, tile=512):
    rows = left.shape[1 if transposed else 0]
    part = lambda height: pl.BlockSpec((height, tile), lambda i: (0, i))
    return pl.pallas_call(
        functools.partial(product_kernel, transposed),
        out_shape=jax.ShapeDtypeStruct((rows, right.shape[1]), out_type),
        grid=(right.shape[1] // tile,),
        in_specs=[
            pl.BlockSpec(left.shape, lambda i: (0, 0)),
            part(right.shape[0]),
            *([] if addend is None else [part(rows)]),
        ],
        out_specs=part(rows),
        compiler_params=pltpu.CompilerParams(vmem_limit_bytes=60 * 2**20),
        cost_estimate=pl.CostEstimate(flops=1000, bytes_accessed=1000, transcendentals=0),
        name="product",
    )(left, right, *([] if addend is None else [addend]))


def expert_kernel(
    rows_ref, upstream_ref, gate_ref, up_ref, down_ref,
    acted_ref, gate_grad_ref, up_grad_ref, row_grad_ref, returned_ref, dots_ref,
    gates, ups, downs, gate_grads, up_grads, acted_rows,
):
    step = pl.program_id(0)
    tile = gate_ref.shape[1]
    gate_part = dot_nn(rows_ref[...], gate_ref[...])
    up_part = dot_nn(rows_ref[...], up_ref[...])
    drive = dot_nt(upstream_ref[...], down_ref[...])
    sigmoid = jax.nn.sigmoid(gate_part)
    silu = gate_part * sigmoid
    acted = silu * up_part
    acted_low = acted.astype(bf16)
    gate_grad = (drive * up_part * sigmoid * (1.0 + gate_part * (1.0 - sigmoid))).astype(bf16)
    up_grad = (drive * silu).astype(bf16)
    acted_ref[...] = acted_low
    gate_grad_ref[...] = gate_grad
    up_grad_ref[...] = up_grad
    dots = jnp.sum(acted * drive, axis=1, keepdims=True)
    for index in range(gates.shape[1] // tile):

        @pl.when(step == index)
        def _():
            here = pl.ds(index * tile, tile)
            gates[:, here] = gate_ref[...]
            ups[:, here] = up_ref[...]
            downs[here, :] = down_ref[...]
            gate_grads[:, here] = gate_grad
            up_grads[:, here] = up_grad
            acted_rows[:, here] = acted_low

    @pl.when(step == 0)
    def _():
        dots_ref[...] = dots

    @pl.when(step > 0)
    def _():
        dots_ref[...] += dots

    @pl.when(step == pl.num_programs(0) - 1)
    def _():
        for first in range(0, row_grad_ref.shape[1], 512):
            here = pl.ds(first, 512)
            row_grad_ref[:, here] = (
                dot_nt(gate_grads[...], gates[here, :]) + dot_nt(up_grads[...], ups[here, :])
            ).astype(bf16)
            returned_ref[:, here] = dot_nn(acted_rows[...], downs[:, here]).astype(bf16)


def expert_block(rows, upstream_rows, gate_weight, up_weight, down_weight, tile=256):
    count, width = rows.shape
    hidden = gate_weight.shape[1]
    shape = jax.ShapeDtypeStruct
    whole = pl.BlockSpec((count, width), lambda j: (0, 0))
    part = pl.BlockSpec((count, tile), lambda j: (0, j))
    return pl.pallas_call(
        expert_kernel,
        out_shape=[
            shape((count, hidden), bf16),
            shape((count, hidden), bf16),
            shape((count, hidden), bf16),
            shape((count, width), bf16),
            shape((count, width), bf16),
            shape((count, 1), f32),
        ],
        grid=(hidden // tile,),
        in_specs=[
            whole,
            whole,
            pl.BlockSpec((width, tile), lambda j: (0, j)),
            pl.BlockSpec((width, tile), lambda j: (0, j)),
            pl.BlockSpec((tile, width), lambda j: (j, 0)),
        ],
        out_specs=[part, part, part, whole, whole, pl.BlockSpec((count, 1), lambda j: (0, 0))],
        scratch_shapes=[
            pltpu.VMEM((width, hidden), bf16),
            pltpu.VMEM((width, hidden), bf16),
            pltpu.VMEM((hidden, width), bf16),
            pltpu.VMEM((count, hidden), bf16),
            pltpu.VMEM((count, hidden), bf16),
            pltpu.VMEM((count, hidden), bf16),
        ],
        compiler_params=pltpu.CompilerParams(vmem_limit_bytes=60 * 2**20),
        cost_estimate=pl.CostEstimate(flops=1000, bytes_accessed=1000, transcendentals=0),
        name="expert_block",
    )(rows, upstream_rows, gate_weight, up_weight, down_weight)


def local(
    inputs,
    expert_ids,
    positions,
    cotangent,
    attn_gain,
    query_proj,
    key_projection,
    value_projection,
    query_norm_gain,
    key_norm_gain,
    out_proj,
    moe_gain,
    router,
    gate_proj,
    up_proj,
    down_proj,
):
    tokens, width = inputs.shape
    head_size = query_norm_gain.shape[0]
    choices = expert_ids.shape[1]
    experts = router.shape[1]
    capacity = tokens * choices * 5 // (4 * experts)
    columns = lax.axis_size("col")
    peers = lax.axis_size("dp") * lax.axis_size("exp")
    col = lax.axis_index("col")
    here = lax.axis_index("dp") * lax.axis_size("exp") + lax.axis_index("exp")
    col_array = jnp.reshape(col, (1,)).astype(jnp.int32)
    heads = query_proj.shape[1] // head_size
    assert key_projection.shape[1] == head_size and experts == peers * columns
    assert columns == 4 and tokens % 32 == 0
    middle = tokens // 2

    def shifted(block, by):
        return lax.ppermute(block, "col", [(i, (i + by) % columns) for i in range(columns)])

    def up(block):
        return shifted(block, 1)

    def down(block):
        return shifted(block, -1)

    def gather_near(block):
        return up(block), down(block)

    def gather_far(former, latter):
        return jnp.concatenate([up(former[:middle]), down(latter[middle:])], axis=0)

    def scatter_first(up_rows, down_rows, *_):
        return up(up_rows), down(down_rows)

    def scatter_second(first, up_rest, down_rest):
        return (
            up((up_rest + first[0][:middle].astype(f32)).astype(bf16)),
            down((down_rest + first[1][middle:].astype(f32)).astype(bf16)),
        )

    def scatter_own(own, first, second):
        return own + jnp.concatenate(
            [
                second[0].astype(f32) + first[1][:middle].astype(f32),
                first[0][middle:].astype(f32) + second[1].astype(f32),
            ],
            axis=0,
        )

    def swap(rows):
        return lax.all_to_all(
            rows.reshape(peers, rows.shape[0] // peers, *rows.shape[1:]), plane, 0, 0, tiled=True
        ).reshape(rows.shape)

    def swap_all(values):
        return lax.all_to_all(values, everyone, 0, 0, tiled=True)

    def after(value, *others):
        return lax.optimization_barrier((value, others))[0]

    def exchange_plane(values, steps):
        parts = {}
        for step in steps:
            part = lax.dynamic_index_in_dim(values, lax.rem(here + step, peers), 0, keepdims=False)
            pairs = [(i, (i + step) % peers) for i in range(peers)]
            parts[step] = lax.ppermute(part, plane, pairs) if step else part
        return parts

    def joined(parts):
        order = lax.rem(here - jnp.arange(peers, dtype=jnp.int32) + peers, peers)
        return jnp.take(jnp.stack([parts[step] for step in range(peers)]), order, axis=0)

    early_steps, late_steps = range(peers // 2), range(peers // 2, peers)

    def exchange_columns(values):
        parts = [values[:, 0], *[shifted(values[:, s], -s) for s in range(1, columns)]]
        return jnp.stack([parts[0], *parts[:0:-1]], axis=1)

    to_ring = lax.rem(col - jnp.arange(columns, dtype=jnp.int32) + columns, columns)

    earlier = (
        lax.broadcasted_iota(jnp.int32, (tokens, tokens), 0)
        < lax.broadcasted_iota(jnp.int32, (tokens, tokens), 1)
    ).astype(bf16)
    all_experts = jnp.arange(experts, dtype=jnp.int32)
    plane_experts = jnp.arange(peers, dtype=jnp.int32) * columns + col

    def chosen_in(ids, named):
        return jnp.any(ids[None, :, :] == named[:, None, None], axis=1)

    def slots_of(ids, named):
        chosen = chosen_in(ids, named)
        rank = dot_nn(chosen.astype(bf16), earlier)
        code = jnp.where(chosen, rank, -1.0)
        place = lax.broadcasted_iota(jnp.int32, (1, capacity, 1), 1).astype(f32)
        return chosen, code[:, None, :] == place

    def slot_mat(ids):
        return slots_of(ids, plane_experts)[1].astype(bf16).reshape(peers * capacity, tokens)

    def pick(step, block):
        return product(slot_mats[step], block)

    def gates_of(chosen, block):
        logits = jnp.where(chosen, dot_general_t(router, block), -1e30)
        exponent = jnp.exp(logits - jnp.max(logits, axis=0, keepdims=True))
        exponent = jnp.where(chosen, exponent, 0.0)
        return exponent / jnp.sum(exponent, axis=0, keepdims=True)

    def weighted_mat(step, block_gates):
        gates_here = block_gates.reshape(peers, columns, 1, tokens)
        gates_here = lax.dynamic_index_in_dim(gates_here, col, 1, keepdims=False)
        mat = slot_mats[step].reshape(peers, capacity, tokens) * gates_here
        return mat.astype(bf16).reshape(peers * capacity, tokens)

    def collect(back, step, addend=None, out_type=bf16):
        return product(weighted_mats[step], back[step], addend, out_type, transposed=True)

    near_inputs = gather_near(inputs)
    local_qkv = jnp.concatenate([query_proj, key_projection, value_projection], axis=1)
    full_qkv = lax.all_gather(local_qkv, "exp", axis=0, tiled=True)
    full_out = lax.all_gather(out_proj, "exp", axis=0, tiled=True)
    own_ids = expert_ids.T
    slot_mats = [slot_mat(own_ids)]
    cotangent_rows = [swap(pick(0, cotangent)), None, None, None]
    near_inputs, full_qkv = after((near_inputs, full_qkv))

    far_inputs = gather_far(*near_inputs)
    def project(block):
        rows = block.astype(f32)
        unit = rows * inverse_rms(rows)
        low = (unit * attn_gain).astype(bf16)
        return unit, low, dot_nn(low, full_qkv)

    projected = [project(inputs), project(near_inputs[0]), None, project(near_inputs[1])]
    cosine, sine = rotary_tables(positions, head_size)
    far_inputs, cotangent_rows[0], cosine, sine = after(
        (far_inputs, cotangent_rows[0], cosine, sine),
        [projected[s][2] for s in (0, 1, 3)],
    )

    near_cotangent = gather_near(after(cotangent, far_inputs))
    later_ids = after(own_ids, far_inputs)
    ids_blocks = [own_ids, *[shifted(later_ids, step) for step in range(1, columns)]]
    projected[2] = project(far_inputs)
    units, normed, qkv = zip(*projected)
    query_gain, key_gain = query_norm_gain[None, :], key_norm_gain[None, :]
    attended = attention_forward(col_array, qkv, cosine, sine, query_gain, key_gain, heads)
    shares = spread(attended, full_out)
    slot_mats += [slot_mat(ids_blocks[s]) for s in (1, 2, 3)]
    near_cotangent, shares, slot_mats = after((near_cotangent, shares, slot_mats))

    up_rows, down_rows, up_rest, down_rest, own_share = shares
    first_up = up(up_rows)
    far_cotangent = gather_far(*near_cotangent)
    cotangent_rows[1] = swap(pick(1, near_cotangent[0]))
    chosen_all, slots_all = slots_of(own_ids, all_experts)
    picked = pick(3, near_cotangent[1])
    first_up, far_cotangent, cotangent_rows[1], chosen_all, slots_all, down_rows, picked = after(
        (first_up, far_cotangent, cotangent_rows[1], chosen_all, slots_all, down_rows, picked)
    )
    first_down = down(down_rows)
    second_up = up((up_rest + first_up[:middle].astype(f32)).astype(bf16))
    cotangent_rows[3] = swap(picked)
    picked = pick(2, far_cotangent)
    first_down, second_up, cotangent_rows[3], picked = after(
        (first_down, second_up, cotangent_rows[3], picked)
    )

    second_down = down((down_rest + first_down[middle:].astype(f32)).astype(bf16))
    cotangent_rows[2] = swap(picked)
    gate_weight, up_weight, down_weight = gate_proj[0], up_proj[0], down_proj[0]
    branch_first, branch_second = (first_up, first_down), (second_up, second_down)
    hidden = inputs.astype(f32) + scatter_own(own_share, branch_first, branch_second)
    inverse_hidden = inverse_rms(hidden)
    routed = (hidden * inverse_hidden * moe_gain).astype(bf16)
    own_rows = after(pick(0, routed), cotangent_rows[2])

    acted_rows, gate_grads, up_grads, row_grads, returned, gate_dots = [], [], [], [], [], []

    def run_expert(step, rows):
        results = expert_block(rows, cotangent_rows[step], gate_weight, up_weight, down_weight)
        for held, result in zip((acted_rows, gate_grads, up_grads, row_grads, returned), results):
            held.append(result)
        gate_dots.append(results[5].reshape(peers, capacity))

    def block_mat(step):
        block_gates = gates_of(chosen_in(ids_blocks[step], all_experts), routed_blocks[step])
        return weighted_mat(step, block_gates)

    routed_blocks, arrived, weighted_mats = [routed], [], {}
    rows, next_rows = own_rows, None
    slot_parts = {}
    for step in range(columns):
        rows = swap(rows)
        coming = None
        if step < columns - 1:
            coming = up(routed_blocks[step])
            next_rows = pick(step + 1, coming)
        if step:
            run_expert(step - 1, arrived[step - 1])
        if step == 0:
            gates = gates_of(chosen_all, routed)
            gate_slots = jnp.sum(jnp.where(slots_all, gates[:, None, :], 0.0), axis=2)
            gate_slots = jnp.take(gate_slots.reshape(peers, columns, capacity), to_ring, axis=1)
            weighted_mats[0] = weighted_mat(0, gates)
            slot_parts = exchange_plane(gate_slots, early_steps)
        elif step == 1:
            slot_parts.update(exchange_plane(gate_slots, late_steps))
        elif step == 2:
            gate_slots = exchange_columns(joined(slot_parts))
            slot_parts = {}
        state = (rows, next_rows, coming, gate_slots, weighted_mats, slot_parts)
        rows, next_rows, coming, gate_slots, weighted_mats, slot_parts = after(state, row_grads)
        arrived.append(rows)
        routed_blocks.append(coming)
        rows = next_rows
    row_weights = [gate_slots[:, step].reshape(peers * capacity, 1) for step in range(columns)]

    row_grads = after(row_grads, arrived[3])
    grad_back = {1: swap(row_grads[1])}
    run_expert(3, arrived[3])
    weighted_mats[1] = block_mat(1)
    grad_back[1], row_grads, gate_dots, weighted_mats = after(
        (grad_back[1], row_grads, gate_dots, weighted_mats)
    )
    grad_back[2] = swap(row_grads[2])
    running = up(collect(grad_back, 1))
    dots = jnp.stack(gate_dots, axis=1)
    dot_parts = exchange_plane(dots, early_steps)
    weighted_mats[2] = block_mat(2)
    running, grad_back[2], dot_parts, weighted_mats = after(
        (running, grad_back[2], dot_parts, weighted_mats)
    )
    grad_back[3] = swap(after(row_grads[3], running))
    running = up(collect(grad_back, 2, running))
    dot_parts.update(exchange_plane(after(dots, grad_back[2]), late_steps))
    weighted_mats[3] = block_mat(3)
    running, grad_back[3], dot_parts, weighted_mats = after(
        (running, grad_back[3], dot_parts, weighted_mats)
    )
    grad_back[0] = swap(after(row_grads[0], running))
    running = up(collect(grad_back, 3, running))
    dots = jnp.take(exchange_columns(joined(dot_parts)), to_ring, axis=1).reshape(experts, capacity)
    running, grad_back[0], dots = after((running, grad_back[0], dots))

    grad_gates = jnp.sum(jnp.where(slots_all, dots[:, :, None], 0.0), axis=1)
    grad_logits = (
        gates * (grad_gates - jnp.sum(gates * grad_gates, axis=0, keepdims=True))
    ).astype(bf16)
    grad_routed = collect(grad_back, 0, running, f32) + lax.dot_general(
        grad_logits, router, (((0,), (1,)), ((), ())), preferred_element_type=f32
    )
    scaled = grad_routed * moe_gain
    grad_hidden = (
        cotangent.astype(f32)
        + scaled * inverse_hidden
        - hidden * (jnp.mean(hidden * scaled, axis=-1, keepdims=True) * inverse_hidden**3)
    )
    grad_moe_gain = jnp.sum(grad_routed * hidden * inverse_hidden, axis=0)
    grad_router = dot_general_t(routed, grad_logits)

    grad_low = grad_hidden.astype(bf16)
    near_gradient = gather_near(grad_low)
    output_back = {1: swap(after(returned[1], grad_low))}
    grad_attended = {0: product(grad_low, full_out)}
    grad_gate_weight, grad_up_weight = weight_gradients(
        after(arrived, grad_low), [gate_grads, up_grads], f32, row_weights
    )
    near_gradient, output_back[1], grad_gate_weight, grad_attended = after(
        (near_gradient, output_back[1], grad_gate_weight, grad_attended)
    )

    far_gradient = gather_far(*near_gradient)
    output_back[2] = swap(after(returned[2], near_gradient))
    grad_attended.update({1: product(near_gradient[0], full_out), 3: product(near_gradient[1], full_out)})
    output_part = collect(output_back, 1)
    router_sums = grad_router.reshape(1, columns, width // columns * experts)
    router_sums = jnp.take(after(router_sums, near_gradient), to_ring, axis=1)
    router_sums = jnp.sum(exchange_columns(router_sums)[0], axis=0)
    far_gradient, output_back[2], grad_attended, output_part, router_sums = after(
        (far_gradient, output_back[2], grad_attended, output_part, router_sums)
    )

    grad_sequence = [grad_low, near_gradient[0], far_gradient, near_gradient[1]]
    running = up(output_part)
    output_back[3] = swap(after(returned[3], output_back[2]))
    grad_attended[2] = product(far_gradient, full_out)
    grad_attended = [grad_attended[s] for s in range(columns)]
    half = heads // 2
    arguments = (col_array, qkv, grad_attended, cosine, sine, query_gain, key_gain, heads)
    first_half = attention_backward(*arguments, 0, half)
    first_half, running = after((first_half, running))
    running = up(collect(output_back, 2, running))
    *grad_qkv, grad_query_gain, grad_key_gain, _, _ = attention_backward(
        *arguments, half, heads - half, first_half
    )
    grad_query_gain, grad_key_gain = grad_query_gain[0], grad_key_gain[0]

    *shares, attn_gain_sums = spread(grad_qkv, full_qkv, units)
    up_rows, down_rows, up_rest, down_rest, own_share = shares
    first_up, first_down = up(up_rows), down(down_rows)
    output_part = collect(after(output_back, attn_gain_sums), 3, running)
    output_back[0] = swap(after(returned[0], output_back[3], attn_gain_sums))
    (grad_down,) = weight_gradients(
        after(acted_rows, attn_gain_sums), [cotangent_rows], f32, row_weights
    )
    first_up, grad_down, output_part = after((first_up, grad_down, output_part))

    second_up = up((up_rest + first_up[:middle].astype(f32)).astype(bf16))
    running = up(output_part)
    dp, exp = lax.axis_size("dp"), lax.axis_size("exp")
    tile = min(256, width // (dp * exp))
    in_order = tile % 128 == 0
    order = (lambda i: i % exp * dp + i // exp) if in_order else None

    def weight_sums(lefts, right):
        (grads,) = weight_gradients(lefts, [right], bf16, tile=tile if in_order else 256, order=order)
        rows, wide = width // (dp * exp), grads.shape[1]
        if not in_order:
            grads = grads.reshape(dp, exp, rows, wide).transpose(1, 0, 2, 3)
        grads = grads.reshape(exp, dp * rows, wide)
        mine = lax.axis_index("exp")
        total = lax.dynamic_index_in_dim(grads, mine, 0, keepdims=False).astype(f32)
        for step in range(1, exp):
            part = lax.dynamic_index_in_dim(grads, lax.rem(mine + step, exp), 0, keepdims=False)
            part = lax.ppermute(part, "exp", [(i, (i + step) % exp) for i in range(exp)])
            total = total + part.astype(f32)
        return total.astype(bf16)

    out_sums = weight_sums(after(grad_sequence, first_up), attended)
    reduced_out = lax.psum_scatter(out_sums, "dp", scatter_dimension=0, tiled=True).astype(f32)
    qkv_sums = weight_sums(normed, after(grad_qkv, out_sums))

    small = jnp.concatenate([attn_gain_sums[0], grad_query_gain, grad_key_gain, grad_moe_gain])
    cuts = [0, width, width + head_size, width + 2 * head_size, 2 * (width + head_size)]
    small = jnp.concatenate([small, router_sums])
    small = swap(after(jnp.broadcast_to(small, (peers, small.shape[0])), output_back[0]))
    first_down, second_up, qkv_sums, small = after((first_down, second_up, qkv_sums, small))

    second_down = down((down_rest + first_down[middle:].astype(f32)).astype(bf16))
    qkv_parts = lax.all_to_all(
        qkv_sums.reshape(dp, -1, qkv_sums.shape[1]), "dp", 0, 0, tiled=True
    )
    reduced_qkv = jnp.sum(qkv_parts.astype(f32), axis=0)
    outputs = (hidden + collect(output_back, 0, running, f32)).astype(bf16)
    small = jnp.sum(small, axis=0)
    small = jnp.stack([small, *[shifted(small, step) for step in range(1, columns)]])
    to_true = lax.rem(col - jnp.arange(columns, dtype=jnp.int32) + columns, columns)
    grad_router = jnp.take(small[:, cuts[-1] :], to_true, axis=0).reshape(width, experts)
    small = jnp.sum(small[:, : cuts[-1]], axis=0)
    shared = [small[i:j] for i, j in zip(cuts, cuts[1:])]

    grad_normed = scatter_own(own_share, (first_up, first_down), (second_up, second_down))
    input_rows = inputs.astype(f32)
    inverse_own = inverse_rms(input_rows)
    scaled_in = grad_normed * attn_gain
    grad_inputs = (
        grad_hidden
        + scaled_in * inverse_own
        - input_rows * (jnp.mean(input_rows * scaled_in, axis=-1, keepdims=True) * inverse_own**3)
    ).astype(bf16)

    split = heads * head_size
    return (
        outputs,
        grad_inputs,
        shared[0],
        reduced_qkv[:, :split],
        reduced_qkv[:, split : split + head_size],
        reduced_qkv[:, split + head_size :],
        shared[1],
        shared[2],
        reduced_out,
        shared[3],
        grad_router,
        grad_gate_weight[None],
        grad_up_weight[None],
        grad_down[None],
    )


def dot_general_t(a, b):
    contract = (((0,), (1,)), ((), ()))
    return lax.dot_general(a, b, contract, preferred_element_type=f32)


def solution(mesh):
    return jax.shard_map(
        local,
        mesh=mesh,
        in_specs=(
            P(("dp", "exp", "col"), None),
            P(("dp", "exp", "col"), None),
            P(("dp", "exp")),
            P(("dp", "exp", "col"), None),
            P(),
            P("exp", "col"),
            P("exp", "col"),
            P("exp", "col"),
            P(),
            P(),
            P("exp", "col"),
            P(),
            P(),
            P(("dp", "exp", "col"), None, None),
            P(("dp", "exp", "col"), None, None),
            P(("dp", "exp", "col"), None, None),
        ),
        out_specs=(
            P(("dp", "exp", "col"), None),
            P(("dp", "exp", "col"), None),
            P(),
            P(("dp", "exp"), "col"),
            P(("dp", "exp"), "col"),
            P(("dp", "exp"), "col"),
            P(),
            P(),
            P(("dp", "exp"), "col"),
            P(),
            P(),
            P(("dp", "exp", "col"), None, None),
            P(("dp", "exp", "col"), None, None),
            P(("dp", "exp", "col"), None, None),
        ),
        check_vma=False,
    )
```

```python
import functools
import math

import jax
import jax.numpy as jnp
from jax import lax
from jax.experimental import pallas as pl
from jax.experimental.pallas import tpu as pltpu
from jax.sharding import PartitionSpec as P

epsilon = 1e-06
rotary_base = 1000000.0
plane = ("dp", "exp")
everyone = ("dp", "exp", "col")
f32 = jnp.float32
bf16 = jnp.bfloat16


def dot_nn(a, b):
    return lax.dot_general(a, b, (((1,), (0,)), ((), ())), preferred_element_type=f32)


def dot_nt(a, b):
    return lax.dot_general(a, b, (((1,), (1,)), ((), ())), preferred_element_type=f32)


def dot_tn(a, b):
    return lax.dot_general(a, b, (((0,), (0,)), ((), ())), preferred_element_type=f32)


def inverse_rms(rows):
    return lax.rsqrt(jnp.mean(rows * rows, axis=-1, keepdims=True) + epsilon)


def rotary_tables(positions, head_size):
    halves = head_size // 2
    frequency = rotary_base ** (-2.0 * jnp.arange(halves, dtype=f32) / head_size)
    angles = positions.astype(f32)[:, None] * frequency[None, :]
    cosine, sine = jnp.cos(angles), jnp.sin(angles)
    return (
        jnp.concatenate([cosine, cosine], axis=1),
        jnp.concatenate([-sine, sine], axis=1),
    )


def turn(rows, cosine, sine):
    return rows * cosine + pltpu.roll(rows, rows.shape[-1] // 2, 1) * sine


def turn_back(rows, cosine, sine):
    return rows * cosine - pltpu.roll(rows, rows.shape[-1] // 2, 1) * sine


def place_of(col_ref, blocks, tokens, step):
    return pl.multiple_of(lax.rem(col_ref[0] - step + blocks, blocks) * tokens, tokens)


def in_order(col_ref, refs, held):
    tokens = refs[0].shape[0]
    for step, ref in enumerate(refs):
        held[pl.ds(place_of(col_ref, len(refs), tokens, step), tokens), :] = ref[...].astype(held.dtype)


def out_of_order(col_ref, held, refs):
    tokens = refs[0].shape[0]
    for step, ref in enumerate(refs):
        ref[...] = held[pl.ds(place_of(col_ref, len(refs), tokens, step), tokens), :].astype(ref.dtype)


def scores_of(keys, query, first, scale):
    count = query.shape[0]
    scores = dot_nt(keys[pl.ds(0, first + count), :], query) * (scale * math.log2(math.e))
    row = lax.broadcasted_iota(jnp.int32, (count, count), 0)
    column = lax.broadcasted_iota(jnp.int32, (count, count), 1)
    last = jnp.where(row <= column, scores[first:], -1e30)
    return jnp.concatenate([scores[:first], last], axis=0) if first else last


def prepare_keys(col_ref, k_refs, v_refs, cos_ref, sin_ref, kg_ref, raw_rows, keys, values):
    in_order(col_ref, k_refs, raw_rows)
    in_order(col_ref, v_refs, values)
    tokens = k_refs[0].shape[0]
    for block in range(len(k_refs)):
        there = pl.ds(block * tokens, tokens)
        raw = raw_rows[there, :]
        rows = raw * inverse_rms(raw) * kg_ref[...]
        keys[there, :] = turn(rows, cos_ref[there, :], sin_ref[there, :]).astype(bf16)


def forward_kernel(blocks, scale, col_ref, *refs):
    q_refs, k_refs, v_refs = refs[:blocks], refs[blocks : 2 * blocks], refs[2 * blocks : 3 * blocks]
    cos_ref, sin_ref, qg_ref, kg_ref = refs[3 * blocks : 3 * blocks + 4]
    out_refs = refs[3 * blocks + 4 : 4 * blocks + 4]
    level_ref, raw_rows, keys, values, mixed_rows = refs[4 * blocks + 4 :]
    tokens = q_refs[0].shape[0]

    @pl.when(pl.program_id(0) == 0)
    def _():
        prepare_keys(col_ref, k_refs, v_refs, cos_ref, sin_ref, kg_ref, raw_rows, keys, values)

    in_order(col_ref, q_refs, raw_rows)
    for block in range(blocks):
        first = block * tokens
        there = pl.ds(first, tokens)
        raw = raw_rows[there, :]
        rows = raw * inverse_rms(raw) * qg_ref[...]
        query = turn(rows, cos_ref[there, :], sin_ref[there, :]).astype(bf16)
        scores = scores_of(keys, query, first, scale)
        peak = jnp.max(scores, axis=0, keepdims=True)
        probs = jnp.exp2(scores - peak)
        total = jnp.sum(probs, axis=0, keepdims=True)
        level_ref[0, :, there] = peak + jnp.log2(total)
        probs = (probs * (1.0 / total)).astype(bf16)
        mixed_rows[there, :] = dot_tn(probs, values[pl.ds(0, first + tokens), :]).astype(bf16)
    out_of_order(col_ref, mixed_rows, out_refs)


def attention_forward(col, qkv, cosine, sine, query_gain, key_gain, heads):
    blocks, tokens, head_size = len(qkv), qkv[0].shape[0], query_gain.shape[-1]
    seq_len = blocks * tokens
    column = lambda index: [pl.BlockSpec((tokens, head_size), index)] * blocks
    whole = pl.BlockSpec((seq_len, head_size), lambda h, c: (0, 0))
    gain = pl.BlockSpec((1, head_size), lambda h, c: (0, 0))
    return pl.pallas_call(
        functools.partial(forward_kernel, blocks, head_size ** (-0.5)),
        out_shape=[
            *[jax.ShapeDtypeStruct((tokens, heads * head_size), bf16)] * blocks,
            jax.ShapeDtypeStruct((heads, 1, seq_len), f32),
        ],
        grid_spec=pltpu.PrefetchScalarGridSpec(
            num_scalar_prefetch=1,
            grid=(heads,),
            in_specs=[
                *column(lambda h, c: (0, h)),
                *column(lambda h, c: (0, heads)),
                *column(lambda h, c: (0, heads + 1)),
                whole,
                whole,
                gain,
                gain,
            ],
            out_specs=[
                *column(lambda h, c: (0, h)),
                pl.BlockSpec((1, 1, seq_len), lambda h, c: (h, 0, 0)),
            ],
            scratch_shapes=[
                pltpu.VMEM((seq_len, head_size), f32),
                pltpu.VMEM((seq_len, head_size), bf16),
                pltpu.VMEM((seq_len, head_size), bf16),
                pltpu.VMEM((seq_len, head_size), bf16),
            ],
        ),
        compiler_params=pltpu.CompilerParams(vmem_limit_bytes=60 * 2**20),
        cost_estimate=pl.CostEstimate(flops=1000, bytes_accessed=1000, transcendentals=0),
        name="attention_forward",
    )(col, *qkv, *qkv, *qkv, cosine, sine, query_gain, key_gain)


def backward_kernel(blocks, scale, first_head, heads, final, col_ref, *refs):
    q_refs, k_refs, v_refs, g_refs = (refs[i * blocks : (i + 1) * blocks] for i in range(4))
    cos_ref, sin_ref, qg_ref, kg_ref, level_ref = refs[4 * blocks : 4 * blocks + 5]
    refs = refs[4 * blocks + 5 :]
    if first_head:
        refs = refs[blocks:]
        held_refs, refs = refs[:4], refs[4:]
    grad_refs, refs = refs[:blocks], refs[blocks:]
    qgain_ref, kgain_ref, out_keys, out_values = refs[:4]
    raw_rows, mixed_rows, keys, values, grad_rows, grad_keys, grad_values = refs[4:]
    tokens = q_refs[0].shape[0]
    step = pl.program_id(0)

    @pl.when(step == 0)
    def _():
        prepare_keys(col_ref, k_refs, v_refs, cos_ref, sin_ref, kg_ref, raw_rows, keys, values)
        if first_head:
            qgain_ref[...] = held_refs[0][...]
            kgain_ref[...] = held_refs[1][...]
            grad_keys[...] = held_refs[2][...]
            grad_values[...] = held_refs[3][...]
        else:
            grad_keys[...] = jnp.zeros_like(grad_keys)
            grad_values[...] = jnp.zeros_like(grad_values)
            qgain_ref[...] = jnp.zeros_like(qgain_ref)
            kgain_ref[...] = jnp.zeros_like(kgain_ref)

    def through_norm(grad_rot, unit, inverse, there, gain_ref, gain_grad_ref):
        grad_scaled = turn_back(grad_rot, cos_ref[there, :], sin_ref[there, :])
        gain_grad_ref[0:1, :] += jnp.sum(grad_scaled * unit, axis=0, keepdims=True)
        grad_unit = grad_scaled * gain_ref[...]
        return inverse * (grad_unit - unit * jnp.mean(grad_unit * unit, axis=1, keepdims=True))

    @pl.when(step < heads)
    def _():
        in_order(col_ref, q_refs, raw_rows)
        in_order(col_ref, g_refs, mixed_rows)
        for block in range(blocks):
            first = block * tokens
            there = pl.ds(first, tokens)
            raw = raw_rows[there, :]
            inverse = inverse_rms(raw)
            unit = raw * inverse
            query = turn(unit * qg_ref[...], cos_ref[there, :], sin_ref[there, :]).astype(bf16)
            grad_mixed = mixed_rows[there, :]
            upto = pl.ds(0, first + tokens)
            probs = jnp.exp2(scores_of(keys, query, first, scale) - level_ref[0, :, there])
            grad_probs = dot_nt(values[upto, :], grad_mixed)
            inner = jnp.sum(probs * grad_probs, axis=0, keepdims=True)
            grad_scores = (probs * (grad_probs - inner)).astype(bf16)
            grad_values[upto, :] += dot_nn(probs.astype(bf16), grad_mixed)
            grad_keys[upto, :] += dot_nn(grad_scores, query)
            grad_query = dot_tn(grad_scores, keys[upto, :])
            grad_rows[there, :] = through_norm(
                grad_query * scale, unit, inverse, there, qg_ref, qgain_ref
            ).astype(bf16)

    if not final:

        @pl.when(step == heads - 1)
        def _():
            out_keys[...] = grad_keys[...]
            out_values[...] = grad_values[...]

    @pl.when(step == heads)
    def _():
        in_order(col_ref, k_refs, raw_rows)
        for block in range(blocks):
            there = pl.ds(block * tokens, tokens)
            raw = raw_rows[there, :]
            inverse = inverse_rms(raw)
            grad_rows[there, :] = through_norm(
                grad_keys[there, :] * scale, raw * inverse, inverse, there, kg_ref, kgain_ref
            ).astype(bf16)

    @pl.when(step == heads + 1)
    def _():
        grad_rows[...] = grad_values[...].astype(bf16)

    out_of_order(col_ref, grad_rows, grad_refs)


def attention_backward(
    col, qkv, grad_attended, cosine, sine, query_gain, key_gain, levels, first, heads, former=None
):
    blocks, tokens, head_size = len(qkv), qkv[0].shape[0], query_gain.shape[-1]
    seq_len = blocks * tokens
    all_heads = levels.shape[0]
    final = first + heads == all_heads
    column = lambda index: [pl.BlockSpec((tokens, head_size), index)] * blocks
    whole = pl.BlockSpec((seq_len, head_size), lambda h, c: (0, 0))
    gain = pl.BlockSpec((1, head_size), lambda h, c: (0, 0))
    gain_out = pl.BlockSpec((8, head_size), lambda h, c: (0, 0))
    last = all_heads - 1
    held = [] if former is None else former
    return pl.pallas_call(
        functools.partial(backward_kernel, blocks, head_size ** (-0.5), first, heads, final),
        out_shape=[
            *[jax.ShapeDtypeStruct(qkv[0].shape, bf16)] * blocks,
            jax.ShapeDtypeStruct((8, head_size), f32),
            jax.ShapeDtypeStruct((8, head_size), f32),
            jax.ShapeDtypeStruct((seq_len, head_size), f32),
            jax.ShapeDtypeStruct((seq_len, head_size), f32),
        ],
        grid_spec=pltpu.PrefetchScalarGridSpec(
            num_scalar_prefetch=1,
            grid=(heads + 2 if final else heads,),
            in_specs=[
                *column(lambda h, c: (0, jnp.minimum(h + first, last))),
                *column(lambda h, c: (0, all_heads)),
                *column(lambda h, c: (0, all_heads + 1)),
                *column(lambda h, c: (0, jnp.minimum(h + first, last))),
                whole,
                whole,
                gain,
                gain,
                pl.BlockSpec((1, 1, seq_len), lambda h, c: (jnp.minimum(h + first, last), 0, 0)),
                *([] if former is None else [pl.BlockSpec(memory_space=pl.ANY)] * blocks),
                *([] if former is None else [gain_out, gain_out, whole, whole]),
            ],
            out_specs=[*column(lambda h, c: (0, h + first)), gain_out, gain_out, whole, whole],
            scratch_shapes=[
                pltpu.VMEM((seq_len, head_size), f32),
                pltpu.VMEM((seq_len, head_size), bf16),
                pltpu.VMEM((seq_len, head_size), bf16),
                pltpu.VMEM((seq_len, head_size), bf16),
                pltpu.VMEM((seq_len, head_size), bf16),
                pltpu.VMEM((seq_len, head_size), f32),
                pltpu.VMEM((seq_len, head_size), f32),
            ],
        ),
        input_output_aliases={} if former is None else {1 + 4 * blocks + 5 + i: i for i in range(blocks)},
        compiler_params=pltpu.CompilerParams(vmem_limit_bytes=60 * 2**20),
        cost_estimate=pl.CostEstimate(flops=1000, bytes_accessed=1000, transcendentals=0),
        name="attention_backward",
    )(col, *qkv, *qkv, *qkv, *grad_attended, cosine, sine, query_gain, key_gain, levels, *held)


def weight_kernel(blocks, rights, weighted, *refs):
    left_refs, refs = refs[:blocks], refs[blocks:]
    right_refs, refs = refs[: blocks * rights], refs[blocks * rights :]
    if weighted:
        weight_refs, refs = refs[:blocks], refs[blocks:]
        out_refs, held = refs[:rights], refs[rights:]

        @pl.when(pl.program_id(0) == 0)
        def _():
            for index, ref in enumerate(right_refs):
                scaled = ref[...].astype(f32) * weight_refs[index % blocks][...]
                held[index][...] = scaled.astype(bf16)

        right_refs = held
    else:
        out_refs = refs
    for index, out_ref in enumerate(out_refs):
        total = dot_tn(left_refs[0][...], right_refs[index * blocks][...])
        for block in range(1, blocks):
            total = total + dot_tn(left_refs[block][...], right_refs[index * blocks + block][...])
        out_ref[...] = total.astype(out_ref.dtype)


def weight_gradients(lefts, rights, out_type, weights=None, tile=256):
    blocks, rows, tall = len(lefts), lefts[0].shape[0], lefts[0].shape[1]
    flat = [block for right in rights for block in right]
    fixed = lambda array: pl.BlockSpec(array.shape, lambda i: (0, 0))
    return pl.pallas_call(
        functools.partial(weight_kernel, blocks, len(rights), weights is not None),
        out_shape=[jax.ShapeDtypeStruct((tall, right[0].shape[1]), out_type) for right in rights],
        grid=(tall // tile,),
        in_specs=[
            *[pl.BlockSpec((rows, tile), lambda i: (0, i))] * blocks,
            *[fixed(block) for block in flat],
            *([] if weights is None else [fixed(weight) for weight in weights]),
        ],
        out_specs=[
            pl.BlockSpec((tile, right[0].shape[1]), lambda i: (i, 0)) for right in rights
        ],
        scratch_shapes=[] if weights is None else [pltpu.VMEM(block.shape, bf16) for block in flat],
        compiler_params=pltpu.CompilerParams(vmem_limit_bytes=60 * 2**20),
        cost_estimate=pl.CostEstimate(flops=1000, bytes_accessed=1000, transcendentals=0),
        name="weight_gradients",
    )(*lefts, *flat, *([] if weights is None else weights))


def split_kernel(blocks, groups, mine_ref, *refs):
    left_refs, right_refs, out_refs = refs[:blocks], refs[blocks : 2 * blocks], refs[2 * blocks :]
    total = dot_tn(left_refs[0][...], right_refs[0][...])
    for block in range(1, blocks):
        total = total + dot_tn(left_refs[block][...], right_refs[block][...])
    for index, out_ref in enumerate(out_refs):

        @pl.when(pl.program_id(0) // groups == index)
        def _():
            out_ref[...] = total.astype(out_ref.dtype)


def split_gradient(lefts, right, mine, devices, groups):
    blocks, rows, tall = len(lefts), lefts[0].shape[0], lefts[0].shape[1]
    tile, wide = tall // (devices * groups), right[0].shape[1]

    def left_tile(i, mine_ref):
        return (0, i % groups * devices + lax.rem(mine_ref[0] + i // groups, devices))

    def out_tile(index):
        return lambda i, mine_ref: (jnp.clip(i - index * groups, 0, groups - 1), 0)

    return pl.pallas_call(
        functools.partial(split_kernel, blocks, groups),
        out_shape=[jax.ShapeDtypeStruct((groups * tile, wide), bf16)] * devices,
        grid_spec=pltpu.PrefetchScalarGridSpec(
            num_scalar_prefetch=1,
            grid=(devices * groups,),
            in_specs=[
                *[pl.BlockSpec((rows, tile), left_tile)] * blocks,
                *[pl.BlockSpec((rows, wide), lambda i, mine_ref: (0, 0))] * blocks,
            ],
            out_specs=[pl.BlockSpec((tile, wide), out_tile(index)) for index in range(devices)],
        ),
        compiler_params=pltpu.CompilerParams(vmem_limit_bytes=60 * 2**20),
        cost_estimate=pl.CostEstimate(flops=1000, bytes_accessed=1000, transcendentals=0),
        name="split_gradient",
    )(mine, *lefts, *right)


def spread_kernel(with_units, *refs):
    block_refs, weight_ref, refs = refs[:4], refs[4], refs[5:]
    if with_units:
        unit_refs, refs = refs[:4], refs[4:]
    far_up, far_down, free_up, free_down, up_rest, down_rest, own_ref = refs[:7]
    weight = weight_ref[...]
    middle = own_ref.shape[0] // 2
    shares = {}
    for step in (2, 3, 1, 0):
        shares[step] = dot_nt(block_refs[step][...], weight)
    far_up[...] = shares[2][:middle].astype(bf16)
    far_down[...] = shares[2][middle:].astype(bf16)
    free_up[...] = shares[3][middle:].astype(bf16)
    free_down[...] = shares[1][:middle].astype(bf16)
    up_rest[...] = shares[3][:middle]
    down_rest[...] = shares[1][middle:]
    own_ref[...] = shares[0]
    if with_units:
        total = sum(
            jnp.sum(shares[step] * unit_refs[step][...], axis=0, keepdims=True) for step in range(4)
        )
        refs[7][...] = jnp.broadcast_to(total, refs[7].shape)


def spread(blocks, weight, units=None, tile=512):
    tokens, depth = blocks[0].shape
    width = weight.shape[0]
    part = lambda rows: pl.BlockSpec((rows, tile), lambda i: (0, i))
    shape = jax.ShapeDtypeStruct
    return pl.pallas_call(
        functools.partial(spread_kernel, units is not None),
        out_shape=[
            *[shape((tokens // 2, width), bf16)] * 4,
            *[shape((tokens // 2, width), f32)] * 2,
            shape((tokens, width), f32),
            *([] if units is None else [shape((8, width), f32)]),
        ],
        grid=(width // tile,),
        in_specs=[
            *[pl.BlockSpec((tokens, depth), lambda i: (0, 0))] * 4,
            pl.BlockSpec((tile, depth), lambda i: (i, 0)),
            *([] if units is None else [part(tokens)] * 4),
        ],
        out_specs=[
            *[part(tokens // 2)] * 6,
            part(tokens),
            *([] if units is None else [part(8)]),
        ],
        compiler_params=pltpu.CompilerParams(vmem_limit_bytes=60 * 2**20),
        cost_estimate=pl.CostEstimate(flops=1000, bytes_accessed=1000, transcendentals=0),
        name="spread",
    )(*blocks, weight, *([] if units is None else units))


def product_kernel(transposed, left_ref, right_ref, *refs):
    result = (dot_tn if transposed else dot_nn)(left_ref[...], right_ref[...])
    if len(refs) > 1:
        result = result + refs[0][...].astype(f32)
    refs[-1][...] = result.astype(refs[-1].dtype)


def product(left, right, addend=None, out_type=bf16, transposed=False, tile=512):
    rows = left.shape[1 if transposed else 0]
    part = lambda height: pl.BlockSpec((height, tile), lambda i: (0, i))
    return pl.pallas_call(
        functools.partial(product_kernel, transposed),
        out_shape=jax.ShapeDtypeStruct((rows, right.shape[1]), out_type),
        grid=(right.shape[1] // tile,),
        in_specs=[
            pl.BlockSpec(left.shape, lambda i: (0, 0)),
            part(right.shape[0]),
            *([] if addend is None else [part(rows)]),
        ],
        out_specs=part(rows),
        compiler_params=pltpu.CompilerParams(vmem_limit_bytes=60 * 2**20),
        cost_estimate=pl.CostEstimate(flops=1000, bytes_accessed=1000, transcendentals=0),
        name="product",
    )(left, right, *([] if addend is None else [addend]))


def expert_kernel(
    rows_ref, upstream_ref, gate_ref, up_ref, down_ref,
    acted_ref, gate_grad_ref, up_grad_ref, row_grad_ref, returned_ref, dots_ref,
    gates, ups, downs, gate_grads, up_grads, acted_rows,
):
    step = pl.program_id(0)
    tile = gate_ref.shape[1]
    gate_part = dot_nn(rows_ref[...], gate_ref[...])
    up_part = dot_nn(rows_ref[...], up_ref[...])
    drive = dot_nt(upstream_ref[...], down_ref[...])
    sigmoid = jax.nn.sigmoid(gate_part)
    silu = gate_part * sigmoid
    acted = silu * up_part
    acted_low = acted.astype(bf16)
    gate_grad = (drive * up_part * sigmoid * (1.0 + gate_part * (1.0 - sigmoid))).astype(bf16)
    up_grad = (drive * silu).astype(bf16)
    acted_ref[...] = acted_low
    gate_grad_ref[...] = gate_grad
    up_grad_ref[...] = up_grad
    dots = jnp.sum(acted * drive, axis=1, keepdims=True)
    for index in range(gates.shape[1] // tile):

        @pl.when(step == index)
        def _():
            here = pl.ds(index * tile, tile)
            gates[:, here] = gate_ref[...]
            ups[:, here] = up_ref[...]
            downs[here, :] = down_ref[...]
            gate_grads[:, here] = gate_grad
            up_grads[:, here] = up_grad
            acted_rows[:, here] = acted_low

    @pl.when(step == 0)
    def _():
        dots_ref[...] = dots

    @pl.when(step > 0)
    def _():
        dots_ref[...] += dots

    @pl.when(step == pl.num_programs(0) - 1)
    def _():
        for first in range(0, row_grad_ref.shape[1], 512):
            here = pl.ds(first, 512)
            row_grad_ref[:, here] = (
                dot_nt(gate_grads[...], gates[here, :]) + dot_nt(up_grads[...], ups[here, :])
            ).astype(bf16)
            returned_ref[:, here] = dot_nn(acted_rows[...], downs[:, here]).astype(bf16)


def expert_block(rows, upstream_rows, gate_weight, up_weight, down_weight, tile=256):
    count, width = rows.shape
    hidden = gate_weight.shape[1]
    shape = jax.ShapeDtypeStruct
    whole = pl.BlockSpec((count, width), lambda j: (0, 0))
    part = pl.BlockSpec((count, tile), lambda j: (0, j))
    return pl.pallas_call(
        expert_kernel,
        out_shape=[
            shape((count, hidden), bf16),
            shape((count, hidden), bf16),
            shape((count, hidden), bf16),
            shape((count, width), bf16),
            shape((count, width), bf16),
            shape((count, 1), f32),
        ],
        grid=(hidden // tile,),
        in_specs=[
            whole,
            whole,
            pl.BlockSpec((width, tile), lambda j: (0, j)),
            pl.BlockSpec((width, tile), lambda j: (0, j)),
            pl.BlockSpec((tile, width), lambda j: (j, 0)),
        ],
        out_specs=[part, part, part, whole, whole, pl.BlockSpec((count, 1), lambda j: (0, 0))],
        scratch_shapes=[
            pltpu.VMEM((width, hidden), bf16),
            pltpu.VMEM((width, hidden), bf16),
            pltpu.VMEM((hidden, width), bf16),
            pltpu.VMEM((count, hidden), bf16),
            pltpu.VMEM((count, hidden), bf16),
            pltpu.VMEM((count, hidden), bf16),
        ],
        compiler_params=pltpu.CompilerParams(vmem_limit_bytes=60 * 2**20),
        cost_estimate=pl.CostEstimate(flops=1000, bytes_accessed=1000, transcendentals=0),
        name="expert_block",
    )(rows, upstream_rows, gate_weight, up_weight, down_weight)


def local(
    inputs,
    expert_ids,
    positions,
    cotangent,
    attn_gain,
    query_proj,
    key_projection,
    value_projection,
    query_norm_gain,
    key_norm_gain,
    out_proj,
    moe_gain,
    router,
    gate_proj,
    up_proj,
    down_proj,
):
    tokens, width = inputs.shape
    head_size = query_norm_gain.shape[0]
    choices = expert_ids.shape[1]
    experts = router.shape[1]
    capacity = tokens * choices * 5 // (4 * experts)
    columns = lax.axis_size("col")
    peers = lax.axis_size("dp") * lax.axis_size("exp")
    col = lax.axis_index("col")
    here = lax.axis_index("dp") * lax.axis_size("exp") + lax.axis_index("exp")
    col_array = jnp.reshape(col, (1,)).astype(jnp.int32)
    heads = query_proj.shape[1] // head_size
    assert key_projection.shape[1] == head_size and experts == peers * columns
    assert columns == 4 and tokens % 32 == 0
    middle = tokens // 2

    def shifted(block, by):
        return lax.ppermute(block, "col", [(i, (i + by) % columns) for i in range(columns)])

    def up(block):
        return shifted(block, 1)

    def down(block):
        return shifted(block, -1)

    def gather_near(block):
        return up(block), down(block)

    def gather_far(former, latter):
        return up(former[:middle]), down(latter[middle:])

    def scatter_second(rest, far):
        return (rest + far.astype(f32)).astype(bf16)

    def scatter_own(own, second_up, second_down, free_up, free_down):
        return own + jnp.concatenate(
            [
                second_up.astype(f32) + free_down.astype(f32),
                free_up.astype(f32) + second_down.astype(f32),
            ],
            axis=0,
        )

    def swap(rows):
        return lax.all_to_all(
            rows.reshape(peers, rows.shape[0] // peers, *rows.shape[1:]), plane, 0, 0, tiled=True
        ).reshape(rows.shape)

    def swap_all(values):
        return lax.all_to_all(values, everyone, 0, 0, tiled=True)

    def after(value, *others):
        return lax.optimization_barrier((value, others))[0]

    def exchange_plane(values, steps):
        parts = {}
        for step in steps:
            part = lax.dynamic_index_in_dim(values, lax.rem(here + step, peers), 0, keepdims=False)
            pairs = [(i, (i + step) % peers) for i in range(peers)]
            parts[step] = lax.ppermute(part, plane, pairs) if step else part
        return parts

    def joined(parts):
        order = lax.rem(here - jnp.arange(peers, dtype=jnp.int32) + peers, peers)
        return jnp.take(jnp.stack([parts[step] for step in range(peers)]), order, axis=0)

    early_steps, late_steps = range(peers // 2), range(peers // 2, peers)

    def exchange_columns(values):
        parts = [values[:, 0], *[shifted(values[:, s], -s) for s in range(1, columns)]]
        return jnp.stack([parts[0], *parts[:0:-1]], axis=1)

    to_ring = lax.rem(col - jnp.arange(columns, dtype=jnp.int32) + columns, columns)

    earlier = (
        lax.broadcasted_iota(jnp.int32, (tokens, tokens), 0)
        < lax.broadcasted_iota(jnp.int32, (tokens, tokens), 1)
    ).astype(bf16)
    all_experts = jnp.arange(experts, dtype=jnp.int32)
    plane_experts = jnp.arange(peers, dtype=jnp.int32) * columns + col

    def chosen_in(ids, named):
        return jnp.any(ids[None, :, :] == named[:, None, None], axis=1)

    def slots_of(ids, named):
        chosen = chosen_in(ids, named)
        rank = dot_nn(chosen.astype(bf16), earlier)
        code = jnp.where(chosen, rank, -1.0)
        place = lax.broadcasted_iota(jnp.int32, (1, capacity, 1), 1).astype(f32)
        return chosen, code[:, None, :] == place

    def slot_mat(ids):
        return slots_of(ids, plane_experts)[1].astype(bf16).reshape(peers * capacity, tokens)

    def pick(step, block):
        return product(slot_mats[step], block)

    def gates_of(chosen, block):
        logits = jnp.where(chosen, dot_general_t(router, block), -1e30)
        exponent = jnp.exp(logits - jnp.max(logits, axis=0, keepdims=True))
        exponent = jnp.where(chosen, exponent, 0.0)
        return exponent / jnp.sum(exponent, axis=0, keepdims=True)

    def weighted_mat(step, block_gates):
        gates_here = block_gates.reshape(peers, columns, 1, tokens)
        gates_here = lax.dynamic_index_in_dim(gates_here, col, 1, keepdims=False)
        mat = slot_mats[step].reshape(peers, capacity, tokens) * gates_here
        return mat.astype(bf16).reshape(peers * capacity, tokens)

    def collect(back, step, addend=None, out_type=bf16):
        return product(weighted_mats[step], back[step], addend, out_type, transposed=True)

    near_inputs = gather_near(inputs)
    local_qkv = jnp.concatenate([query_proj, key_projection, value_projection], axis=1)
    full_qkv = lax.all_gather(local_qkv, "exp", axis=0, tiled=True)
    full_out = lax.all_gather(out_proj, "exp", axis=0, tiled=True)
    own_ids = expert_ids.T
    slot_mats = [slot_mat(own_ids)]
    cotangent_rows = [swap(pick(0, cotangent)), None, None, None]
    near_inputs, full_qkv = after((near_inputs, full_qkv))

    far_inputs = jnp.concatenate(gather_far(*near_inputs), axis=0)
    def project(block):
        rows = block.astype(f32)
        unit = rows * inverse_rms(rows)
        low = (unit * attn_gain).astype(bf16)
        return unit, low, dot_nn(low, full_qkv)

    projected = [project(inputs), project(near_inputs[0]), None, project(near_inputs[1])]
    cosine, sine = rotary_tables(positions, head_size)
    far_inputs, cotangent_rows[0], cosine, sine = after(
        (far_inputs, cotangent_rows[0], cosine, sine),
        [projected[s][2] for s in (0, 1, 3)],
    )

    near_cotangent = gather_near(after(cotangent, far_inputs))
    later_ids = after(own_ids, far_inputs)
    ids_blocks = [own_ids, *[shifted(later_ids, step) for step in range(1, columns)]]
    projected[2] = project(far_inputs)
    units, normed, qkv = zip(*projected)
    query_gain, key_gain = query_norm_gain[None, :], key_norm_gain[None, :]
    *attended, levels = attention_forward(col_array, qkv, cosine, sine, query_gain, key_gain, heads)
    shares = spread(attended, full_out)
    ids_blocks = after(ids_blocks, attended)
    slot_mats += [slot_mat(ids_blocks[s]) for s in (1, 2, 3)]
    picked = pick(1, after(near_cotangent[0], attended))
    near_cotangent, shares, slot_mats, picked = after((near_cotangent, shares, slot_mats, picked))

    send_up, send_down, free_up, free_down, up_rest, down_rest, own_share = shares
    cotangent_rows[1] = swap(picked)
    first_up, first_down = up(send_up), down(send_down)
    far_up = up(near_cotangent[0][:middle])
    chosen_all, slots_all = slots_of(own_ids, all_experts)
    picked = pick(3, near_cotangent[1])
    late_half = near_cotangent[1][middle:]
    first_up, first_down, far_up, cotangent_rows[1], chosen_all, slots_all, picked, late_half, frees = after(
        (
            first_up, first_down, far_up, cotangent_rows[1], chosen_all, slots_all, picked, late_half,
            (free_up, free_down),
        )
    )
    cotangent_rows[3] = swap(picked)
    far_down = down(late_half)
    second_up = up(scatter_second(up_rest, first_up))
    second_down = down(scatter_second(down_rest, first_down))
    picked = pick(2, jnp.concatenate([far_up, far_down], axis=0))
    second_up, second_down, picked, cotangent_rows[3], frees = after(
        (second_up, second_down, picked, cotangent_rows[3], frees)
    )

    free_up, free_down = up(frees[0]), down(frees[1])
    cotangent_rows[2] = swap(picked)
    gate_weight, up_weight, down_weight = gate_proj[0], up_proj[0], down_proj[0]
    hidden = inputs.astype(f32) + scatter_own(own_share, second_up, second_down, free_up, free_down)
    inverse_hidden = inverse_rms(hidden)
    routed = (hidden * inverse_hidden * moe_gain).astype(bf16)
    own_rows = after(pick(0, routed), cotangent_rows[2])

    acted_rows, gate_grads, up_grads, row_grads, returned, gate_dots = [], [], [], [], [], []

    def run_expert(step, rows):
        results = expert_block(rows, cotangent_rows[step], gate_weight, up_weight, down_weight)
        for held, result in zip((acted_rows, gate_grads, up_grads, row_grads, returned), results):
            held.append(result)
        gate_dots.append(results[5].reshape(peers, capacity))

    def block_mat(step):
        block_gates = gates_of(chosen_in(ids_blocks[step], all_experts), routed_blocks[step])
        return weighted_mat(step, block_gates)

    routed_blocks, arrived, weighted_mats = [routed], [], {}
    rows, next_rows = own_rows, None
    slot_parts = {}
    for step in range(columns):
        rows = swap(rows)
        coming = None
        if step < columns - 1:
            coming = up(routed_blocks[step])
            next_rows = pick(step + 1, coming)
        if step:
            run_expert(step - 1, arrived[step - 1])
        if step == 0:
            gates = gates_of(chosen_all, routed)
            gate_slots = jnp.sum(jnp.where(slots_all, gates[:, None, :], 0.0), axis=2)
            gate_slots = jnp.take(gate_slots.reshape(peers, columns, capacity), to_ring, axis=1)
            weighted_mats[0] = weighted_mat(0, gates)
            slot_parts = exchange_plane(gate_slots, early_steps)
        elif step == 1:
            slot_parts.update(exchange_plane(gate_slots, late_steps))
        elif step == 2:
            gate_slots = exchange_columns(joined(slot_parts))
            slot_parts = {}
        state = (rows, next_rows, coming, gate_slots, weighted_mats, slot_parts)
        rows, next_rows, coming, gate_slots, weighted_mats, slot_parts = after(state, row_grads)
        arrived.append(rows)
        routed_blocks.append(coming)
        rows = next_rows
    row_weights = [gate_slots[:, step].reshape(peers * capacity, 1) for step in range(columns)]

    row_grads = after(row_grads, arrived[3])
    grad_back = {1: swap(row_grads[1])}
    run_expert(3, arrived[3])
    weighted_mats[1] = block_mat(1)
    grad_back[1], row_grads, gate_dots, weighted_mats = after(
        (grad_back[1], row_grads, gate_dots, weighted_mats)
    )
    grad_back[2] = swap(row_grads[2])
    running = up(collect(grad_back, 1))
    dots = jnp.stack(gate_dots, axis=1)
    dot_parts = exchange_plane(dots, early_steps)
    weighted_mats[2] = block_mat(2)
    running, grad_back[2], dot_parts, weighted_mats = after(
        (running, grad_back[2], dot_parts, weighted_mats)
    )
    grad_back[3] = swap(after(row_grads[3], running))
    running = up(collect(grad_back, 2, running))
    dot_parts.update(exchange_plane(after(dots, grad_back[2]), late_steps))
    weighted_mats[3] = block_mat(3)
    running, grad_back[3], dot_parts, weighted_mats = after(
        (running, grad_back[3], dot_parts, weighted_mats)
    )
    grad_back[0] = swap(after(row_grads[0], running))
    running = up(collect(grad_back, 3, running))
    dots = jnp.take(exchange_columns(joined(dot_parts)), to_ring, axis=1).reshape(experts, capacity)
    running, grad_back[0], dots = after((running, grad_back[0], dots))

    grad_gates = jnp.sum(jnp.where(slots_all, dots[:, :, None], 0.0), axis=1)
    grad_logits = (
        gates * (grad_gates - jnp.sum(gates * grad_gates, axis=0, keepdims=True))
    ).astype(bf16)
    grad_routed = collect(grad_back, 0, running, f32) + lax.dot_general(
        grad_logits, router, (((0,), (1,)), ((), ())), preferred_element_type=f32
    )
    scaled = grad_routed * moe_gain
    grad_hidden = (
        cotangent.astype(f32)
        + scaled * inverse_hidden
        - hidden * (jnp.mean(hidden * scaled, axis=-1, keepdims=True) * inverse_hidden**3)
    )
    grad_moe_gain = jnp.sum(grad_routed * hidden * inverse_hidden, axis=0)
    grad_router = dot_general_t(routed, grad_logits)

    grad_low = grad_hidden.astype(bf16)
    near_gradient = gather_near(grad_low)
    output_back = {1: swap(after(returned[1], grad_back[0]))}
    grad_attended = {0: product(grad_low, full_out)}
    grad_gate_weight, grad_up_weight = weight_gradients(
        after(arrived, grad_low), [gate_grads, up_grads], f32, row_weights
    )
    near_gradient, grad_gate_weight, grad_attended = after(
        (near_gradient, grad_gate_weight, grad_attended)
    )

    far_gradient = gather_far(*near_gradient)
    output_back[2] = swap(after(returned[2], output_back[1], grad_low))
    grad_attended.update({1: product(near_gradient[0], full_out), 3: product(near_gradient[1], full_out)})
    output_part = collect(output_back, 1)
    far_gradient = jnp.concatenate(after(far_gradient, output_part), axis=0)
    router_sums = grad_router.reshape(1, columns, width // columns * experts)
    router_sums = jnp.take(after(router_sums, near_gradient), to_ring, axis=1)
    router_sums = jnp.sum(exchange_columns(router_sums)[0], axis=0)
    far_gradient, grad_attended, output_part, router_sums = after(
        (far_gradient, grad_attended, output_part, router_sums)
    )

    grad_sequence = [grad_low, near_gradient[0], far_gradient, near_gradient[1]]
    running = up(output_part)
    output_back[3] = swap(after(returned[3], output_back[2]))
    grad_attended[2] = product(far_gradient, full_out)
    grad_attended = [grad_attended[s] for s in range(columns)]
    half = heads // 2
    arguments = (col_array, qkv, grad_attended, cosine, sine, query_gain, key_gain, levels)
    dp, exp = lax.axis_size("dp"), lax.axis_size("exp")
    tile = width // (dp * exp)

    def weight_parts(lefts, right):
        mine = lax.axis_index("exp")
        if tile % 128 == 0:
            return split_gradient(lefts, right, jnp.reshape(mine, (1,)).astype(jnp.int32), exp, dp)
        (grads,) = weight_gradients(lefts, [right], bf16)
        grads = grads.reshape(dp, exp, tile, -1).transpose(1, 0, 2, 3).reshape(exp, dp * tile, -1)
        return [
            lax.dynamic_index_in_dim(grads, lax.rem(mine + step, exp), 0, keepdims=False)
            for step in range(exp)
        ]

    def exchange_parts(parts):
        return [
            lax.ppermute(part, "exp", [(i, (i + step) % exp) for i in range(exp)]) if step else part
            for step, part in enumerate(parts)
        ]

    def sum_of(parts):
        return sum(part.astype(f32) for part in parts).astype(bf16)

    def swap_parts(sums):
        parts = sums.reshape(dp, -1, sums.shape[1])
        return lax.all_to_all(parts, "dp", 0, 0, tiled=True)

    out_parts = exchange_parts(weight_parts(grad_sequence, attended))
    first_half = attention_backward(*arguments, 0, half)
    first_half, running, out_parts = after((first_half, running, out_parts))
    out_sums = sum_of(out_parts)
    out_sums = swap_parts(after(out_sums, output_back[3]))
    output_part = collect(output_back, 2, running)
    running = up(output_part)
    *grad_qkv, grad_query_gain, grad_key_gain, _, _ = attention_backward(
        *arguments, half, heads - half, after(first_half, output_part)
    )
    grad_query_gain, grad_key_gain = grad_query_gain[0], grad_key_gain[0]

    grad_qkv, out_sums = after((grad_qkv, out_sums))
    *shares, attn_gain_sums = spread(grad_qkv, full_qkv, units)
    send_up, send_down, free_up, free_down, up_rest, down_rest, own_share = shares
    first_up, first_down = up(send_up), down(send_down)
    output_part = collect(after(output_back, attn_gain_sums), 3, running)
    (grad_down,) = weight_gradients(
        after(acted_rows, attn_gain_sums), [cotangent_rows], f32, row_weights
    )
    output_back[0] = swap(after(returned[0], out_sums))
    free_up, free_down = up(free_up), down(free_down)
    qkv_parts = weight_parts(normed, after(grad_qkv, attn_gain_sums))
    first_up, first_down, free_up, free_down, grad_down, output_part, qkv_parts = after(
        (first_up, first_down, free_up, free_down, grad_down, output_part, qkv_parts)
    )

    second_up = up(scatter_second(up_rest, first_up))
    second_down = down(scatter_second(down_rest, first_down))
    running = up(output_part)
    reduced_out = jnp.sum(out_sums.astype(f32), axis=0)
    qkv_sums = sum_of(exchange_parts(qkv_parts))

    qkv_parts = swap_parts(after(qkv_sums, output_back[0]))
    small = jnp.concatenate([attn_gain_sums[0], grad_query_gain, grad_key_gain, grad_moe_gain])
    cuts = [0, width, width + head_size, width + 2 * head_size, 2 * (width + head_size)]
    small = jnp.concatenate([small, router_sums])
    small = swap(after(jnp.broadcast_to(small, (peers, small.shape[0])), qkv_parts))
    reduced_qkv = jnp.sum(qkv_parts.astype(f32), axis=0)
    outputs = (hidden + collect(output_back, 0, running, f32)).astype(bf16)
    small = jnp.sum(small, axis=0)
    small = jnp.stack([small, *[shifted(small, step) for step in range(1, columns)]])
    to_true = lax.rem(col - jnp.arange(columns, dtype=jnp.int32) + columns, columns)
    grad_router = jnp.take(small[:, cuts[-1] :], to_true, axis=0).reshape(width, experts)
    small = jnp.sum(small[:, : cuts[-1]], axis=0)
    shared = [small[i:j] for i, j in zip(cuts, cuts[1:])]

    grad_normed = scatter_own(own_share, second_up, second_down, free_up, free_down)
    input_rows = inputs.astype(f32)
    inverse_own = inverse_rms(input_rows)
    scaled_in = grad_normed * attn_gain
    grad_inputs = (
        grad_hidden
        + scaled_in * inverse_own
        - input_rows * (jnp.mean(input_rows * scaled_in, axis=-1, keepdims=True) * inverse_own**3)
    ).astype(bf16)

    split = heads * head_size
    return (
        outputs,
        grad_inputs,
        shared[0],
        reduced_qkv[:, :split],
        reduced_qkv[:, split : split + head_size],
        reduced_qkv[:, split + head_size :],
        shared[1],
        shared[2],
        reduced_out,
        shared[3],
        grad_router,
        grad_gate_weight[None],
        grad_up_weight[None],
        grad_down[None],
    )


def dot_general_t(a, b):
    contract = (((0,), (1,)), ((), ()))
    return lax.dot_general(a, b, contract, preferred_element_type=f32)


def solution(mesh):
    return jax.shard_map(
        local,
        mesh=mesh,
        in_specs=(
            P(("dp", "exp", "col"), None),
            P(("dp", "exp", "col"), None),
            P(("dp", "exp")),
            P(("dp", "exp", "col"), None),
            P(),
            P("exp", "col"),
            P("exp", "col"),
            P("exp", "col"),
            P(),
            P(),
            P("exp", "col"),
            P(),
            P(),
            P(("dp", "exp", "col"), None, None),
            P(("dp", "exp", "col"), None, None),
            P(("dp", "exp", "col"), None, None),
        ),
        out_specs=(
            P(("dp", "exp", "col"), None),
            P(("dp", "exp", "col"), None),
            P(),
            P(("dp", "exp"), "col"),
            P(("dp", "exp"), "col"),
            P(("dp", "exp"), "col"),
            P(),
            P(),
            P(("dp", "exp"), "col"),
            P(),
            P(),
            P(("dp", "exp", "col"), None, None),
            P(("dp", "exp", "col"), None, None),
            P(("dp", "exp", "col"), None, None),
        ),
        check_vma=False,
    )
```

```python
import functools
import math

import jax
import jax.numpy as jnp
from jax import lax
from jax.experimental import pallas as pl
from jax.experimental.pallas import tpu as pltpu
from jax.sharding import PartitionSpec as P

epsilon = 1e-06
rotary_base = 1000000.0
plane = ("dp", "exp")
everyone = ("dp", "exp", "col")
f32 = jnp.float32
bf16 = jnp.bfloat16


def dot_nn(a, b):
    return lax.dot_general(a, b, (((1,), (0,)), ((), ())), preferred_element_type=f32)


def dot_nt(a, b):
    return lax.dot_general(a, b, (((1,), (1,)), ((), ())), preferred_element_type=f32)


def dot_tn(a, b):
    return lax.dot_general(a, b, (((0,), (0,)), ((), ())), preferred_element_type=f32)


def inverse_rms(rows):
    return lax.rsqrt(jnp.mean(rows * rows, axis=-1, keepdims=True) + epsilon)


def rotary_tables(positions, head_size):
    halves = head_size // 2
    frequency = rotary_base ** (-2.0 * jnp.arange(halves, dtype=f32) / head_size)
    angles = positions.astype(f32)[:, None] * frequency[None, :]
    cosine, sine = jnp.cos(angles), jnp.sin(angles)
    return (
        jnp.concatenate([cosine, cosine], axis=1),
        jnp.concatenate([-sine, sine], axis=1),
    )


def turn(rows, cosine, sine):
    return rows * cosine + pltpu.roll(rows, rows.shape[-1] // 2, 1) * sine


def turn_back(rows, cosine, sine):
    return rows * cosine - pltpu.roll(rows, rows.shape[-1] // 2, 1) * sine


def place_of(col_ref, blocks, tokens, step):
    return pl.multiple_of(lax.rem(col_ref[0] - step + blocks, blocks) * tokens, tokens)


def in_order(col_ref, refs, held):
    tokens = refs[0].shape[0]
    for step, ref in enumerate(refs):
        held[pl.ds(place_of(col_ref, len(refs), tokens, step), tokens), :] = ref[...].astype(held.dtype)


def out_of_order(col_ref, held, refs):
    tokens = refs[0].shape[0]
    for step, ref in enumerate(refs):
        ref[...] = held[pl.ds(place_of(col_ref, len(refs), tokens, step), tokens), :].astype(ref.dtype)


def scores_of(keys, query, first, scale):
    count = query.shape[0]
    scores = dot_nt(keys[pl.ds(0, first + count), :], query) * (scale * math.log2(math.e))
    row = lax.broadcasted_iota(jnp.int32, (count, count), 0)
    column = lax.broadcasted_iota(jnp.int32, (count, count), 1)
    last = jnp.where(row <= column, scores[first:], -1e30)
    return jnp.concatenate([scores[:first], last], axis=0) if first else last


def prepare_keys(col_ref, k_refs, v_refs, cos_ref, sin_ref, kg_ref, raw_rows, keys, values):
    in_order(col_ref, k_refs, raw_rows)
    in_order(col_ref, v_refs, values)
    tokens = k_refs[0].shape[0]
    for block in range(len(k_refs)):
        there = pl.ds(block * tokens, tokens)
        raw = raw_rows[there, :]
        rows = raw * inverse_rms(raw) * kg_ref[...]
        keys[there, :] = turn(rows, cos_ref[there, :], sin_ref[there, :]).astype(bf16)


def forward_kernel(blocks, scale, col_ref, *refs):
    q_refs, k_refs, v_refs = refs[:blocks], refs[blocks : 2 * blocks], refs[2 * blocks : 3 * blocks]
    cos_ref, sin_ref, qg_ref, kg_ref = refs[3 * blocks : 3 * blocks + 4]
    out_refs = refs[3 * blocks + 4 : 4 * blocks + 4]
    level_ref, raw_rows, keys, values, mixed_rows = refs[4 * blocks + 4 :]
    tokens = q_refs[0].shape[0]

    @pl.when(pl.program_id(0) == 0)
    def _():
        prepare_keys(col_ref, k_refs, v_refs, cos_ref, sin_ref, kg_ref, raw_rows, keys, values)

    in_order(col_ref, q_refs, raw_rows)
    for block in range(blocks):
        first = block * tokens
        there = pl.ds(first, tokens)
        raw = raw_rows[there, :]
        rows = raw * inverse_rms(raw) * qg_ref[...]
        query = turn(rows, cos_ref[there, :], sin_ref[there, :]).astype(bf16)
        scores = scores_of(keys, query, first, scale)
        peak = jnp.max(scores, axis=0, keepdims=True)
        probs = jnp.exp2(scores - peak)
        total = jnp.sum(probs, axis=0, keepdims=True)
        level_ref[0, :, there] = peak + jnp.log2(total)
        probs = (probs * (1.0 / total)).astype(bf16)
        mixed_rows[there, :] = dot_tn(probs, values[pl.ds(0, first + tokens), :]).astype(bf16)
    out_of_order(col_ref, mixed_rows, out_refs)


def attention_forward(col, qkv, cosine, sine, query_gain, key_gain, heads):
    blocks, tokens, head_size = len(qkv), qkv[0].shape[0], query_gain.shape[-1]
    seq_len = blocks * tokens
    column = lambda index: [pl.BlockSpec((tokens, head_size), index)] * blocks
    whole = pl.BlockSpec((seq_len, head_size), lambda h, c: (0, 0))
    gain = pl.BlockSpec((1, head_size), lambda h, c: (0, 0))
    return pl.pallas_call(
        functools.partial(forward_kernel, blocks, head_size ** (-0.5)),
        out_shape=[
            *[jax.ShapeDtypeStruct((tokens, heads * head_size), bf16)] * blocks,
            jax.ShapeDtypeStruct((heads, 1, seq_len), f32),
        ],
        grid_spec=pltpu.PrefetchScalarGridSpec(
            num_scalar_prefetch=1,
            grid=(heads,),
            in_specs=[
                *column(lambda h, c: (0, h)),
                *column(lambda h, c: (0, heads)),
                *column(lambda h, c: (0, heads + 1)),
                whole,
                whole,
                gain,
                gain,
            ],
            out_specs=[
                *column(lambda h, c: (0, h)),
                pl.BlockSpec((1, 1, seq_len), lambda h, c: (h, 0, 0)),
            ],
            scratch_shapes=[
                pltpu.VMEM((seq_len, head_size), f32),
                pltpu.VMEM((seq_len, head_size), bf16),
                pltpu.VMEM((seq_len, head_size), bf16),
                pltpu.VMEM((seq_len, head_size), bf16),
            ],
        ),
        compiler_params=pltpu.CompilerParams(vmem_limit_bytes=60 * 2**20),
        cost_estimate=pl.CostEstimate(flops=1000, bytes_accessed=1000, transcendentals=0),
        name="attention_forward",
    )(col, *qkv, *qkv, *qkv, cosine, sine, query_gain, key_gain)


def backward_kernel(blocks, scale, first_head, heads, final, col_ref, *refs):
    q_refs, k_refs, v_refs, g_refs = (refs[i * blocks : (i + 1) * blocks] for i in range(4))
    cos_ref, sin_ref, qg_ref, kg_ref, level_ref = refs[4 * blocks : 4 * blocks + 5]
    refs = refs[4 * blocks + 5 :]
    if first_head:
        refs = refs[blocks:]
        held_refs, refs = refs[:4], refs[4:]
    grad_refs, refs = refs[:blocks], refs[blocks:]
    qgain_ref, kgain_ref, out_keys, out_values = refs[:4]
    raw_rows, mixed_rows, keys, values, grad_rows, grad_keys, grad_values = refs[4:]
    tokens = q_refs[0].shape[0]
    step = pl.program_id(0)

    @pl.when(step == 0)
    def _():
        prepare_keys(col_ref, k_refs, v_refs, cos_ref, sin_ref, kg_ref, raw_rows, keys, values)
        if first_head:
            qgain_ref[...] = held_refs[0][...]
            kgain_ref[...] = held_refs[1][...]
            grad_keys[...] = held_refs[2][...]
            grad_values[...] = held_refs[3][...]
        else:
            grad_keys[...] = jnp.zeros_like(grad_keys)
            grad_values[...] = jnp.zeros_like(grad_values)
            qgain_ref[...] = jnp.zeros_like(qgain_ref)
            kgain_ref[...] = jnp.zeros_like(kgain_ref)

    def through_norm(grad_rot, unit, inverse, there, gain_ref, gain_grad_ref):
        grad_scaled = turn_back(grad_rot, cos_ref[there, :], sin_ref[there, :])
        gain_grad_ref[0:1, :] += jnp.sum(grad_scaled * unit, axis=0, keepdims=True)
        grad_unit = grad_scaled * gain_ref[...]
        return inverse * (grad_unit - unit * jnp.mean(grad_unit * unit, axis=1, keepdims=True))

    @pl.when(step < heads)
    def _():
        in_order(col_ref, q_refs, raw_rows)
        in_order(col_ref, g_refs, mixed_rows)
        for block in range(blocks):
            first = block * tokens
            there = pl.ds(first, tokens)
            raw = raw_rows[there, :]
            inverse = inverse_rms(raw)
            unit = raw * inverse
            query = turn(unit * qg_ref[...], cos_ref[there, :], sin_ref[there, :]).astype(bf16)
            grad_mixed = mixed_rows[there, :]
            upto = pl.ds(0, first + tokens)
            probs = jnp.exp2(scores_of(keys, query, first, scale) - level_ref[0, :, there])
            grad_probs = dot_nt(values[upto, :], grad_mixed)
            inner = jnp.sum(probs * grad_probs, axis=0, keepdims=True)
            grad_scores = (probs * (grad_probs - inner)).astype(bf16)
            grad_values[upto, :] += dot_nn(probs.astype(bf16), grad_mixed)
            grad_keys[upto, :] += dot_nn(grad_scores, query)
            grad_query = dot_tn(grad_scores, keys[upto, :])
            grad_rows[there, :] = through_norm(
                grad_query * scale, unit, inverse, there, qg_ref, qgain_ref
            ).astype(bf16)

    if not final:

        @pl.when(step == heads - 1)
        def _():
            out_keys[...] = grad_keys[...]
            out_values[...] = grad_values[...]

    @pl.when(step == heads)
    def _():
        in_order(col_ref, k_refs, raw_rows)
        for block in range(blocks):
            there = pl.ds(block * tokens, tokens)
            raw = raw_rows[there, :]
            inverse = inverse_rms(raw)
            grad_rows[there, :] = through_norm(
                grad_keys[there, :] * scale, raw * inverse, inverse, there, kg_ref, kgain_ref
            ).astype(bf16)

    @pl.when(step == heads + 1)
    def _():
        grad_rows[...] = grad_values[...].astype(bf16)

    out_of_order(col_ref, grad_rows, grad_refs)


def attention_backward(
    col, qkv, grad_attended, cosine, sine, query_gain, key_gain, levels, first, heads, former=None
):
    blocks, tokens, head_size = len(qkv), qkv[0].shape[0], query_gain.shape[-1]
    seq_len = blocks * tokens
    all_heads = levels.shape[0]
    final = first + heads == all_heads
    column = lambda index: [pl.BlockSpec((tokens, head_size), index)] * blocks
    whole = pl.BlockSpec((seq_len, head_size), lambda h, c: (0, 0))
    gain = pl.BlockSpec((1, head_size), lambda h, c: (0, 0))
    gain_out = pl.BlockSpec((8, head_size), lambda h, c: (0, 0))
    last = all_heads - 1
    held = [] if former is None else former
    return pl.pallas_call(
        functools.partial(backward_kernel, blocks, head_size ** (-0.5), first, heads, final),
        out_shape=[
            *[jax.ShapeDtypeStruct(qkv[0].shape, bf16)] * blocks,
            jax.ShapeDtypeStruct((8, head_size), f32),
            jax.ShapeDtypeStruct((8, head_size), f32),
            jax.ShapeDtypeStruct((seq_len, head_size), f32),
            jax.ShapeDtypeStruct((seq_len, head_size), f32),
        ],
        grid_spec=pltpu.PrefetchScalarGridSpec(
            num_scalar_prefetch=1,
            grid=(heads + 2 if final else heads,),
            in_specs=[
                *column(lambda h, c: (0, jnp.minimum(h + first, last))),
                *column(lambda h, c: (0, all_heads)),
                *column(lambda h, c: (0, all_heads + 1)),
                *column(lambda h, c: (0, jnp.minimum(h + first, last))),
                whole,
                whole,
                gain,
                gain,
                pl.BlockSpec((1, 1, seq_len), lambda h, c: (jnp.minimum(h + first, last), 0, 0)),
                *([] if former is None else [pl.BlockSpec(memory_space=pl.ANY)] * blocks),
                *([] if former is None else [gain_out, gain_out, whole, whole]),
            ],
            out_specs=[*column(lambda h, c: (0, h + first)), gain_out, gain_out, whole, whole],
            scratch_shapes=[
                pltpu.VMEM((seq_len, head_size), f32),
                pltpu.VMEM((seq_len, head_size), bf16),
                pltpu.VMEM((seq_len, head_size), bf16),
                pltpu.VMEM((seq_len, head_size), bf16),
                pltpu.VMEM((seq_len, head_size), bf16),
                pltpu.VMEM((seq_len, head_size), f32),
                pltpu.VMEM((seq_len, head_size), f32),
            ],
        ),
        input_output_aliases={} if former is None else {1 + 4 * blocks + 5 + i: i for i in range(blocks)},
        compiler_params=pltpu.CompilerParams(vmem_limit_bytes=60 * 2**20),
        cost_estimate=pl.CostEstimate(flops=1000, bytes_accessed=1000, transcendentals=0),
        name="attention_backward",
    )(col, *qkv, *qkv, *qkv, *grad_attended, cosine, sine, query_gain, key_gain, levels, *held)


def weight_kernel(blocks, rights, weighted, *refs):
    left_refs, refs = refs[:blocks], refs[blocks:]
    right_refs, refs = refs[: blocks * rights], refs[blocks * rights :]
    if weighted:
        weight_refs, refs = refs[:blocks], refs[blocks:]
        out_refs, held = refs[:rights], refs[rights:]

        @pl.when(pl.program_id(0) == 0)
        def _():
            for index, ref in enumerate(right_refs):
                scaled = ref[...].astype(f32) * weight_refs[index % blocks][...]
                held[index][...] = scaled.astype(bf16)

        right_refs = held
    else:
        out_refs = refs
    for index, out_ref in enumerate(out_refs):
        total = dot_tn(left_refs[0][...], right_refs[index * blocks][...])
        for block in range(1, blocks):
            total = total + dot_tn(left_refs[block][...], right_refs[index * blocks + block][...])
        out_ref[...] = total.astype(out_ref.dtype)


def weight_gradients(lefts, rights, out_type, weights=None, tile=256):
    blocks, rows, tall = len(lefts), lefts[0].shape[0], lefts[0].shape[1]
    flat = [block for right in rights for block in right]
    fixed = lambda array: pl.BlockSpec(array.shape, lambda i: (0, 0))
    return pl.pallas_call(
        functools.partial(weight_kernel, blocks, len(rights), weights is not None),
        out_shape=[jax.ShapeDtypeStruct((tall, right[0].shape[1]), out_type) for right in rights],
        grid=(tall // tile,),
        in_specs=[
            *[pl.BlockSpec((rows, tile), lambda i: (0, i))] * blocks,
            *[fixed(block) for block in flat],
            *([] if weights is None else [fixed(weight) for weight in weights]),
        ],
        out_specs=[
            pl.BlockSpec((tile, right[0].shape[1]), lambda i: (i, 0)) for right in rights
        ],
        scratch_shapes=[] if weights is None else [pltpu.VMEM(block.shape, bf16) for block in flat],
        compiler_params=pltpu.CompilerParams(vmem_limit_bytes=60 * 2**20),
        cost_estimate=pl.CostEstimate(flops=1000, bytes_accessed=1000, transcendentals=0),
        name="weight_gradients",
    )(*lefts, *flat, *([] if weights is None else weights))


def split_kernel(blocks, groups, mine_ref, *refs):
    left_refs, right_refs, out_refs = refs[:blocks], refs[blocks : 2 * blocks], refs[2 * blocks :]
    total = dot_tn(left_refs[0][...], right_refs[0][...])
    for block in range(1, blocks):
        total = total + dot_tn(left_refs[block][...], right_refs[block][...])
    for index, out_ref in enumerate(out_refs):

        @pl.when(pl.program_id(0) // groups == index)
        def _():
            out_ref[...] = total.astype(out_ref.dtype)


def split_gradient(lefts, right, mine, devices, groups):
    blocks, rows, tall = len(lefts), lefts[0].shape[0], lefts[0].shape[1]
    tile, wide = tall // (devices * groups), right[0].shape[1]

    def left_tile(i, mine_ref):
        return (0, i % groups * devices + lax.rem(mine_ref[0] + i // groups, devices))

    def out_tile(index):
        return lambda i, mine_ref: (jnp.clip(i - index * groups, 0, groups - 1), 0)

    return pl.pallas_call(
        functools.partial(split_kernel, blocks, groups),
        out_shape=[jax.ShapeDtypeStruct((groups * tile, wide), bf16)] * devices,
        grid_spec=pltpu.PrefetchScalarGridSpec(
            num_scalar_prefetch=1,
            grid=(devices * groups,),
            in_specs=[
                *[pl.BlockSpec((rows, tile), left_tile)] * blocks,
                *[pl.BlockSpec((rows, wide), lambda i, mine_ref: (0, 0))] * blocks,
            ],
            out_specs=[pl.BlockSpec((tile, wide), out_tile(index)) for index in range(devices)],
        ),
        compiler_params=pltpu.CompilerParams(vmem_limit_bytes=60 * 2**20),
        cost_estimate=pl.CostEstimate(flops=1000, bytes_accessed=1000, transcendentals=0),
        name="split_gradient",
    )(mine, *lefts, *right)


def spread_kernel(with_units, *refs):
    block_refs, weight_ref, refs = refs[:4], refs[4], refs[5:]
    if with_units:
        unit_refs, refs = refs[:4], refs[4:]
    far_up, far_down, free_up, free_down, up_rest, down_rest, own_ref = refs[:7]
    weight = weight_ref[...]
    middle = own_ref.shape[0] // 2
    shares = {}
    for step in (2, 3, 1, 0):
        shares[step] = dot_nt(block_refs[step][...], weight)
    far_up[...] = shares[2][:middle].astype(bf16)
    far_down[...] = shares[2][middle:].astype(bf16)
    free_up[...] = shares[3][middle:].astype(bf16)
    free_down[...] = shares[1][:middle].astype(bf16)
    up_rest[...] = shares[3][:middle]
    down_rest[...] = shares[1][middle:]
    own_ref[...] = shares[0]
    if with_units:
        total = sum(
            jnp.sum(shares[step] * unit_refs[step][...], axis=0, keepdims=True) for step in range(4)
        )
        refs[7][...] = jnp.broadcast_to(total, refs[7].shape)


def spread(blocks, weight, units=None, tile=512):
    tokens, depth = blocks[0].shape
    width = weight.shape[0]
    part = lambda rows: pl.BlockSpec((rows, tile), lambda i: (0, i))
    shape = jax.ShapeDtypeStruct
    return pl.pallas_call(
        functools.partial(spread_kernel, units is not None),
        out_shape=[
            *[shape((tokens // 2, width), bf16)] * 4,
            *[shape((tokens // 2, width), f32)] * 2,
            shape((tokens, width), f32),
            *([] if units is None else [shape((8, width), f32)]),
        ],
        grid=(width // tile,),
        in_specs=[
            *[pl.BlockSpec((tokens, depth), lambda i: (0, 0))] * 4,
            pl.BlockSpec((tile, depth), lambda i: (i, 0)),
            *([] if units is None else [part(tokens)] * 4),
        ],
        out_specs=[
            *[part(tokens // 2)] * 6,
            part(tokens),
            *([] if units is None else [part(8)]),
        ],
        compiler_params=pltpu.CompilerParams(vmem_limit_bytes=60 * 2**20),
        cost_estimate=pl.CostEstimate(flops=1000, bytes_accessed=1000, transcendentals=0),
        name="spread",
    )(*blocks, weight, *([] if units is None else units))


def product_kernel(transposed, left_ref, right_ref, *refs):
    result = (dot_tn if transposed else dot_nn)(left_ref[...], right_ref[...])
    if len(refs) > 1:
        result = result + refs[0][...].astype(f32)
    refs[-1][...] = result.astype(refs[-1].dtype)


def product(left, right, addend=None, out_type=bf16, transposed=False, tile=512):
    rows = left.shape[1 if transposed else 0]
    part = lambda height: pl.BlockSpec((height, tile), lambda i: (0, i))
    return pl.pallas_call(
        functools.partial(product_kernel, transposed),
        out_shape=jax.ShapeDtypeStruct((rows, right.shape[1]), out_type),
        grid=(right.shape[1] // tile,),
        in_specs=[
            pl.BlockSpec(left.shape, lambda i: (0, 0)),
            part(right.shape[0]),
            *([] if addend is None else [part(rows)]),
        ],
        out_specs=part(rows),
        compiler_params=pltpu.CompilerParams(vmem_limit_bytes=60 * 2**20),
        cost_estimate=pl.CostEstimate(flops=1000, bytes_accessed=1000, transcendentals=0),
        name="product",
    )(left, right, *([] if addend is None else [addend]))


def expert_kernel(
    rows_ref, upstream_ref, gate_ref, up_ref, down_ref,
    acted_ref, gate_grad_ref, up_grad_ref, row_grad_ref, returned_ref, dots_ref,
    gates, ups, downs, gate_grads, up_grads, acted_rows,
):
    step = pl.program_id(0)
    tile = gate_ref.shape[1]
    gate_part = dot_nn(rows_ref[...], gate_ref[...])
    up_part = dot_nn(rows_ref[...], up_ref[...])
    drive = dot_nt(upstream_ref[...], down_ref[...])
    sigmoid = jax.nn.sigmoid(gate_part)
    silu = gate_part * sigmoid
    acted = silu * up_part
    acted_low = acted.astype(bf16)
    gate_grad = (drive * up_part * sigmoid * (1.0 + gate_part * (1.0 - sigmoid))).astype(bf16)
    up_grad = (drive * silu).astype(bf16)
    acted_ref[...] = acted_low
    gate_grad_ref[...] = gate_grad
    up_grad_ref[...] = up_grad
    dots = jnp.sum(acted * drive, axis=1, keepdims=True)
    for index in range(gates.shape[1] // tile):

        @pl.when(step == index)
        def _():
            here = pl.ds(index * tile, tile)
            gates[:, here] = gate_ref[...]
            ups[:, here] = up_ref[...]
            downs[here, :] = down_ref[...]
            gate_grads[:, here] = gate_grad
            up_grads[:, here] = up_grad
            acted_rows[:, here] = acted_low

    @pl.when(step == 0)
    def _():
        dots_ref[...] = dots

    @pl.when(step > 0)
    def _():
        dots_ref[...] += dots

    @pl.when(step == pl.num_programs(0) - 1)
    def _():
        for first in range(0, row_grad_ref.shape[1], 512):
            here = pl.ds(first, 512)
            row_grad_ref[:, here] = (
                dot_nt(gate_grads[...], gates[here, :]) + dot_nt(up_grads[...], ups[here, :])
            ).astype(bf16)
            returned_ref[:, here] = dot_nn(acted_rows[...], downs[:, here]).astype(bf16)


def expert_block(rows, upstream_rows, gate_weight, up_weight, down_weight, tile=256):
    count, width = rows.shape
    hidden = gate_weight.shape[1]
    shape = jax.ShapeDtypeStruct
    whole = pl.BlockSpec((count, width), lambda j: (0, 0))
    part = pl.BlockSpec((count, tile), lambda j: (0, j))
    return pl.pallas_call(
        expert_kernel,
        out_shape=[
            shape((count, hidden), bf16),
            shape((count, hidden), bf16),
            shape((count, hidden), bf16),
            shape((count, width), bf16),
            shape((count, width), bf16),
            shape((count, 1), f32),
        ],
        grid=(hidden // tile,),
        in_specs=[
            whole,
            whole,
            pl.BlockSpec((width, tile), lambda j: (0, j)),
            pl.BlockSpec((width, tile), lambda j: (0, j)),
            pl.BlockSpec((tile, width), lambda j: (j, 0)),
        ],
        out_specs=[part, part, part, whole, whole, pl.BlockSpec((count, 1), lambda j: (0, 0))],
        scratch_shapes=[
            pltpu.VMEM((width, hidden), bf16),
            pltpu.VMEM((width, hidden), bf16),
            pltpu.VMEM((hidden, width), bf16),
            pltpu.VMEM((count, hidden), bf16),
            pltpu.VMEM((count, hidden), bf16),
            pltpu.VMEM((count, hidden), bf16),
        ],
        compiler_params=pltpu.CompilerParams(vmem_limit_bytes=60 * 2**20),
        cost_estimate=pl.CostEstimate(flops=1000, bytes_accessed=1000, transcendentals=0),
        name="expert_block",
    )(rows, upstream_rows, gate_weight, up_weight, down_weight)


def local(
    inputs,
    expert_ids,
    positions,
    cotangent,
    attn_gain,
    query_proj,
    key_projection,
    value_projection,
    query_norm_gain,
    key_norm_gain,
    out_proj,
    moe_gain,
    router,
    gate_proj,
    up_proj,
    down_proj,
):
    tokens, width = inputs.shape
    head_size = query_norm_gain.shape[0]
    choices = expert_ids.shape[1]
    experts = router.shape[1]
    capacity = tokens * choices * 5 // (4 * experts)
    columns = lax.axis_size("col")
    peers = lax.axis_size("dp") * lax.axis_size("exp")
    col = lax.axis_index("col")
    here = lax.axis_index("dp") * lax.axis_size("exp") + lax.axis_index("exp")
    col_array = jnp.reshape(col, (1,)).astype(jnp.int32)
    heads = query_proj.shape[1] // head_size
    assert key_projection.shape[1] == head_size and experts == peers * columns
    assert columns == 4 and tokens % 32 == 0
    middle = tokens // 2

    def shifted(block, by):
        return lax.ppermute(block, "col", [(i, (i + by) % columns) for i in range(columns)])

    def up(block):
        return shifted(block, 1)

    def down(block):
        return shifted(block, -1)

    def gather_near(block):
        return up(block), down(block)

    def gather_far(former, latter):
        return up(former[:middle]), down(latter[middle:])

    def scatter_second(rest, far):
        return (rest + far.astype(f32)).astype(bf16)

    def scatter_own(own, second_up, second_down, free_up, free_down):
        return own + jnp.concatenate(
            [
                second_up.astype(f32) + free_down.astype(f32),
                free_up.astype(f32) + second_down.astype(f32),
            ],
            axis=0,
        )

    def swap(rows):
        return lax.all_to_all(
            rows.reshape(peers, rows.shape[0] // peers, *rows.shape[1:]), plane, 0, 0, tiled=True
        ).reshape(rows.shape)

    def swap_all(values):
        return lax.all_to_all(values, everyone, 0, 0, tiled=True)

    def after(value, *others):
        return lax.optimization_barrier((value, others))[0]

    def exchange_plane(values, steps):
        parts = {}
        for step in steps:
            part = lax.dynamic_index_in_dim(values, lax.rem(here + step, peers), 0, keepdims=False)
            pairs = [(i, (i + step) % peers) for i in range(peers)]
            parts[step] = lax.ppermute(part, plane, pairs) if step else part
        return parts

    def joined(parts):
        order = lax.rem(here - jnp.arange(peers, dtype=jnp.int32) + peers, peers)
        return jnp.take(jnp.stack([parts[step] for step in range(peers)]), order, axis=0)

    early_steps, late_steps = range(peers // 2), range(peers // 2, peers)

    def exchange_columns(values):
        parts = [values[:, 0], *[shifted(values[:, s], -s) for s in range(1, columns)]]
        return jnp.stack([parts[0], *parts[:0:-1]], axis=1)

    to_ring = lax.rem(col - jnp.arange(columns, dtype=jnp.int32) + columns, columns)

    earlier = (
        lax.broadcasted_iota(jnp.int32, (tokens, tokens), 0)
        < lax.broadcasted_iota(jnp.int32, (tokens, tokens), 1)
    ).astype(bf16)
    all_experts = jnp.arange(experts, dtype=jnp.int32)
    plane_experts = jnp.arange(peers, dtype=jnp.int32) * columns + col

    def chosen_in(ids, named):
        return jnp.any(ids[None, :, :] == named[:, None, None], axis=1)

    def slots_of(ids, named):
        chosen = chosen_in(ids, named)
        rank = dot_nn(chosen.astype(bf16), earlier)
        code = jnp.where(chosen, rank, -1.0)
        place = lax.broadcasted_iota(jnp.int32, (1, capacity, 1), 1).astype(f32)
        return chosen, code[:, None, :] == place

    def slot_mat(ids):
        return slots_of(ids, plane_experts)[1].astype(bf16).reshape(peers * capacity, tokens)

    def pick(step, block):
        return product(slot_mats[step], block)

    def gates_of(chosen, block):
        logits = jnp.where(chosen, dot_general_t(router, block), -1e30)
        exponent = jnp.exp(logits - jnp.max(logits, axis=0, keepdims=True))
        exponent = jnp.where(chosen, exponent, 0.0)
        return exponent / jnp.sum(exponent, axis=0, keepdims=True)

    def weighted_mat(step, block_gates):
        gates_here = block_gates.reshape(peers, columns, 1, tokens)
        gates_here = lax.dynamic_index_in_dim(gates_here, col, 1, keepdims=False)
        mat = slot_mats[step].reshape(peers, capacity, tokens) * gates_here
        return mat.astype(bf16).reshape(peers * capacity, tokens)

    def collect(back, step, addend=None, out_type=bf16):
        return product(weighted_mats[step], back[step], addend, out_type, transposed=True)

    near_inputs = gather_near(inputs)
    local_qkv = jnp.concatenate([query_proj, key_projection, value_projection], axis=1)
    full_qkv = lax.all_gather(local_qkv, "exp", axis=0, tiled=True)
    full_out = lax.all_gather(out_proj, "exp", axis=0, tiled=True)
    own_ids = expert_ids.T
    slot_mats = [slot_mat(own_ids)]
    cotangent_rows = [swap(pick(0, cotangent)), None, None, None]
    near_inputs, full_qkv = after((near_inputs, full_qkv))

    far_inputs = jnp.concatenate(gather_far(*near_inputs), axis=0)
    def project(block):
        rows = block.astype(f32)
        unit = rows * inverse_rms(rows)
        low = (unit * attn_gain).astype(bf16)
        return unit, low, dot_nn(low, full_qkv)

    projected = [project(inputs), project(near_inputs[0]), None, project(near_inputs[1])]
    cosine, sine = rotary_tables(positions, head_size)
    far_inputs, cotangent_rows[0], cosine, sine = after(
        (far_inputs, cotangent_rows[0], cosine, sine),
        [projected[s][2] for s in (0, 1, 3)],
    )

    near_cotangent = gather_near(after(cotangent, far_inputs))
    later_ids = after(own_ids, far_inputs)
    ids_blocks = [own_ids, *[shifted(later_ids, step) for step in range(1, columns)]]
    projected[2] = project(far_inputs)
    units, normed, qkv = zip(*projected)
    query_gain, key_gain = query_norm_gain[None, :], key_norm_gain[None, :]
    *attended, levels = attention_forward(col_array, qkv, cosine, sine, query_gain, key_gain, heads)
    shares = spread(attended, full_out)
    ids_blocks = after(ids_blocks, attended)
    slot_mats += [slot_mat(ids_blocks[s]) for s in (1, 2, 3)]
    first_rows = after(near_cotangent[0], attended)
    picked = pick(1, first_rows)
    late_cotangent, slot_mats = after((near_cotangent[1], slot_mats), shares)

    send_up, send_down, free_up, free_down, up_rest, down_rest, own_share = shares
    cotangent_rows[1] = swap(picked)
    first_up, first_down = up(send_up), down(send_down)
    far_up = up(first_rows[:middle])
    chosen_all, slots_all = slots_of(own_ids, all_experts)
    picked = pick(3, late_cotangent)
    late_half = late_cotangent[middle:]
    first_up, first_down, far_up, cotangent_rows[1], chosen_all, slots_all, picked, late_half, frees = after(
        (
            first_up, first_down, far_up, cotangent_rows[1], chosen_all, slots_all, picked, late_half,
            (free_up, free_down),
        )
    )
    cotangent_rows[3] = swap(picked)
    far_down = down(late_half)
    second_up = up(scatter_second(up_rest, first_up))
    second_down = down(scatter_second(down_rest, first_down))
    picked = pick(2, jnp.concatenate([far_up, far_down], axis=0))
    second_up, second_down, picked, cotangent_rows[3], frees = after(
        (second_up, second_down, picked, cotangent_rows[3], frees)
    )

    free_up, free_down = up(frees[0]), down(frees[1])
    cotangent_rows[2] = swap(picked)
    gate_weight, up_weight, down_weight = gate_proj[0], up_proj[0], down_proj[0]
    hidden = inputs.astype(f32) + scatter_own(own_share, second_up, second_down, free_up, free_down)
    inverse_hidden = inverse_rms(hidden)
    routed = (hidden * inverse_hidden * moe_gain).astype(bf16)
    own_rows = after(pick(0, routed), cotangent_rows[2])

    acted_rows, gate_grads, up_grads, row_grads, returned, gate_dots = [], [], [], [], [], []

    def run_expert(step, rows):
        results = expert_block(rows, cotangent_rows[step], gate_weight, up_weight, down_weight)
        for held, result in zip((acted_rows, gate_grads, up_grads, row_grads, returned), results):
            held.append(result)
        gate_dots.append(results[5].reshape(peers, capacity))

    def block_mat(step):
        block_gates = gates_of(chosen_in(ids_blocks[step], all_experts), routed_blocks[step])
        return weighted_mat(step, block_gates)

    routed_blocks, arrived, weighted_mats = [routed], [], {}
    rows, next_rows = own_rows, None
    slot_parts = {}
    for step in range(columns):
        rows = swap(rows)
        coming = None
        if step < columns - 1:
            coming = up(routed_blocks[step])
            next_rows = pick(step + 1, coming)
        if step:
            run_expert(step - 1, arrived[step - 1])
        if step == 0:
            gates = gates_of(chosen_all, routed)
            gate_slots = jnp.sum(jnp.where(slots_all, gates[:, None, :], 0.0), axis=2)
            gate_slots = jnp.take(gate_slots.reshape(peers, columns, capacity), to_ring, axis=1)
            weighted_mats[0] = weighted_mat(0, gates)
            slot_parts = exchange_plane(gate_slots, early_steps)
        elif step == 1:
            slot_parts.update(exchange_plane(gate_slots, late_steps))
        elif step == 2:
            gate_slots = exchange_columns(joined(slot_parts))
            slot_parts = {}
        state = (rows, next_rows, coming, gate_slots, weighted_mats, slot_parts)
        rows, next_rows, coming, gate_slots, weighted_mats, slot_parts = after(state, row_grads)
        arrived.append(rows)
        routed_blocks.append(coming)
        rows = next_rows
    row_weights = [gate_slots[:, step].reshape(peers * capacity, 1) for step in range(columns)]

    row_grads = after(row_grads, arrived[3])
    grad_back = {1: swap(row_grads[1])}
    run_expert(3, arrived[3])
    weighted_mats[1] = block_mat(1)
    grad_back[1], row_grads, gate_dots, weighted_mats = after(
        (grad_back[1], row_grads, gate_dots, weighted_mats)
    )
    grad_back[2] = swap(row_grads[2])
    running = up(collect(grad_back, 1))
    dots = jnp.stack(gate_dots, axis=1)
    dot_parts = exchange_plane(dots, early_steps)
    weighted_mats[2] = block_mat(2)
    running, grad_back[2], dot_parts, weighted_mats = after(
        (running, grad_back[2], dot_parts, weighted_mats)
    )
    grad_back[3] = swap(after(row_grads[3], running))
    running = up(collect(grad_back, 2, running))
    dot_parts.update(exchange_plane(after(dots, grad_back[2]), late_steps))
    weighted_mats[3] = block_mat(3)
    running, grad_back[3], dot_parts, weighted_mats = after(
        (running, grad_back[3], dot_parts, weighted_mats)
    )
    grad_back[0] = swap(after(row_grads[0], running))
    running = up(collect(grad_back, 3, running))
    dots = jnp.take(exchange_columns(joined(dot_parts)), to_ring, axis=1).reshape(experts, capacity)
    running, grad_back[0], dots = after((running, grad_back[0], dots))

    grad_gates = jnp.sum(jnp.where(slots_all, dots[:, :, None], 0.0), axis=1)
    grad_logits = (
        gates * (grad_gates - jnp.sum(gates * grad_gates, axis=0, keepdims=True))
    ).astype(bf16)
    grad_routed = collect(grad_back, 0, running, f32) + lax.dot_general(
        grad_logits, router, (((0,), (1,)), ((), ())), preferred_element_type=f32
    )
    scaled = grad_routed * moe_gain
    grad_hidden = (
        cotangent.astype(f32)
        + scaled * inverse_hidden
        - hidden * (jnp.mean(hidden * scaled, axis=-1, keepdims=True) * inverse_hidden**3)
    )
    grad_moe_gain = jnp.sum(grad_routed * hidden * inverse_hidden, axis=0)
    grad_router = dot_general_t(routed, grad_logits)

    grad_low = grad_hidden.astype(bf16)
    near_gradient = gather_near(grad_low)
    output_back = {1: swap(after(returned[1], grad_back[0]))}
    grad_attended = {0: product(grad_low, full_out)}
    grad_gate_weight, grad_up_weight = weight_gradients(
        after(arrived, grad_low), [gate_grads, up_grads], f32, row_weights
    )
    near_gradient, grad_gate_weight, grad_attended = after(
        (near_gradient, grad_gate_weight, grad_attended)
    )

    far_gradient = gather_far(*near_gradient)
    output_back[2] = swap(after(returned[2], output_back[1], grad_low))
    grad_attended.update({1: product(near_gradient[0], full_out), 3: product(near_gradient[1], full_out)})
    output_part = collect(output_back, 1)
    far_gradient = jnp.concatenate(after(far_gradient, output_part), axis=0)
    far_gradient, grad_attended, output_part = after((far_gradient, grad_attended, output_part))

    grad_sequence = [grad_low, near_gradient[0], far_gradient, near_gradient[1]]
    running = up(output_part)
    output_back[3] = swap(after(returned[3], output_back[2]))
    grad_attended[2] = product(far_gradient, full_out)
    grad_attended = [grad_attended[s] for s in range(columns)]
    half = heads // 2
    arguments = (col_array, qkv, grad_attended, cosine, sine, query_gain, key_gain, levels)
    dp, exp = lax.axis_size("dp"), lax.axis_size("exp")
    tile = width // (dp * exp)

    def weight_parts(lefts, right):
        mine = lax.axis_index("exp")
        if tile % 128 == 0:
            return split_gradient(lefts, right, jnp.reshape(mine, (1,)).astype(jnp.int32), exp, dp)
        (grads,) = weight_gradients(lefts, [right], bf16)
        grads = grads.reshape(dp, exp, tile, -1).transpose(1, 0, 2, 3).reshape(exp, dp * tile, -1)
        return [
            lax.dynamic_index_in_dim(grads, lax.rem(mine + step, exp), 0, keepdims=False)
            for step in range(exp)
        ]

    def exchange_parts(parts):
        return [
            lax.ppermute(part, "exp", [(i, (i + step) % exp) for i in range(exp)]) if step else part
            for step, part in enumerate(parts)
        ]

    def sum_of(parts):
        return sum(part.astype(f32) for part in parts).astype(bf16)

    def swap_parts(sums):
        parts = sums.reshape(dp, -1, sums.shape[1])
        return lax.all_to_all(parts, "dp", 0, 0, tiled=True)

    out_parts = exchange_parts(weight_parts(grad_sequence, attended))
    first_half = attention_backward(*arguments, 0, half)
    first_half, out_parts = after((first_half, out_parts))
    out_sums = sum_of(out_parts)
    running = after(running, out_sums)
    out_sums = swap_parts(after(out_sums, output_back[3]))
    output_part = collect(output_back, 2, running)
    router_sums = grad_router.reshape(1, columns, width // columns * experts)
    router_sums = jnp.take(after(router_sums, running), to_ring, axis=1)
    router_sums = jnp.sum(exchange_columns(router_sums)[0], axis=0)
    running = up(output_part)
    *grad_qkv, grad_query_gain, grad_key_gain, _, _ = attention_backward(
        *arguments, half, heads - half, after(first_half, output_part)
    )
    grad_query_gain, grad_key_gain = grad_query_gain[0], grad_key_gain[0]

    grad_qkv, out_sums = after((grad_qkv, out_sums))
    *shares, attn_gain_sums = spread(grad_qkv, full_qkv, units)
    send_up, send_down, free_up, free_down, up_rest, down_rest, own_share = shares
    first_up, first_down = up(send_up), down(send_down)
    output_part = collect(after(output_back, attn_gain_sums), 3, running)
    (grad_down,) = weight_gradients(
        after(acted_rows, attn_gain_sums), [cotangent_rows], f32, row_weights
    )
    output_back[0] = swap(after(returned[0], out_sums))
    free_up, free_down = up(free_up), down(free_down)
    qkv_parts = weight_parts(normed, after(grad_qkv, attn_gain_sums))
    first_up, first_down, free_up, free_down, grad_down, output_part, qkv_parts, output_back[0] = after(
        (first_up, first_down, free_up, free_down, grad_down, output_part, qkv_parts, output_back[0])
    )

    second_up = up(scatter_second(up_rest, first_up))
    second_down = down(scatter_second(down_rest, first_down))
    running = up(output_part)
    reduced_out = jnp.sum(out_sums.astype(f32), axis=0)
    qkv_sums = sum_of(exchange_parts(qkv_parts))

    qkv_parts = swap_parts(after(qkv_sums, output_back[0]))
    small = jnp.concatenate([attn_gain_sums[0], grad_query_gain, grad_key_gain, grad_moe_gain])
    cuts = [0, width, width + head_size, width + 2 * head_size, 2 * (width + head_size)]
    small = jnp.concatenate([small, router_sums])
    small = swap(after(jnp.broadcast_to(small, (peers, small.shape[0])), qkv_parts))
    reduced_qkv = jnp.sum(qkv_parts.astype(f32), axis=0)
    outputs = (hidden + collect(output_back, 0, running, f32)).astype(bf16)
    small = jnp.sum(small, axis=0)
    small = jnp.stack([small, *[shifted(small, step) for step in range(1, columns)]])
    to_true = lax.rem(col - jnp.arange(columns, dtype=jnp.int32) + columns, columns)
    grad_router = jnp.take(small[:, cuts[-1] :], to_true, axis=0).reshape(width, experts)
    small = jnp.sum(small[:, : cuts[-1]], axis=0)
    shared = [small[i:j] for i, j in zip(cuts, cuts[1:])]

    grad_normed = scatter_own(own_share, second_up, second_down, free_up, free_down)
    input_rows = inputs.astype(f32)
    inverse_own = inverse_rms(input_rows)
    scaled_in = grad_normed * attn_gain
    grad_inputs = (
        grad_hidden
        + scaled_in * inverse_own
        - input_rows * (jnp.mean(input_rows * scaled_in, axis=-1, keepdims=True) * inverse_own**3)
    ).astype(bf16)

    split = heads * head_size
    return (
        outputs,
        grad_inputs,
        shared[0],
        reduced_qkv[:, :split],
        reduced_qkv[:, split : split + head_size],
        reduced_qkv[:, split + head_size :],
        shared[1],
        shared[2],
        reduced_out,
        shared[3],
        grad_router,
        grad_gate_weight[None],
        grad_up_weight[None],
        grad_down[None],
    )


def dot_general_t(a, b):
    contract = (((0,), (1,)), ((), ()))
    return lax.dot_general(a, b, contract, preferred_element_type=f32)


def solution(mesh):
    return jax.shard_map(
        local,
        mesh=mesh,
        in_specs=(
            P(("dp", "exp", "col"), None),
            P(("dp", "exp", "col"), None),
            P(("dp", "exp")),
            P(("dp", "exp", "col"), None),
            P(),
            P("exp", "col"),
            P("exp", "col"),
            P("exp", "col"),
            P(),
            P(),
            P("exp", "col"),
            P(),
            P(),
            P(("dp", "exp", "col"), None, None),
            P(("dp", "exp", "col"), None, None),
            P(("dp", "exp", "col"), None, None),
        ),
        out_specs=(
            P(("dp", "exp", "col"), None),
            P(("dp", "exp", "col"), None),
            P(),
            P(("dp", "exp"), "col"),
            P(("dp", "exp"), "col"),
            P(("dp", "exp"), "col"),
            P(),
            P(),
            P(("dp", "exp"), "col"),
            P(),
            P(),
            P(("dp", "exp", "col"), None, None),
            P(("dp", "exp", "col"), None, None),
            P(("dp", "exp", "col"), None, None),
        ),
        check_vma=False,
    )
```

```python
import functools
import math

import jax
import jax.numpy as jnp
from jax import lax
from jax.experimental import pallas as pl
from jax.experimental.pallas import tpu as pltpu
from jax.sharding import PartitionSpec as P

epsilon = 1e-06
rotary_base = 1000000.0
plane = ("dp", "exp")
everyone = ("dp", "exp", "col")
f32 = jnp.float32
bf16 = jnp.bfloat16


def dot_nn(a, b):
    return lax.dot_general(a, b, (((1,), (0,)), ((), ())), preferred_element_type=f32)


def dot_nt(a, b):
    return lax.dot_general(a, b, (((1,), (1,)), ((), ())), preferred_element_type=f32)


def dot_tn(a, b):
    return lax.dot_general(a, b, (((0,), (0,)), ((), ())), preferred_element_type=f32)


def inverse_rms(rows):
    return lax.rsqrt(jnp.mean(rows * rows, axis=-1, keepdims=True) + epsilon)


def rotary_tables(positions, head_size):
    halves = head_size // 2
    frequency = rotary_base ** (-2.0 * jnp.arange(halves, dtype=f32) / head_size)
    angles = positions.astype(f32)[:, None] * frequency[None, :]
    cosine, sine = jnp.cos(angles), jnp.sin(angles)
    return (
        jnp.concatenate([cosine, cosine], axis=1),
        jnp.concatenate([-sine, sine], axis=1),
    )


def turn(rows, cosine, sine):
    return rows * cosine + pltpu.roll(rows, rows.shape[-1] // 2, 1) * sine


def turn_back(rows, cosine, sine):
    return rows * cosine - pltpu.roll(rows, rows.shape[-1] // 2, 1) * sine


def place_of(col_ref, blocks, tokens, step):
    return pl.multiple_of(lax.rem(col_ref[0] - step + blocks, blocks) * tokens, tokens)


def in_order(col_ref, refs, held):
    tokens = refs[0].shape[0]
    for step, ref in enumerate(refs):
        held[pl.ds(place_of(col_ref, len(refs), tokens, step), tokens), :] = ref[...].astype(held.dtype)


def out_of_order(col_ref, held, refs):
    tokens = refs[0].shape[0]
    for step, ref in enumerate(refs):
        ref[...] = held[pl.ds(place_of(col_ref, len(refs), tokens, step), tokens), :].astype(ref.dtype)


def scores_of(keys, query, first, scale):
    count = query.shape[0]
    scores = dot_nt(keys[pl.ds(0, first + count), :], query) * (scale * math.log2(math.e))
    row = lax.broadcasted_iota(jnp.int32, (count, count), 0)
    column = lax.broadcasted_iota(jnp.int32, (count, count), 1)
    last = jnp.where(row <= column, scores[first:], -1e30)
    return jnp.concatenate([scores[:first], last], axis=0) if first else last


def prepare_keys(col_ref, k_refs, v_refs, cos_ref, sin_ref, kg_ref, raw_rows, keys, values):
    in_order(col_ref, k_refs, raw_rows)
    in_order(col_ref, v_refs, values)
    tokens = k_refs[0].shape[0]
    for block in range(len(k_refs)):
        there = pl.ds(block * tokens, tokens)
        raw = raw_rows[there, :]
        rows = raw * inverse_rms(raw) * kg_ref[...]
        keys[there, :] = turn(rows, cos_ref[there, :], sin_ref[there, :]).astype(bf16)


def forward_kernel(blocks, scale, col_ref, *refs):
    q_refs, k_refs, v_refs = refs[:blocks], refs[blocks : 2 * blocks], refs[2 * blocks : 3 * blocks]
    cos_ref, sin_ref, qg_ref, kg_ref = refs[3 * blocks : 3 * blocks + 4]
    out_refs = refs[3 * blocks + 4 : 4 * blocks + 4]
    level_ref, raw_rows, keys, values, mixed_rows = refs[4 * blocks + 4 :]
    tokens = q_refs[0].shape[0]

    @pl.when(pl.program_id(0) == 0)
    def _():
        prepare_keys(col_ref, k_refs, v_refs, cos_ref, sin_ref, kg_ref, raw_rows, keys, values)

    in_order(col_ref, q_refs, raw_rows)
    for block in range(blocks):
        first = block * tokens
        there = pl.ds(first, tokens)
        raw = raw_rows[there, :]
        rows = raw * inverse_rms(raw) * qg_ref[...]
        query = turn(rows, cos_ref[there, :], sin_ref[there, :]).astype(bf16)
        scores = scores_of(keys, query, first, scale)
        peak = jnp.max(scores, axis=0, keepdims=True)
        probs = jnp.exp2(scores - peak)
        total = jnp.sum(probs, axis=0, keepdims=True)
        level_ref[0, :, there] = peak + jnp.log2(total)
        probs = (probs * (1.0 / total)).astype(bf16)
        mixed_rows[there, :] = dot_tn(probs, values[pl.ds(0, first + tokens), :]).astype(bf16)
    out_of_order(col_ref, mixed_rows, out_refs)


def attention_forward(col, qkv, cosine, sine, query_gain, key_gain, heads):
    blocks, tokens, head_size = len(qkv), qkv[0].shape[0], query_gain.shape[-1]
    seq_len = blocks * tokens
    column = lambda index: [pl.BlockSpec((tokens, head_size), index)] * blocks
    whole = pl.BlockSpec((seq_len, head_size), lambda h, c: (0, 0))
    gain = pl.BlockSpec((1, head_size), lambda h, c: (0, 0))
    return pl.pallas_call(
        functools.partial(forward_kernel, blocks, head_size ** (-0.5)),
        out_shape=[
            *[jax.ShapeDtypeStruct((tokens, heads * head_size), bf16)] * blocks,
            jax.ShapeDtypeStruct((heads, 1, seq_len), f32),
        ],
        grid_spec=pltpu.PrefetchScalarGridSpec(
            num_scalar_prefetch=1,
            grid=(heads,),
            in_specs=[
                *column(lambda h, c: (0, h)),
                *column(lambda h, c: (0, heads)),
                *column(lambda h, c: (0, heads + 1)),
                whole,
                whole,
                gain,
                gain,
            ],
            out_specs=[
                *column(lambda h, c: (0, h)),
                pl.BlockSpec((1, 1, seq_len), lambda h, c: (h, 0, 0)),
            ],
            scratch_shapes=[
                pltpu.VMEM((seq_len, head_size), f32),
                pltpu.VMEM((seq_len, head_size), bf16),
                pltpu.VMEM((seq_len, head_size), bf16),
                pltpu.VMEM((seq_len, head_size), bf16),
            ],
        ),
        compiler_params=pltpu.CompilerParams(vmem_limit_bytes=60 * 2**20),
        cost_estimate=pl.CostEstimate(flops=1000, bytes_accessed=1000, transcendentals=0),
        name="attention_forward",
    )(col, *qkv, *qkv, *qkv, cosine, sine, query_gain, key_gain)


def backward_kernel(blocks, scale, first_head, heads, final, col_ref, *refs):
    q_refs, k_refs, v_refs, g_refs = (refs[i * blocks : (i + 1) * blocks] for i in range(4))
    cos_ref, sin_ref, qg_ref, kg_ref, level_ref = refs[4 * blocks : 4 * blocks + 5]
    refs = refs[4 * blocks + 5 :]
    if first_head:
        refs = refs[blocks:]
        held_refs, refs = refs[:4], refs[4:]
    grad_refs, refs = refs[:blocks], refs[blocks:]
    qgain_ref, kgain_ref, out_keys, out_values = refs[:4]
    raw_rows, mixed_rows, keys, values, grad_rows, grad_keys, grad_values = refs[4:]
    tokens = q_refs[0].shape[0]
    step = pl.program_id(0)

    @pl.when(step == 0)
    def _():
        prepare_keys(col_ref, k_refs, v_refs, cos_ref, sin_ref, kg_ref, raw_rows, keys, values)
        if first_head:
            qgain_ref[...] = held_refs[0][...]
            kgain_ref[...] = held_refs[1][...]
            grad_keys[...] = held_refs[2][...]
            grad_values[...] = held_refs[3][...]
        else:
            grad_keys[...] = jnp.zeros_like(grad_keys)
            grad_values[...] = jnp.zeros_like(grad_values)
            qgain_ref[...] = jnp.zeros_like(qgain_ref)
            kgain_ref[...] = jnp.zeros_like(kgain_ref)

    def through_norm(grad_rot, unit, inverse, there, gain_ref, gain_grad_ref):
        grad_scaled = turn_back(grad_rot, cos_ref[there, :], sin_ref[there, :])
        gain_grad_ref[0:1, :] += jnp.sum(grad_scaled * unit, axis=0, keepdims=True)
        grad_unit = grad_scaled * gain_ref[...]
        return inverse * (grad_unit - unit * jnp.mean(grad_unit * unit, axis=1, keepdims=True))

    @pl.when(step < heads)
    def _():
        in_order(col_ref, q_refs, raw_rows)
        in_order(col_ref, g_refs, mixed_rows)
        for block in range(blocks):
            first = block * tokens
            there = pl.ds(first, tokens)
            raw = raw_rows[there, :]
            inverse = inverse_rms(raw)
            unit = raw * inverse
            query = turn(unit * qg_ref[...], cos_ref[there, :], sin_ref[there, :]).astype(bf16)
            grad_mixed = mixed_rows[there, :]
            upto = pl.ds(0, first + tokens)
            probs = jnp.exp2(scores_of(keys, query, first, scale) - level_ref[0, :, there])
            grad_probs = dot_nt(values[upto, :], grad_mixed)
            inner = jnp.sum(probs * grad_probs, axis=0, keepdims=True)
            grad_scores = (probs * (grad_probs - inner)).astype(bf16)
            grad_values[upto, :] += dot_nn(probs.astype(bf16), grad_mixed)
            grad_keys[upto, :] += dot_nn(grad_scores, query)
            grad_query = dot_tn(grad_scores, keys[upto, :])
            grad_rows[there, :] = through_norm(
                grad_query * scale, unit, inverse, there, qg_ref, qgain_ref
            ).astype(bf16)

    if not final:

        @pl.when(step == heads - 1)
        def _():
            out_keys[...] = grad_keys[...]
            out_values[...] = grad_values[...]

    @pl.when(step == heads)
    def _():
        in_order(col_ref, k_refs, raw_rows)
        for block in range(blocks):
            there = pl.ds(block * tokens, tokens)
            raw = raw_rows[there, :]
            inverse = inverse_rms(raw)
            grad_rows[there, :] = through_norm(
                grad_keys[there, :] * scale, raw * inverse, inverse, there, kg_ref, kgain_ref
            ).astype(bf16)

    @pl.when(step == heads + 1)
    def _():
        grad_rows[...] = grad_values[...].astype(bf16)

    out_of_order(col_ref, grad_rows, grad_refs)


def attention_backward(
    col, qkv, grad_attended, cosine, sine, query_gain, key_gain, levels, first, heads, former=None
):
    blocks, tokens, head_size = len(qkv), qkv[0].shape[0], query_gain.shape[-1]
    seq_len = blocks * tokens
    all_heads = levels.shape[0]
    final = first + heads == all_heads
    column = lambda index: [pl.BlockSpec((tokens, head_size), index)] * blocks
    whole = pl.BlockSpec((seq_len, head_size), lambda h, c: (0, 0))
    gain = pl.BlockSpec((1, head_size), lambda h, c: (0, 0))
    gain_out = pl.BlockSpec((8, head_size), lambda h, c: (0, 0))
    last = all_heads - 1
    held = [] if former is None else former
    return pl.pallas_call(
        functools.partial(backward_kernel, blocks, head_size ** (-0.5), first, heads, final),
        out_shape=[
            *[jax.ShapeDtypeStruct(qkv[0].shape, bf16)] * blocks,
            jax.ShapeDtypeStruct((8, head_size), f32),
            jax.ShapeDtypeStruct((8, head_size), f32),
            jax.ShapeDtypeStruct((seq_len, head_size), f32),
            jax.ShapeDtypeStruct((seq_len, head_size), f32),
        ],
        grid_spec=pltpu.PrefetchScalarGridSpec(
            num_scalar_prefetch=1,
            grid=(heads + 2 if final else heads,),
            in_specs=[
                *column(lambda h, c: (0, jnp.minimum(h + first, last))),
                *column(lambda h, c: (0, all_heads)),
                *column(lambda h, c: (0, all_heads + 1)),
                *column(lambda h, c: (0, jnp.minimum(h + first, last))),
                whole,
                whole,
                gain,
                gain,
                pl.BlockSpec((1, 1, seq_len), lambda h, c: (jnp.minimum(h + first, last), 0, 0)),
                *([] if former is None else [pl.BlockSpec(memory_space=pl.ANY)] * blocks),
                *([] if former is None else [gain_out, gain_out, whole, whole]),
            ],
            out_specs=[*column(lambda h, c: (0, h + first)), gain_out, gain_out, whole, whole],
            scratch_shapes=[
                pltpu.VMEM((seq_len, head_size), f32),
                pltpu.VMEM((seq_len, head_size), bf16),
                pltpu.VMEM((seq_len, head_size), bf16),
                pltpu.VMEM((seq_len, head_size), bf16),
                pltpu.VMEM((seq_len, head_size), bf16),
                pltpu.VMEM((seq_len, head_size), f32),
                pltpu.VMEM((seq_len, head_size), f32),
            ],
        ),
        input_output_aliases={} if former is None else {1 + 4 * blocks + 5 + i: i for i in range(blocks)},
        compiler_params=pltpu.CompilerParams(vmem_limit_bytes=60 * 2**20),
        cost_estimate=pl.CostEstimate(flops=1000, bytes_accessed=1000, transcendentals=0),
        name="attention_backward",
    )(col, *qkv, *qkv, *qkv, *grad_attended, cosine, sine, query_gain, key_gain, levels, *held)


def weight_kernel(blocks, rights, weighted, *refs):
    left_refs, refs = refs[:blocks], refs[blocks:]
    right_refs, refs = refs[: blocks * rights], refs[blocks * rights :]
    if weighted:
        weight_refs, refs = refs[:blocks], refs[blocks:]
        out_refs, held = refs[:rights], refs[rights:]

        @pl.when(pl.program_id(0) == 0)
        def _():
            for index, ref in enumerate(right_refs):
                scaled = ref[...].astype(f32) * weight_refs[index % blocks][...]
                held[index][...] = scaled.astype(bf16)

        right_refs = held
    else:
        out_refs = refs
    for index, out_ref in enumerate(out_refs):
        total = dot_tn(left_refs[0][...], right_refs[index * blocks][...])
        for block in range(1, blocks):
            total = total + dot_tn(left_refs[block][...], right_refs[index * blocks + block][...])
        out_ref[...] = total.astype(out_ref.dtype)


def weight_gradients(lefts, rights, out_type, weights=None, tile=256):
    blocks, rows, tall = len(lefts), lefts[0].shape[0], lefts[0].shape[1]
    flat = [block for right in rights for block in right]
    fixed = lambda array: pl.BlockSpec(array.shape, lambda i: (0, 0))
    return pl.pallas_call(
        functools.partial(weight_kernel, blocks, len(rights), weights is not None),
        out_shape=[jax.ShapeDtypeStruct((tall, right[0].shape[1]), out_type) for right in rights],
        grid=(tall // tile,),
        in_specs=[
            *[pl.BlockSpec((rows, tile), lambda i: (0, i))] * blocks,
            *[fixed(block) for block in flat],
            *([] if weights is None else [fixed(weight) for weight in weights]),
        ],
        out_specs=[
            pl.BlockSpec((tile, right[0].shape[1]), lambda i: (i, 0)) for right in rights
        ],
        scratch_shapes=[] if weights is None else [pltpu.VMEM(block.shape, bf16) for block in flat],
        compiler_params=pltpu.CompilerParams(vmem_limit_bytes=60 * 2**20),
        cost_estimate=pl.CostEstimate(flops=1000, bytes_accessed=1000, transcendentals=0),
        name="weight_gradients",
    )(*lefts, *flat, *([] if weights is None else weights))


def split_kernel(blocks, groups, mine_ref, *refs):
    left_refs, right_refs, out_refs = refs[:blocks], refs[blocks : 2 * blocks], refs[2 * blocks :]
    total = dot_tn(left_refs[0][...], right_refs[0][...])
    for block in range(1, blocks):
        total = total + dot_tn(left_refs[block][...], right_refs[block][...])
    for index, out_ref in enumerate(out_refs):

        @pl.when(pl.program_id(0) // groups == index)
        def _():
            out_ref[...] = total.astype(out_ref.dtype)


def split_gradient(lefts, right, mine, devices, groups):
    blocks, rows, tall = len(lefts), lefts[0].shape[0], lefts[0].shape[1]
    tile, wide = tall // (devices * groups), right[0].shape[1]

    def left_tile(i, mine_ref):
        return (0, i % groups * devices + lax.rem(mine_ref[0] + i // groups, devices))

    def out_tile(index):
        return lambda i, mine_ref: (jnp.clip(i - index * groups, 0, groups - 1), 0)

    return pl.pallas_call(
        functools.partial(split_kernel, blocks, groups),
        out_shape=[jax.ShapeDtypeStruct((groups * tile, wide), bf16)] * devices,
        grid_spec=pltpu.PrefetchScalarGridSpec(
            num_scalar_prefetch=1,
            grid=(devices * groups,),
            in_specs=[
                *[pl.BlockSpec((rows, tile), left_tile)] * blocks,
                *[pl.BlockSpec((rows, wide), lambda i, mine_ref: (0, 0))] * blocks,
            ],
            out_specs=[pl.BlockSpec((tile, wide), out_tile(index)) for index in range(devices)],
        ),
        compiler_params=pltpu.CompilerParams(vmem_limit_bytes=60 * 2**20),
        cost_estimate=pl.CostEstimate(flops=1000, bytes_accessed=1000, transcendentals=0),
        name="split_gradient",
    )(mine, *lefts, *right)


def spread_kernel(with_units, *refs):
    block_refs, weight_ref, refs = refs[:4], refs[4], refs[5:]
    if with_units:
        unit_refs, refs = refs[:4], refs[4:]
    far_up, far_down, free_up, free_down, up_rest, down_rest, own_ref = refs[:7]
    weight = weight_ref[...]
    middle = own_ref.shape[0] // 2
    shares = {}
    for step in (2, 3, 1, 0):
        shares[step] = dot_nt(block_refs[step][...], weight)
    far_up[...] = shares[2][:middle].astype(bf16)
    far_down[...] = shares[2][middle:].astype(bf16)
    free_up[...] = shares[3][middle:].astype(bf16)
    free_down[...] = shares[1][:middle].astype(bf16)
    up_rest[...] = shares[3][:middle]
    down_rest[...] = shares[1][middle:]
    own_ref[...] = shares[0]
    if with_units:
        total = sum(
            jnp.sum(shares[step] * unit_refs[step][...], axis=0, keepdims=True) for step in range(4)
        )
        refs[7][...] = jnp.broadcast_to(total, refs[7].shape)


def spread(blocks, weight, units=None, tile=512):
    tokens, depth = blocks[0].shape
    width = weight.shape[0]
    part = lambda rows: pl.BlockSpec((rows, tile), lambda i: (0, i))
    shape = jax.ShapeDtypeStruct
    return pl.pallas_call(
        functools.partial(spread_kernel, units is not None),
        out_shape=[
            *[shape((tokens // 2, width), bf16)] * 4,
            *[shape((tokens // 2, width), f32)] * 2,
            shape((tokens, width), f32),
            *([] if units is None else [shape((8, width), f32)]),
        ],
        grid=(width // tile,),
        in_specs=[
            *[pl.BlockSpec((tokens, depth), lambda i: (0, 0))] * 4,
            pl.BlockSpec((tile, depth), lambda i: (i, 0)),
            *([] if units is None else [part(tokens)] * 4),
        ],
        out_specs=[
            *[part(tokens // 2)] * 6,
            part(tokens),
            *([] if units is None else [part(8)]),
        ],
        compiler_params=pltpu.CompilerParams(vmem_limit_bytes=60 * 2**20),
        cost_estimate=pl.CostEstimate(flops=1000, bytes_accessed=1000, transcendentals=0),
        name="spread",
    )(*blocks, weight, *([] if units is None else units))


def product_kernel(transposed, left_ref, right_ref, *refs):
    result = (dot_tn if transposed else dot_nn)(left_ref[...], right_ref[...])
    if len(refs) > 1:
        result = result + refs[0][...].astype(f32)
    refs[-1][...] = result.astype(refs[-1].dtype)


def product(left, right, addend=None, out_type=bf16, transposed=False, tile=512):
    rows = left.shape[1 if transposed else 0]
    part = lambda height: pl.BlockSpec((height, tile), lambda i: (0, i))
    return pl.pallas_call(
        functools.partial(product_kernel, transposed),
        out_shape=jax.ShapeDtypeStruct((rows, right.shape[1]), out_type),
        grid=(right.shape[1] // tile,),
        in_specs=[
            pl.BlockSpec(left.shape, lambda i: (0, 0)),
            part(right.shape[0]),
            *([] if addend is None else [part(rows)]),
        ],
        out_specs=part(rows),
        compiler_params=pltpu.CompilerParams(vmem_limit_bytes=60 * 2**20),
        cost_estimate=pl.CostEstimate(flops=1000, bytes_accessed=1000, transcendentals=0),
        name="product",
    )(left, right, *([] if addend is None else [addend]))


def expert_kernel(
    rows_ref, upstream_ref, gate_ref, up_ref, down_ref,
    acted_ref, gate_grad_ref, up_grad_ref, row_grad_ref, returned_ref, dots_ref,
    gates, ups, downs, gate_grads, up_grads, acted_rows,
):
    step = pl.program_id(0)
    tile = gate_ref.shape[1]
    gate_part = dot_nn(rows_ref[...], gate_ref[...])
    up_part = dot_nn(rows_ref[...], up_ref[...])
    drive = dot_nt(upstream_ref[...], down_ref[...])
    sigmoid = jax.nn.sigmoid(gate_part)
    silu = gate_part * sigmoid
    acted = silu * up_part
    acted_low = acted.astype(bf16)
    gate_grad = (drive * up_part * sigmoid * (1.0 + gate_part * (1.0 - sigmoid))).astype(bf16)
    up_grad = (drive * silu).astype(bf16)
    acted_ref[...] = acted_low
    gate_grad_ref[...] = gate_grad
    up_grad_ref[...] = up_grad
    dots = jnp.sum(acted * drive, axis=1, keepdims=True)
    for index in range(gates.shape[1] // tile):

        @pl.when(step == index)
        def _():
            here = pl.ds(index * tile, tile)
            gates[:, here] = gate_ref[...]
            ups[:, here] = up_ref[...]
            downs[here, :] = down_ref[...]
            gate_grads[:, here] = gate_grad
            up_grads[:, here] = up_grad
            acted_rows[:, here] = acted_low

    @pl.when(step == 0)
    def _():
        dots_ref[...] = dots

    @pl.when(step > 0)
    def _():
        dots_ref[...] += dots

    @pl.when(step == pl.num_programs(0) - 1)
    def _():
        for first in range(0, row_grad_ref.shape[1], 512):
            here = pl.ds(first, 512)
            row_grad_ref[:, here] = (
                dot_nt(gate_grads[...], gates[here, :]) + dot_nt(up_grads[...], ups[here, :])
            ).astype(bf16)
            returned_ref[:, here] = dot_nn(acted_rows[...], downs[:, here]).astype(bf16)


def expert_block(rows, upstream_rows, gate_weight, up_weight, down_weight, tile=256):
    count, width = rows.shape
    hidden = gate_weight.shape[1]
    shape = jax.ShapeDtypeStruct
    whole = pl.BlockSpec((count, width), lambda j: (0, 0))
    part = pl.BlockSpec((count, tile), lambda j: (0, j))
    return pl.pallas_call(
        expert_kernel,
        out_shape=[
            shape((count, hidden), bf16),
            shape((count, hidden), bf16),
            shape((count, hidden), bf16),
            shape((count, width), bf16),
            shape((count, width), bf16),
            shape((count, 1), f32),
        ],
        grid=(hidden // tile,),
        in_specs=[
            whole,
            whole,
            pl.BlockSpec((width, tile), lambda j: (0, j)),
            pl.BlockSpec((width, tile), lambda j: (0, j)),
            pl.BlockSpec((tile, width), lambda j: (j, 0)),
        ],
        out_specs=[part, part, part, whole, whole, pl.BlockSpec((count, 1), lambda j: (0, 0))],
        scratch_shapes=[
            pltpu.VMEM((width, hidden), bf16),
            pltpu.VMEM((width, hidden), bf16),
            pltpu.VMEM((hidden, width), bf16),
            pltpu.VMEM((count, hidden), bf16),
            pltpu.VMEM((count, hidden), bf16),
            pltpu.VMEM((count, hidden), bf16),
        ],
        compiler_params=pltpu.CompilerParams(vmem_limit_bytes=60 * 2**20),
        cost_estimate=pl.CostEstimate(flops=1000, bytes_accessed=1000, transcendentals=0),
        name="expert_block",
    )(rows, upstream_rows, gate_weight, up_weight, down_weight)


def local(
    inputs,
    expert_ids,
    positions,
    cotangent,
    attn_gain,
    query_proj,
    key_projection,
    value_projection,
    query_norm_gain,
    key_norm_gain,
    out_proj,
    moe_gain,
    router,
    gate_proj,
    up_proj,
    down_proj,
):
    tokens, width = inputs.shape
    head_size = query_norm_gain.shape[0]
    choices = expert_ids.shape[1]
    experts = router.shape[1]
    capacity = tokens * choices * 5 // (4 * experts)
    columns = lax.axis_size("col")
    peers = lax.axis_size("dp") * lax.axis_size("exp")
    col = lax.axis_index("col")
    here = lax.axis_index("dp") * lax.axis_size("exp") + lax.axis_index("exp")
    col_array = jnp.reshape(col, (1,)).astype(jnp.int32)
    heads = query_proj.shape[1] // head_size
    assert key_projection.shape[1] == head_size and experts == peers * columns
    assert columns == 4 and tokens % 32 == 0
    middle = tokens // 2

    def shifted(block, by):
        return lax.ppermute(block, "col", [(i, (i + by) % columns) for i in range(columns)])

    def up(block):
        return shifted(block, 1)

    def down(block):
        return shifted(block, -1)

    def gather_near(block):
        return up(block), down(block)

    def gather_far(former, latter):
        return up(former[:middle]), down(latter[middle:])

    def scatter_second(rest, far):
        return (rest + far.astype(f32)).astype(bf16)

    def scatter_own(own, second_up, second_down, free_up, free_down):
        return own + jnp.concatenate(
            [
                second_up.astype(f32) + free_down.astype(f32),
                free_up.astype(f32) + second_down.astype(f32),
            ],
            axis=0,
        )

    def swap(rows):
        return lax.all_to_all(
            rows.reshape(peers, rows.shape[0] // peers, *rows.shape[1:]), plane, 0, 0, tiled=True
        ).reshape(rows.shape)

    def swap_all(values):
        return lax.all_to_all(values, everyone, 0, 0, tiled=True)

    def after(value, *others):
        return lax.optimization_barrier((value, others))[0]

    def exchange_plane(values, steps):
        parts = {}
        for step in steps:
            part = lax.dynamic_index_in_dim(values, lax.rem(here + step, peers), 0, keepdims=False)
            pairs = [(i, (i + step) % peers) for i in range(peers)]
            parts[step] = lax.ppermute(part, plane, pairs) if step else part
        return parts

    def joined(parts):
        order = lax.rem(here - jnp.arange(peers, dtype=jnp.int32) + peers, peers)
        return jnp.take(jnp.stack([parts[step] for step in range(peers)]), order, axis=0)

    early_steps, late_steps = range(peers // 2), range(peers // 2, peers)

    def exchange_columns(values):
        parts = [values[:, 0], *[shifted(values[:, s], -s) for s in range(1, columns)]]
        return jnp.stack([parts[0], *parts[:0:-1]], axis=1)

    to_ring = lax.rem(col - jnp.arange(columns, dtype=jnp.int32) + columns, columns)

    earlier = (
        lax.broadcasted_iota(jnp.int32, (tokens, tokens), 0)
        < lax.broadcasted_iota(jnp.int32, (tokens, tokens), 1)
    ).astype(bf16)
    all_experts = jnp.arange(experts, dtype=jnp.int32)
    plane_experts = jnp.arange(peers, dtype=jnp.int32) * columns + col

    def chosen_in(ids, named):
        return jnp.any(ids[None, :, :] == named[:, None, None], axis=1)

    def slots_of(ids, named):
        chosen = chosen_in(ids, named)
        rank = dot_nn(chosen.astype(bf16), earlier)
        code = jnp.where(chosen, rank, -1.0)
        place = lax.broadcasted_iota(jnp.int32, (1, capacity, 1), 1).astype(f32)
        return chosen, code[:, None, :] == place

    def slot_mat(ids):
        return slots_of(ids, plane_experts)[1].astype(bf16).reshape(peers * capacity, tokens)

    def pick(step, block):
        return product(slot_mats[step], block)

    def gates_of(chosen, block):
        logits = jnp.where(chosen, dot_general_t(router, block), -1e30)
        exponent = jnp.exp(logits - jnp.max(logits, axis=0, keepdims=True))
        exponent = jnp.where(chosen, exponent, 0.0)
        return exponent / jnp.sum(exponent, axis=0, keepdims=True)

    def weighted_mat(step, block_gates):
        gates_here = block_gates.reshape(peers, columns, 1, tokens)
        gates_here = lax.dynamic_index_in_dim(gates_here, col, 1, keepdims=False)
        mat = slot_mats[step].reshape(peers, capacity, tokens) * gates_here
        return mat.astype(bf16).reshape(peers * capacity, tokens)

    def collect(back, step, addend=None, out_type=bf16):
        return product(weighted_mats[step], back[step], addend, out_type, transposed=True)

    near_inputs = gather_near(inputs)
    local_qkv = jnp.concatenate([query_proj, key_projection, value_projection], axis=1)
    full_qkv = lax.all_gather(local_qkv, "exp", axis=0, tiled=True)
    full_out = lax.all_gather(out_proj, "exp", axis=0, tiled=True)
    own_ids = expert_ids.T
    slot_mats = [slot_mat(own_ids)]
    cotangent_rows = [swap(pick(0, cotangent)), None, None, None]
    near_inputs, full_qkv = after((near_inputs, full_qkv))

    far_inputs = jnp.concatenate(gather_far(*near_inputs), axis=0)
    def project(block):
        rows = block.astype(f32)
        unit = rows * inverse_rms(rows)
        low = (unit * attn_gain).astype(bf16)
        return unit, low, dot_nn(low, full_qkv)

    projected = [project(inputs), project(near_inputs[0]), None, project(near_inputs[1])]
    cosine, sine = rotary_tables(positions, head_size)
    far_inputs, cotangent_rows[0], cosine, sine = after(
        (far_inputs, cotangent_rows[0], cosine, sine),
        [projected[s][2] for s in (0, 1, 3)],
    )

    near_cotangent = gather_near(after(cotangent, far_inputs))
    later_ids = after(own_ids, far_inputs)
    ids_blocks = [own_ids, *[shifted(later_ids, step) for step in range(1, columns)]]
    projected[2] = project(far_inputs)
    units, normed, qkv = zip(*projected)
    query_gain, key_gain = query_norm_gain[None, :], key_norm_gain[None, :]
    *attended, levels = attention_forward(col_array, qkv, cosine, sine, query_gain, key_gain, heads)
    shares = spread(attended, full_out)
    ids_blocks = after(ids_blocks, attended)
    slot_mats += [slot_mat(ids_blocks[s]) for s in (1, 2, 3)]
    picked = pick(1, after(near_cotangent[0], attended))
    near_cotangent, shares, slot_mats, picked = after((near_cotangent, shares, slot_mats, picked))

    send_up, send_down, free_up, free_down, up_rest, down_rest, own_share = shares
    cotangent_rows[1] = swap(picked)
    first_up, first_down = up(send_up), down(send_down)
    far_up = up(near_cotangent[0][:middle])
    chosen_all, slots_all = slots_of(own_ids, all_experts)
    picked = pick(3, near_cotangent[1])
    late_half = near_cotangent[1][middle:]
    first_up, first_down, far_up, cotangent_rows[1], chosen_all, slots_all, picked, late_half, frees = after(
        (
            first_up, first_down, far_up, cotangent_rows[1], chosen_all, slots_all, picked, late_half,
            (free_up, free_down),
        )
    )
    cotangent_rows[3] = swap(picked)
    far_down = down(late_half)
    second_up = up(scatter_second(up_rest, first_up))
    second_down = down(scatter_second(down_rest, first_down))
    picked = pick(2, jnp.concatenate([far_up, far_down], axis=0))
    second_up, second_down, picked, cotangent_rows[3], frees = after(
        (second_up, second_down, picked, cotangent_rows[3], frees)
    )

    free_up, free_down = up(frees[0]), down(frees[1])
    cotangent_rows[2] = swap(picked)
    gate_weight, up_weight, down_weight = gate_proj[0], up_proj[0], down_proj[0]
    hidden = inputs.astype(f32) + scatter_own(own_share, second_up, second_down, free_up, free_down)
    inverse_hidden = inverse_rms(hidden)
    routed = (hidden * inverse_hidden * moe_gain).astype(bf16)
    own_rows = after(pick(0, routed), cotangent_rows[2])

    acted_rows, gate_grads, up_grads, row_grads, returned, gate_dots = [], [], [], [], [], []

    def run_expert(step, rows):
        results = expert_block(rows, cotangent_rows[step], gate_weight, up_weight, down_weight)
        for held, result in zip((acted_rows, gate_grads, up_grads, row_grads, returned), results):
            held.append(result)
        gate_dots.append(results[5].reshape(peers, capacity))

    def block_mat(step):
        block_gates = gates_of(chosen_in(ids_blocks[step], all_experts), routed_blocks[step])
        return weighted_mat(step, block_gates)

    routed_blocks, arrived, weighted_mats = [routed], [], {}
    rows, next_rows = own_rows, None
    slot_parts = {}
    for step in range(columns):
        rows = swap(rows)
        coming = None
        if step < columns - 1:
            coming = up(routed_blocks[step])
            next_rows = pick(step + 1, coming)
        if step:
            run_expert(step - 1, arrived[step - 1])
        if step == 0:
            gates = gates_of(chosen_all, routed)
            gate_slots = jnp.sum(jnp.where(slots_all, gates[:, None, :], 0.0), axis=2)
            gate_slots = jnp.take(gate_slots.reshape(peers, columns, capacity), to_ring, axis=1)
            weighted_mats[0] = weighted_mat(0, gates)
            slot_parts = exchange_plane(gate_slots, early_steps)
        elif step == 1:
            slot_parts.update(exchange_plane(gate_slots, late_steps))
        elif step == 2:
            gate_slots = exchange_columns(joined(slot_parts))
            slot_parts = {}
        state = (rows, next_rows, coming, gate_slots, weighted_mats, slot_parts)
        rows, next_rows, coming, gate_slots, weighted_mats, slot_parts = after(state, row_grads)
        arrived.append(rows)
        routed_blocks.append(coming)
        rows = next_rows
    row_weights = [gate_slots[:, step].reshape(peers * capacity, 1) for step in range(columns)]

    row_grads = after(row_grads, arrived[3])
    grad_back = {1: swap(row_grads[1])}
    run_expert(3, arrived[3])
    weighted_mats[1] = block_mat(1)
    grad_back[1], row_grads, gate_dots, weighted_mats = after(
        (grad_back[1], row_grads, gate_dots, weighted_mats)
    )
    grad_back[2] = swap(row_grads[2])
    running = up(collect(grad_back, 1))
    dots = jnp.stack(gate_dots, axis=1)
    dot_parts = exchange_plane(dots, early_steps)
    weighted_mats[2] = block_mat(2)
    running, grad_back[2], dot_parts, weighted_mats = after(
        (running, grad_back[2], dot_parts, weighted_mats)
    )
    grad_back[3] = swap(after(row_grads[3], running))
    running = up(collect(grad_back, 2, running))
    dot_parts.update(exchange_plane(after(dots, grad_back[2]), late_steps))
    weighted_mats[3] = block_mat(3)
    running, grad_back[3], dot_parts, weighted_mats = after(
        (running, grad_back[3], dot_parts, weighted_mats)
    )
    grad_back[0] = swap(after(row_grads[0], running))
    running = up(collect(grad_back, 3, running))
    dots = jnp.take(exchange_columns(joined(dot_parts)), to_ring, axis=1).reshape(experts, capacity)
    running, grad_back[0], dots = after((running, grad_back[0], dots))

    grad_gates = jnp.sum(jnp.where(slots_all, dots[:, :, None], 0.0), axis=1)
    grad_logits = (
        gates * (grad_gates - jnp.sum(gates * grad_gates, axis=0, keepdims=True))
    ).astype(bf16)
    grad_routed = collect(grad_back, 0, running, f32) + lax.dot_general(
        grad_logits, router, (((0,), (1,)), ((), ())), preferred_element_type=f32
    )
    scaled = grad_routed * moe_gain
    grad_hidden = (
        cotangent.astype(f32)
        + scaled * inverse_hidden
        - hidden * (jnp.mean(hidden * scaled, axis=-1, keepdims=True) * inverse_hidden**3)
    )
    grad_moe_gain = jnp.sum(grad_routed * hidden * inverse_hidden, axis=0)
    grad_router = dot_general_t(routed, grad_logits)

    grad_low = grad_hidden.astype(bf16)
    near_gradient = gather_near(grad_low)
    output_back = {1: swap(after(returned[1], grad_low))}
    grad_attended = {0: product(grad_low, full_out)}
    grad_gate_weight, grad_up_weight = weight_gradients(
        after(arrived, grad_low), [gate_grads, up_grads], f32, row_weights
    )
    near_gradient, grad_gate_weight, grad_attended = after(
        (near_gradient, grad_gate_weight, grad_attended)
    )

    far_gradient = gather_far(*near_gradient)
    output_back[2] = swap(after(returned[2], output_back[1], near_gradient))
    grad_attended.update({1: product(near_gradient[0], full_out), 3: product(near_gradient[1], full_out)})
    output_part = collect(output_back, 1)
    far_gradient = jnp.concatenate(after(far_gradient, output_part), axis=0)
    far_gradient, grad_attended, output_part = after((far_gradient, grad_attended, output_part))

    grad_sequence = [grad_low, near_gradient[0], far_gradient, near_gradient[1]]
    running = up(output_part)
    output_back[3] = swap(after(returned[3], output_back[2], grad_attended))
    grad_attended[2] = product(far_gradient, full_out)
    grad_attended = [grad_attended[s] for s in range(columns)]
    half = heads // 2
    arguments = (col_array, qkv, grad_attended, cosine, sine, query_gain, key_gain, levels)
    dp, exp = lax.axis_size("dp"), lax.axis_size("exp")
    tile = width // (dp * exp)

    def weight_parts(lefts, right):
        mine = lax.axis_index("exp")
        if tile % 128 == 0:
            return split_gradient(lefts, right, jnp.reshape(mine, (1,)).astype(jnp.int32), exp, dp)
        (grads,) = weight_gradients(lefts, [right], bf16)
        grads = grads.reshape(dp, exp, tile, -1).transpose(1, 0, 2, 3).reshape(exp, dp * tile, -1)
        return [
            lax.dynamic_index_in_dim(grads, lax.rem(mine + step, exp), 0, keepdims=False)
            for step in range(exp)
        ]

    def exchange_parts(parts):
        return [
            lax.ppermute(part, "exp", [(i, (i + step) % exp) for i in range(exp)]) if step else part
            for step, part in enumerate(parts)
        ]

    def sum_of(parts):
        return sum(part.astype(f32) for part in parts).astype(bf16)

    def swap_parts(sums):
        parts = sums.reshape(dp, -1, sums.shape[1])
        return lax.all_to_all(parts, "dp", 0, 0, tiled=True)

    out_parts = exchange_parts(weight_parts(grad_sequence, attended))
    first_half = attention_backward(*arguments, 0, half)
    router_sums = grad_router.reshape(1, columns, width // columns * experts)
    router_sums = jnp.take(after(router_sums, far_gradient), to_ring, axis=1)
    router_sums = exchange_columns(router_sums)
    first_half, running, out_parts, router_sums = after((first_half, running, out_parts, router_sums))
    router_sums = jnp.sum(router_sums[0], axis=0)
    out_sums = sum_of(out_parts)
    out_sums = swap_parts(after(out_sums, output_back[3]))
    output_part = collect(output_back, 2, running)
    running = up(output_part)
    *grad_qkv, grad_query_gain, grad_key_gain, _, _ = attention_backward(
        *arguments, half, heads - half, after(first_half, output_part)
    )
    grad_query_gain, grad_key_gain = grad_query_gain[0], grad_key_gain[0]

    grad_qkv, out_sums = after((grad_qkv, out_sums))
    *shares, attn_gain_sums = spread(grad_qkv, full_qkv, units)
    send_up, send_down, free_up, free_down, up_rest, down_rest, own_share = shares
    first_up, first_down = up(send_up), down(send_down)
    output_part = collect(after(output_back, attn_gain_sums), 3, running)
    (grad_down,) = weight_gradients(
        after(acted_rows, attn_gain_sums), [cotangent_rows], f32, row_weights
    )
    output_back[0] = swap(after(returned[0], out_sums))
    free_up, free_down = up(free_up), down(free_down)
    qkv_parts = weight_parts(normed, after(grad_qkv, attn_gain_sums))
    first_up, first_down, free_up, free_down, grad_down, output_part, qkv_parts, output_back[0] = after(
        (first_up, first_down, free_up, free_down, grad_down, output_part, qkv_parts, output_back[0])
    )

    second_up = up(scatter_second(up_rest, first_up))
    second_down = down(scatter_second(down_rest, first_down))
    running = up(output_part)
    reduced_out = jnp.sum(out_sums.astype(f32), axis=0)
    qkv_sums = sum_of(exchange_parts(qkv_parts))

    qkv_parts = swap_parts(after(qkv_sums, output_back[0]))
    small = jnp.concatenate([attn_gain_sums[0], grad_query_gain, grad_key_gain, grad_moe_gain])
    cuts = [0, width, width + head_size, width + 2 * head_size, 2 * (width + head_size)]
    small = jnp.concatenate([small, router_sums])
    small = swap(after(jnp.broadcast_to(small, (peers, small.shape[0])), qkv_parts))
    reduced_qkv = jnp.sum(qkv_parts.astype(f32), axis=0)
    outputs = (hidden + collect(output_back, 0, running, f32)).astype(bf16)
    small = jnp.sum(small, axis=0)
    small = jnp.stack([small, *[shifted(small, step) for step in range(1, columns)]])
    to_true = lax.rem(col - jnp.arange(columns, dtype=jnp.int32) + columns, columns)
    grad_router = jnp.take(small[:, cuts[-1] :], to_true, axis=0).reshape(width, experts)
    small = jnp.sum(small[:, : cuts[-1]], axis=0)
    shared = [small[i:j] for i, j in zip(cuts, cuts[1:])]

    grad_normed = scatter_own(own_share, second_up, second_down, free_up, free_down)
    input_rows = inputs.astype(f32)
    inverse_own = inverse_rms(input_rows)
    scaled_in = grad_normed * attn_gain
    grad_inputs = (
        grad_hidden
        + scaled_in * inverse_own
        - input_rows * (jnp.mean(input_rows * scaled_in, axis=-1, keepdims=True) * inverse_own**3)
    ).astype(bf16)

    split = heads * head_size
    return (
        outputs,
        grad_inputs,
        shared[0],
        reduced_qkv[:, :split],
        reduced_qkv[:, split : split + head_size],
        reduced_qkv[:, split + head_size :],
        shared[1],
        shared[2],
        reduced_out,
        shared[3],
        grad_router,
        grad_gate_weight[None],
        grad_up_weight[None],
        grad_down[None],
    )


def dot_general_t(a, b):
    contract = (((0,), (1,)), ((), ()))
    return lax.dot_general(a, b, contract, preferred_element_type=f32)


def solution(mesh):
    return jax.shard_map(
        local,
        mesh=mesh,
        in_specs=(
            P(("dp", "exp", "col"), None),
            P(("dp", "exp", "col"), None),
            P(("dp", "exp")),
            P(("dp", "exp", "col"), None),
            P(),
            P("exp", "col"),
            P("exp", "col"),
            P("exp", "col"),
            P(),
            P(),
            P("exp", "col"),
            P(),
            P(),
            P(("dp", "exp", "col"), None, None),
            P(("dp", "exp", "col"), None, None),
            P(("dp", "exp", "col"), None, None),
        ),
        out_specs=(
            P(("dp", "exp", "col"), None),
            P(("dp", "exp", "col"), None),
            P(),
            P(("dp", "exp"), "col"),
            P(("dp", "exp"), "col"),
            P(("dp", "exp"), "col"),
            P(),
            P(),
            P(("dp", "exp"), "col"),
            P(),
            P(),
            P(("dp", "exp", "col"), None, None),
            P(("dp", "exp", "col"), None, None),
            P(("dp", "exp", "col"), None, None),
        ),
        check_vma=False,
    )
```

```python
import functools
import math

import jax
import jax.numpy as jnp
from jax import lax
from jax.experimental import pallas as pl
from jax.experimental.pallas import tpu as pltpu
from jax.sharding import PartitionSpec as P

epsilon = 1e-06
rotary_base = 1000000.0
plane = ("dp", "exp")
everyone = ("dp", "exp", "col")
f32 = jnp.float32
bf16 = jnp.bfloat16


def dot_nn(a, b):
    return lax.dot_general(a, b, (((1,), (0,)), ((), ())), preferred_element_type=f32)


def dot_nt(a, b):
    return lax.dot_general(a, b, (((1,), (1,)), ((), ())), preferred_element_type=f32)


def dot_tn(a, b):
    return lax.dot_general(a, b, (((0,), (0,)), ((), ())), preferred_element_type=f32)


def inverse_rms(rows):
    return lax.rsqrt(jnp.mean(rows * rows, axis=-1, keepdims=True) + epsilon)


def rotary_tables(positions, head_size):
    halves = head_size // 2
    frequency = rotary_base ** (-2.0 * jnp.arange(halves, dtype=f32) / head_size)
    angles = positions.astype(f32)[:, None] * frequency[None, :]
    cosine, sine = jnp.cos(angles), jnp.sin(angles)
    return (
        jnp.concatenate([cosine, cosine], axis=1),
        jnp.concatenate([-sine, sine], axis=1),
    )


def turn(rows, cosine, sine):
    return rows * cosine + pltpu.roll(rows, rows.shape[-1] // 2, 1) * sine


def turn_back(rows, cosine, sine):
    return rows * cosine - pltpu.roll(rows, rows.shape[-1] // 2, 1) * sine


def place_of(col_ref, blocks, tokens, step):
    return pl.multiple_of(lax.rem(col_ref[0] - step + blocks, blocks) * tokens, tokens)


def in_order(col_ref, refs, held):
    tokens = refs[0].shape[0]
    for step, ref in enumerate(refs):
        held[pl.ds(place_of(col_ref, len(refs), tokens, step), tokens), :] = ref[...].astype(held.dtype)


def out_of_order(col_ref, held, refs):
    tokens = refs[0].shape[0]
    for step, ref in enumerate(refs):
        ref[...] = held[pl.ds(place_of(col_ref, len(refs), tokens, step), tokens), :].astype(ref.dtype)


def scores_of(keys, query, first, scale):
    count = query.shape[0]
    scores = dot_nt(keys[pl.ds(0, first + count), :], query) * (scale * math.log2(math.e))
    row = lax.broadcasted_iota(jnp.int32, (count, count), 0)
    column = lax.broadcasted_iota(jnp.int32, (count, count), 1)
    last = jnp.where(row <= column, scores[first:], -1e30)
    return jnp.concatenate([scores[:first], last], axis=0) if first else last


def prepare_keys(col_ref, k_refs, v_refs, cos_ref, sin_ref, kg_ref, raw_rows, keys, values):
    in_order(col_ref, k_refs, raw_rows)
    in_order(col_ref, v_refs, values)
    tokens = k_refs[0].shape[0]
    for block in range(len(k_refs)):
        there = pl.ds(block * tokens, tokens)
        raw = raw_rows[there, :]
        rows = raw * inverse_rms(raw) * kg_ref[...]
        keys[there, :] = turn(rows, cos_ref[there, :], sin_ref[there, :]).astype(bf16)


def forward_kernel(blocks, scale, col_ref, *refs):
    q_refs, k_refs, v_refs = refs[:blocks], refs[blocks : 2 * blocks], refs[2 * blocks : 3 * blocks]
    cos_ref, sin_ref, qg_ref, kg_ref = refs[3 * blocks : 3 * blocks + 4]
    out_refs = refs[3 * blocks + 4 : 4 * blocks + 4]
    level_ref, raw_rows, keys, values, mixed_rows = refs[4 * blocks + 4 :]
    tokens = q_refs[0].shape[0]

    @pl.when(pl.program_id(0) == 0)
    def _():
        prepare_keys(col_ref, k_refs, v_refs, cos_ref, sin_ref, kg_ref, raw_rows, keys, values)

    in_order(col_ref, q_refs, raw_rows)
    for block in range(blocks):
        first = block * tokens
        there = pl.ds(first, tokens)
        raw = raw_rows[there, :]
        rows = raw * inverse_rms(raw) * qg_ref[...]
        query = turn(rows, cos_ref[there, :], sin_ref[there, :]).astype(bf16)
        scores = scores_of(keys, query, first, scale)
        peak = jnp.max(scores, axis=0, keepdims=True)
        probs = jnp.exp2(scores - peak)
        total = jnp.sum(probs, axis=0, keepdims=True)
        level_ref[0, :, there] = peak + jnp.log2(total)
        probs = (probs * (1.0 / total)).astype(bf16)
        mixed_rows[there, :] = dot_tn(probs, values[pl.ds(0, first + tokens), :]).astype(bf16)
    out_of_order(col_ref, mixed_rows, out_refs)


def attention_forward(col, qkv, cosine, sine, query_gain, key_gain, heads):
    blocks, tokens, head_size = len(qkv), qkv[0].shape[0], query_gain.shape[-1]
    seq_len = blocks * tokens
    column = lambda index: [pl.BlockSpec((tokens, head_size), index)] * blocks
    whole = pl.BlockSpec((seq_len, head_size), lambda h, c: (0, 0))
    gain = pl.BlockSpec((1, head_size), lambda h, c: (0, 0))
    return pl.pallas_call(
        functools.partial(forward_kernel, blocks, head_size ** (-0.5)),
        out_shape=[
            *[jax.ShapeDtypeStruct((tokens, heads * head_size), bf16)] * blocks,
            jax.ShapeDtypeStruct((heads, 1, seq_len), f32),
        ],
        grid_spec=pltpu.PrefetchScalarGridSpec(
            num_scalar_prefetch=1,
            grid=(heads,),
            in_specs=[
                *column(lambda h, c: (0, h)),
                *column(lambda h, c: (0, heads)),
                *column(lambda h, c: (0, heads + 1)),
                whole,
                whole,
                gain,
                gain,
            ],
            out_specs=[
                *column(lambda h, c: (0, h)),
                pl.BlockSpec((1, 1, seq_len), lambda h, c: (h, 0, 0)),
            ],
            scratch_shapes=[
                pltpu.VMEM((seq_len, head_size), f32),
                pltpu.VMEM((seq_len, head_size), bf16),
                pltpu.VMEM((seq_len, head_size), bf16),
                pltpu.VMEM((seq_len, head_size), bf16),
            ],
        ),
        compiler_params=pltpu.CompilerParams(vmem_limit_bytes=60 * 2**20),
        cost_estimate=pl.CostEstimate(flops=1000, bytes_accessed=1000, transcendentals=0),
        name="attention_forward",
    )(col, *qkv, *qkv, *qkv, cosine, sine, query_gain, key_gain)


def backward_kernel(blocks, scale, first_head, heads, final, col_ref, *refs):
    q_refs, k_refs, v_refs, g_refs = (refs[i * blocks : (i + 1) * blocks] for i in range(4))
    cos_ref, sin_ref, qg_ref, kg_ref, level_ref = refs[4 * blocks : 4 * blocks + 5]
    refs = refs[4 * blocks + 5 :]
    if first_head:
        refs = refs[blocks:]
        held_refs, refs = refs[:4], refs[4:]
    grad_refs, refs = refs[:blocks], refs[blocks:]
    qgain_ref, kgain_ref, out_keys, out_values = refs[:4]
    raw_rows, mixed_rows, keys, values, grad_rows, grad_keys, grad_values = refs[4:]
    tokens = q_refs[0].shape[0]
    step = pl.program_id(0)

    @pl.when(step == 0)
    def _():
        prepare_keys(col_ref, k_refs, v_refs, cos_ref, sin_ref, kg_ref, raw_rows, keys, values)
        if first_head:
            qgain_ref[...] = held_refs[0][...]
            kgain_ref[...] = held_refs[1][...]
            grad_keys[...] = held_refs[2][...]
            grad_values[...] = held_refs[3][...]
        else:
            grad_keys[...] = jnp.zeros_like(grad_keys)
            grad_values[...] = jnp.zeros_like(grad_values)
            qgain_ref[...] = jnp.zeros_like(qgain_ref)
            kgain_ref[...] = jnp.zeros_like(kgain_ref)

    def through_norm(grad_rot, unit, inverse, there, gain_ref, gain_grad_ref):
        grad_scaled = turn_back(grad_rot, cos_ref[there, :], sin_ref[there, :])
        gain_grad_ref[0:1, :] += jnp.sum(grad_scaled * unit, axis=0, keepdims=True)
        grad_unit = grad_scaled * gain_ref[...]
        return inverse * (grad_unit - unit * jnp.mean(grad_unit * unit, axis=1, keepdims=True))

    @pl.when(step < heads)
    def _():
        in_order(col_ref, q_refs, raw_rows)
        in_order(col_ref, g_refs, mixed_rows)
        for block in range(blocks):
            first = block * tokens
            there = pl.ds(first, tokens)
            raw = raw_rows[there, :]
            inverse = inverse_rms(raw)
            unit = raw * inverse
            query = turn(unit * qg_ref[...], cos_ref[there, :], sin_ref[there, :]).astype(bf16)
            grad_mixed = mixed_rows[there, :]
            upto = pl.ds(0, first + tokens)
            probs = jnp.exp2(scores_of(keys, query, first, scale) - level_ref[0, :, there])
            grad_probs = dot_nt(values[upto, :], grad_mixed)
            inner = jnp.sum(probs * grad_probs, axis=0, keepdims=True)
            grad_scores = (probs * (grad_probs - inner)).astype(bf16)
            grad_values[upto, :] += dot_nn(probs.astype(bf16), grad_mixed)
            grad_keys[upto, :] += dot_nn(grad_scores, query)
            grad_query = dot_tn(grad_scores, keys[upto, :])
            grad_rows[there, :] = through_norm(
                grad_query * scale, unit, inverse, there, qg_ref, qgain_ref
            ).astype(bf16)

    if not final:

        @pl.when(step == heads - 1)
        def _():
            out_keys[...] = grad_keys[...]
            out_values[...] = grad_values[...]

    @pl.when(step == heads)
    def _():
        in_order(col_ref, k_refs, raw_rows)
        for block in range(blocks):
            there = pl.ds(block * tokens, tokens)
            raw = raw_rows[there, :]
            inverse = inverse_rms(raw)
            grad_rows[there, :] = through_norm(
                grad_keys[there, :] * scale, raw * inverse, inverse, there, kg_ref, kgain_ref
            ).astype(bf16)

    @pl.when(step == heads + 1)
    def _():
        grad_rows[...] = grad_values[...].astype(bf16)

    out_of_order(col_ref, grad_rows, grad_refs)


def attention_backward(
    col, qkv, grad_attended, cosine, sine, query_gain, key_gain, levels, first, heads, former=None
):
    blocks, tokens, head_size = len(qkv), qkv[0].shape[0], query_gain.shape[-1]
    seq_len = blocks * tokens
    all_heads = levels.shape[0]
    final = first + heads == all_heads
    column = lambda index: [pl.BlockSpec((tokens, head_size), index)] * blocks
    whole = pl.BlockSpec((seq_len, head_size), lambda h, c: (0, 0))
    gain = pl.BlockSpec((1, head_size), lambda h, c: (0, 0))
    gain_out = pl.BlockSpec((8, head_size), lambda h, c: (0, 0))
    last = all_heads - 1
    held = [] if former is None else former
    return pl.pallas_call(
        functools.partial(backward_kernel, blocks, head_size ** (-0.5), first, heads, final),
        out_shape=[
            *[jax.ShapeDtypeStruct(qkv[0].shape, bf16)] * blocks,
            jax.ShapeDtypeStruct((8, head_size), f32),
            jax.ShapeDtypeStruct((8, head_size), f32),
            jax.ShapeDtypeStruct((seq_len, head_size), f32),
            jax.ShapeDtypeStruct((seq_len, head_size), f32),
        ],
        grid_spec=pltpu.PrefetchScalarGridSpec(
            num_scalar_prefetch=1,
            grid=(heads + 2 if final else heads,),
            in_specs=[
                *column(lambda h, c: (0, jnp.minimum(h + first, last))),
                *column(lambda h, c: (0, all_heads)),
                *column(lambda h, c: (0, all_heads + 1)),
                *column(lambda h, c: (0, jnp.minimum(h + first, last))),
                whole,
                whole,
                gain,
                gain,
                pl.BlockSpec((1, 1, seq_len), lambda h, c: (jnp.minimum(h + first, last), 0, 0)),
                *([] if former is None else [pl.BlockSpec(memory_space=pl.ANY)] * blocks),
                *([] if former is None else [gain_out, gain_out, whole, whole]),
            ],
            out_specs=[*column(lambda h, c: (0, h + first)), gain_out, gain_out, whole, whole],
            scratch_shapes=[
                pltpu.VMEM((seq_len, head_size), f32),
                pltpu.VMEM((seq_len, head_size), bf16),
                pltpu.VMEM((seq_len, head_size), bf16),
                pltpu.VMEM((seq_len, head_size), bf16),
                pltpu.VMEM((seq_len, head_size), bf16),
                pltpu.VMEM((seq_len, head_size), f32),
                pltpu.VMEM((seq_len, head_size), f32),
            ],
        ),
        input_output_aliases={} if former is None else {1 + 4 * blocks + 5 + i: i for i in range(blocks)},
        compiler_params=pltpu.CompilerParams(vmem_limit_bytes=60 * 2**20),
        cost_estimate=pl.CostEstimate(flops=1000, bytes_accessed=1000, transcendentals=0),
        name="attention_backward",
    )(col, *qkv, *qkv, *qkv, *grad_attended, cosine, sine, query_gain, key_gain, levels, *held)


def weight_kernel(blocks, rights, weighted, *refs):
    left_refs, refs = refs[:blocks], refs[blocks:]
    right_refs, refs = refs[: blocks * rights], refs[blocks * rights :]
    if weighted:
        weight_refs, refs = refs[:blocks], refs[blocks:]
        out_refs, held = refs[:rights], refs[rights:]

        @pl.when(pl.program_id(0) == 0)
        def _():
            for index, ref in enumerate(right_refs):
                scaled = ref[...].astype(f32) * weight_refs[index % blocks][...]
                held[index][...] = scaled.astype(bf16)

        right_refs = held
    else:
        out_refs = refs
    for index, out_ref in enumerate(out_refs):
        total = dot_tn(left_refs[0][...], right_refs[index * blocks][...])
        for block in range(1, blocks):
            total = total + dot_tn(left_refs[block][...], right_refs[index * blocks + block][...])
        out_ref[...] = total.astype(out_ref.dtype)


def weight_gradients(lefts, rights, out_type, weights=None, tile=256):
    blocks, rows, tall = len(lefts), lefts[0].shape[0], lefts[0].shape[1]
    flat = [block for right in rights for block in right]
    fixed = lambda array: pl.BlockSpec(array.shape, lambda i: (0, 0))
    return pl.pallas_call(
        functools.partial(weight_kernel, blocks, len(rights), weights is not None),
        out_shape=[jax.ShapeDtypeStruct((tall, right[0].shape[1]), out_type) for right in rights],
        grid=(tall // tile,),
        in_specs=[
            *[pl.BlockSpec((rows, tile), lambda i: (0, i))] * blocks,
            *[fixed(block) for block in flat],
            *([] if weights is None else [fixed(weight) for weight in weights]),
        ],
        out_specs=[
            pl.BlockSpec((tile, right[0].shape[1]), lambda i: (i, 0)) for right in rights
        ],
        scratch_shapes=[] if weights is None else [pltpu.VMEM(block.shape, bf16) for block in flat],
        compiler_params=pltpu.CompilerParams(vmem_limit_bytes=60 * 2**20),
        cost_estimate=pl.CostEstimate(flops=1000, bytes_accessed=1000, transcendentals=0),
        name="weight_gradients",
    )(*lefts, *flat, *([] if weights is None else weights))


def split_kernel(blocks, groups, mine_ref, *refs):
    left_refs, right_refs, out_refs = refs[:blocks], refs[blocks : 2 * blocks], refs[2 * blocks :]
    total = dot_tn(left_refs[0][...], right_refs[0][...])
    for block in range(1, blocks):
        total = total + dot_tn(left_refs[block][...], right_refs[block][...])
    for index, out_ref in enumerate(out_refs):

        @pl.when(pl.program_id(0) // groups == index)
        def _():
            out_ref[...] = total.astype(out_ref.dtype)


def split_gradient(lefts, right, mine, devices, groups):
    blocks, rows, tall = len(lefts), lefts[0].shape[0], lefts[0].shape[1]
    tile, wide = tall // (devices * groups), right[0].shape[1]

    def left_tile(i, mine_ref):
        return (0, i % groups * devices + lax.rem(mine_ref[0] + i // groups, devices))

    def out_tile(index):
        return lambda i, mine_ref: (jnp.clip(i - index * groups, 0, groups - 1), 0)

    return pl.pallas_call(
        functools.partial(split_kernel, blocks, groups),
        out_shape=[jax.ShapeDtypeStruct((groups * tile, wide), bf16)] * devices,
        grid_spec=pltpu.PrefetchScalarGridSpec(
            num_scalar_prefetch=1,
            grid=(devices * groups,),
            in_specs=[
                *[pl.BlockSpec((rows, tile), left_tile)] * blocks,
                *[pl.BlockSpec((rows, wide), lambda i, mine_ref: (0, 0))] * blocks,
            ],
            out_specs=[pl.BlockSpec((tile, wide), out_tile(index)) for index in range(devices)],
        ),
        compiler_params=pltpu.CompilerParams(vmem_limit_bytes=60 * 2**20),
        cost_estimate=pl.CostEstimate(flops=1000, bytes_accessed=1000, transcendentals=0),
        name="split_gradient",
    )(mine, *lefts, *right)


def spread_kernel(with_units, *refs):
    block_refs, weight_ref, refs = refs[:4], refs[4], refs[5:]
    if with_units:
        unit_refs, refs = refs[:4], refs[4:]
    far_up, far_down, free_up, free_down, up_rest, down_rest, own_ref = refs[:7]
    weight = weight_ref[...]
    middle = own_ref.shape[0] // 2
    shares = {}
    for step in (2, 3, 1, 0):
        shares[step] = dot_nt(block_refs[step][...], weight)
    far_up[...] = shares[2][:middle].astype(bf16)
    far_down[...] = shares[2][middle:].astype(bf16)
    free_up[...] = shares[3][middle:].astype(bf16)
    free_down[...] = shares[1][:middle].astype(bf16)
    up_rest[...] = shares[3][:middle]
    down_rest[...] = shares[1][middle:]
    own_ref[...] = shares[0]
    if with_units:
        total = sum(
            jnp.sum(shares[step] * unit_refs[step][...], axis=0, keepdims=True) for step in range(4)
        )
        refs[7][...] = jnp.broadcast_to(total, refs[7].shape)


def spread(blocks, weight, units=None, tile=512):
    tokens, depth = blocks[0].shape
    width = weight.shape[0]
    part = lambda rows: pl.BlockSpec((rows, tile), lambda i: (0, i))
    shape = jax.ShapeDtypeStruct
    return pl.pallas_call(
        functools.partial(spread_kernel, units is not None),
        out_shape=[
            *[shape((tokens // 2, width), bf16)] * 4,
            *[shape((tokens // 2, width), f32)] * 2,
            shape((tokens, width), f32),
            *([] if units is None else [shape((8, width), f32)]),
        ],
        grid=(width // tile,),
        in_specs=[
            *[pl.BlockSpec((tokens, depth), lambda i: (0, 0))] * 4,
            pl.BlockSpec((tile, depth), lambda i: (i, 0)),
            *([] if units is None else [part(tokens)] * 4),
        ],
        out_specs=[
            *[part(tokens // 2)] * 6,
            part(tokens),
            *([] if units is None else [part(8)]),
        ],
        compiler_params=pltpu.CompilerParams(vmem_limit_bytes=60 * 2**20),
        cost_estimate=pl.CostEstimate(flops=1000, bytes_accessed=1000, transcendentals=0),
        name="spread",
    )(*blocks, weight, *([] if units is None else units))


def product_kernel(transposed, left_ref, right_ref, *refs):
    result = (dot_tn if transposed else dot_nn)(left_ref[...], right_ref[...])
    if len(refs) > 1:
        result = result + refs[0][...].astype(f32)
    refs[-1][...] = result.astype(refs[-1].dtype)


def product(left, right, addend=None, out_type=bf16, transposed=False, tile=512):
    rows = left.shape[1 if transposed else 0]
    part = lambda height: pl.BlockSpec((height, tile), lambda i: (0, i))
    return pl.pallas_call(
        functools.partial(product_kernel, transposed),
        out_shape=jax.ShapeDtypeStruct((rows, right.shape[1]), out_type),
        grid=(right.shape[1] // tile,),
        in_specs=[
            pl.BlockSpec(left.shape, lambda i: (0, 0)),
            part(right.shape[0]),
            *([] if addend is None else [part(rows)]),
        ],
        out_specs=part(rows),
        compiler_params=pltpu.CompilerParams(vmem_limit_bytes=60 * 2**20),
        cost_estimate=pl.CostEstimate(flops=1000, bytes_accessed=1000, transcendentals=0),
        name="product",
    )(left, right, *([] if addend is None else [addend]))


def expert_kernel(
    rows_ref, upstream_ref, gate_ref, up_ref, down_ref,
    acted_ref, gate_grad_ref, up_grad_ref, row_grad_ref, returned_ref, dots_ref,
    gates, ups, downs, gate_grads, up_grads, acted_rows,
):
    step = pl.program_id(0)
    tile = gate_ref.shape[1]
    gate_part = dot_nn(rows_ref[...], gate_ref[...])
    up_part = dot_nn(rows_ref[...], up_ref[...])
    drive = dot_nt(upstream_ref[...], down_ref[...])
    sigmoid = jax.nn.sigmoid(gate_part)
    silu = gate_part * sigmoid
    acted = silu * up_part
    acted_low = acted.astype(bf16)
    gate_grad = (drive * up_part * sigmoid * (1.0 + gate_part * (1.0 - sigmoid))).astype(bf16)
    up_grad = (drive * silu).astype(bf16)
    acted_ref[...] = acted_low
    gate_grad_ref[...] = gate_grad
    up_grad_ref[...] = up_grad
    dots = jnp.sum(acted * drive, axis=1, keepdims=True)
    for index in range(gates.shape[1] // tile):

        @pl.when(step == index)
        def _():
            here = pl.ds(index * tile, tile)
            gates[:, here] = gate_ref[...]
            ups[:, here] = up_ref[...]
            downs[here, :] = down_ref[...]
            gate_grads[:, here] = gate_grad
            up_grads[:, here] = up_grad
            acted_rows[:, here] = acted_low

    @pl.when(step == 0)
    def _():
        dots_ref[...] = dots

    @pl.when(step > 0)
    def _():
        dots_ref[...] += dots

    @pl.when(step == pl.num_programs(0) - 1)
    def _():
        for first in range(0, row_grad_ref.shape[1], 512):
            here = pl.ds(first, 512)
            row_grad_ref[:, here] = (
                dot_nt(gate_grads[...], gates[here, :]) + dot_nt(up_grads[...], ups[here, :])
            ).astype(bf16)
            returned_ref[:, here] = dot_nn(acted_rows[...], downs[:, here]).astype(bf16)


def expert_block(rows, upstream_rows, gate_weight, up_weight, down_weight, tile=256):
    count, width = rows.shape
    hidden = gate_weight.shape[1]
    shape = jax.ShapeDtypeStruct
    whole = pl.BlockSpec((count, width), lambda j: (0, 0))
    part = pl.BlockSpec((count, tile), lambda j: (0, j))
    return pl.pallas_call(
        expert_kernel,
        out_shape=[
            shape((count, hidden), bf16),
            shape((count, hidden), bf16),
            shape((count, hidden), bf16),
            shape((count, width), bf16),
            shape((count, width), bf16),
            shape((count, 1), f32),
        ],
        grid=(hidden // tile,),
        in_specs=[
            whole,
            whole,
            pl.BlockSpec((width, tile), lambda j: (0, j)),
            pl.BlockSpec((width, tile), lambda j: (0, j)),
            pl.BlockSpec((tile, width), lambda j: (j, 0)),
        ],
        out_specs=[part, part, part, whole, whole, pl.BlockSpec((count, 1), lambda j: (0, 0))],
        scratch_shapes=[
            pltpu.VMEM((width, hidden), bf16),
            pltpu.VMEM((width, hidden), bf16),
            pltpu.VMEM((hidden, width), bf16),
            pltpu.VMEM((count, hidden), bf16),
            pltpu.VMEM((count, hidden), bf16),
            pltpu.VMEM((count, hidden), bf16),
        ],
        compiler_params=pltpu.CompilerParams(vmem_limit_bytes=60 * 2**20),
        cost_estimate=pl.CostEstimate(flops=1000, bytes_accessed=1000, transcendentals=0),
        name="expert_block",
    )(rows, upstream_rows, gate_weight, up_weight, down_weight)


def local(
    inputs,
    expert_ids,
    positions,
    cotangent,
    attn_gain,
    query_proj,
    key_projection,
    value_projection,
    query_norm_gain,
    key_norm_gain,
    out_proj,
    moe_gain,
    router,
    gate_proj,
    up_proj,
    down_proj,
):
    tokens, width = inputs.shape
    head_size = query_norm_gain.shape[0]
    choices = expert_ids.shape[1]
    experts = router.shape[1]
    capacity = tokens * choices * 5 // (4 * experts)
    columns = lax.axis_size("col")
    peers = lax.axis_size("dp") * lax.axis_size("exp")
    col = lax.axis_index("col")
    here = lax.axis_index("dp") * lax.axis_size("exp") + lax.axis_index("exp")
    col_array = jnp.reshape(col, (1,)).astype(jnp.int32)
    heads = query_proj.shape[1] // head_size
    assert key_projection.shape[1] == head_size and experts == peers * columns
    assert columns == 4 and tokens % 32 == 0
    middle = tokens // 2

    def shifted(block, by):
        return lax.ppermute(block, "col", [(i, (i + by) % columns) for i in range(columns)])

    def up(block):
        return shifted(block, 1)

    def down(block):
        return shifted(block, -1)

    def gather_near(block):
        return up(block), down(block)

    def gather_far(former, latter):
        return up(former[:middle]), down(latter[middle:])

    def scatter_second(rest, far):
        return (rest + far.astype(f32)).astype(bf16)

    def scatter_own(own, second_up, second_down, free_up, free_down):
        return own + jnp.concatenate(
            [
                second_up.astype(f32) + free_down.astype(f32),
                free_up.astype(f32) + second_down.astype(f32),
            ],
            axis=0,
        )

    def swap(rows):
        return lax.all_to_all(
            rows.reshape(peers, rows.shape[0] // peers, *rows.shape[1:]), plane, 0, 0, tiled=True
        ).reshape(rows.shape)

    def swap_all(values):
        return lax.all_to_all(values, everyone, 0, 0, tiled=True)

    def after(value, *others):
        return lax.optimization_barrier((value, others))[0]

    def exchange_plane(values, steps):
        parts = {}
        for step in steps:
            part = lax.dynamic_index_in_dim(values, lax.rem(here + step, peers), 0, keepdims=False)
            pairs = [(i, (i + step) % peers) for i in range(peers)]
            parts[step] = lax.ppermute(part, plane, pairs) if step else part
        return parts

    def joined(parts):
        order = lax.rem(here - jnp.arange(peers, dtype=jnp.int32) + peers, peers)
        return jnp.take(jnp.stack([parts[step] for step in range(peers)]), order, axis=0)

    early_steps, late_steps = range(peers // 2), range(peers // 2, peers)

    def exchange_columns(values):
        parts = [values[:, 0], *[shifted(values[:, s], -s) for s in range(1, columns)]]
        return jnp.stack([parts[0], *parts[:0:-1]], axis=1)

    to_ring = lax.rem(col - jnp.arange(columns, dtype=jnp.int32) + columns, columns)

    earlier = (
        lax.broadcasted_iota(jnp.int32, (tokens, tokens), 0)
        < lax.broadcasted_iota(jnp.int32, (tokens, tokens), 1)
    ).astype(bf16)
    all_experts = jnp.arange(experts, dtype=jnp.int32)
    plane_experts = jnp.arange(peers, dtype=jnp.int32) * columns + col

    def chosen_in(ids, named):
        return jnp.any(ids[None, :, :] == named[:, None, None], axis=1)

    def slots_of(ids, named):
        chosen = chosen_in(ids, named)
        rank = dot_nn(chosen.astype(bf16), earlier)
        code = jnp.where(chosen, rank, -1.0)
        place = lax.broadcasted_iota(jnp.int32, (1, capacity, 1), 1).astype(f32)
        return chosen, code[:, None, :] == place

    def slot_mat(ids):
        return slots_of(ids, plane_experts)[1].astype(bf16).reshape(peers * capacity, tokens)

    def pick(step, block):
        return product(slot_mats[step], block)

    def gates_of(chosen, block):
        logits = jnp.where(chosen, dot_general_t(router, block), -1e30)
        exponent = jnp.exp(logits - jnp.max(logits, axis=0, keepdims=True))
        exponent = jnp.where(chosen, exponent, 0.0)
        return exponent / jnp.sum(exponent, axis=0, keepdims=True)

    def weighted_mat(step, block_gates):
        gates_here = block_gates.reshape(peers, columns, 1, tokens)
        gates_here = lax.dynamic_index_in_dim(gates_here, col, 1, keepdims=False)
        mat = slot_mats[step].reshape(peers, capacity, tokens) * gates_here
        return mat.astype(bf16).reshape(peers * capacity, tokens)

    def collect(back, step, addend=None, out_type=bf16):
        return product(weighted_mats[step], back[step], addend, out_type, transposed=True)

    near_inputs = gather_near(inputs)
    local_qkv = jnp.concatenate([query_proj, key_projection, value_projection], axis=1)
    full_qkv = lax.all_gather(local_qkv, "exp", axis=0, tiled=True)
    full_out = lax.all_gather(out_proj, "exp", axis=0, tiled=True)
    own_ids = expert_ids.T
    slot_mats = [slot_mat(own_ids)]
    cotangent_rows = [swap(pick(0, cotangent)), None, None, None]
    near_inputs, full_qkv = after((near_inputs, full_qkv))

    far_inputs = jnp.concatenate(gather_far(*near_inputs), axis=0)
    def project(block):
        rows = block.astype(f32)
        unit = rows * inverse_rms(rows)
        low = (unit * attn_gain).astype(bf16)
        return unit, low, dot_nn(low, full_qkv)

    projected = [project(inputs), project(near_inputs[0]), None, project(near_inputs[1])]
    cosine, sine = rotary_tables(positions, head_size)
    far_inputs, cotangent_rows[0], cosine, sine = after(
        (far_inputs, cotangent_rows[0], cosine, sine),
        [projected[s][2] for s in (0, 1, 3)],
    )

    near_cotangent = gather_near(after(cotangent, far_inputs))
    later_ids = after(own_ids, far_inputs)
    ids_blocks = [own_ids, *[shifted(later_ids, step) for step in range(1, columns)]]
    projected[2] = project(far_inputs)
    units, normed, qkv = zip(*projected)
    query_gain, key_gain = query_norm_gain[None, :], key_norm_gain[None, :]
    *attended, levels = attention_forward(col_array, qkv, cosine, sine, query_gain, key_gain, heads)
    shares = spread(attended, full_out)
    ids_blocks = after(ids_blocks, attended)
    slot_mats += [slot_mat(ids_blocks[s]) for s in (1, 2, 3)]
    picked = pick(1, after(near_cotangent[0], attended))
    near_cotangent, shares, slot_mats, picked = after((near_cotangent, shares, slot_mats, picked))

    send_up, send_down, free_up, free_down, up_rest, down_rest, own_share = shares
    cotangent_rows[1] = swap(picked)
    first_up, first_down = up(send_up), down(send_down)
    far_up = up(near_cotangent[0][:middle])
    chosen_all, slots_all = slots_of(own_ids, all_experts)
    picked = pick(3, near_cotangent[1])
    late_half = near_cotangent[1][middle:]
    first_up, first_down, far_up, cotangent_rows[1], chosen_all, slots_all, picked, late_half, frees = after(
        (
            first_up, first_down, far_up, cotangent_rows[1], chosen_all, slots_all, picked, late_half,
            (free_up, free_down),
        )
    )
    cotangent_rows[3] = swap(picked)
    far_down = down(late_half)
    second_up = up(scatter_second(up_rest, first_up))
    second_down = down(scatter_second(down_rest, first_down))
    picked = pick(2, jnp.concatenate([far_up, far_down], axis=0))
    second_up, second_down, picked, cotangent_rows[3], frees = after(
        (second_up, second_down, picked, cotangent_rows[3], frees)
    )

    free_up, free_down = up(frees[0]), down(frees[1])
    cotangent_rows[2] = swap(picked)
    gate_weight, up_weight, down_weight = gate_proj[0], up_proj[0], down_proj[0]
    hidden = inputs.astype(f32) + scatter_own(own_share, second_up, second_down, free_up, free_down)
    inverse_hidden = inverse_rms(hidden)
    routed = (hidden * inverse_hidden * moe_gain).astype(bf16)
    own_rows = after(pick(0, routed), cotangent_rows[2])

    acted_rows, gate_grads, up_grads, row_grads, returned, gate_dots = [], [], [], [], [], []

    def run_expert(step, rows):
        results = expert_block(rows, cotangent_rows[step], gate_weight, up_weight, down_weight)
        for held, result in zip((acted_rows, gate_grads, up_grads, row_grads, returned), results):
            held.append(result)
        gate_dots.append(results[5].reshape(peers, capacity))

    def block_mat(step):
        block_gates = gates_of(chosen_in(ids_blocks[step], all_experts), routed_blocks[step])
        return weighted_mat(step, block_gates)

    routed_blocks, arrived, weighted_mats = [routed], [], {}
    rows, next_rows = own_rows, None
    slot_parts = {}
    for step in range(columns):
        rows = swap(rows)
        coming = None
        if step < columns - 1:
            coming = up(routed_blocks[step])
            next_rows = pick(step + 1, coming)
        if step:
            run_expert(step - 1, arrived[step - 1])
        if step == 0:
            gates = gates_of(chosen_all, routed)
            gate_slots = jnp.sum(jnp.where(slots_all, gates[:, None, :], 0.0), axis=2)
            gate_slots = jnp.take(gate_slots.reshape(peers, columns, capacity), to_ring, axis=1)
            weighted_mats[0] = weighted_mat(0, gates)
            slot_parts = exchange_plane(gate_slots, early_steps)
        elif step == 1:
            slot_parts.update(exchange_plane(gate_slots, late_steps))
        elif step == 2:
            gate_slots = exchange_columns(joined(slot_parts))
            slot_parts = {}
        state = (rows, next_rows, coming, gate_slots, weighted_mats, slot_parts)
        rows, next_rows, coming, gate_slots, weighted_mats, slot_parts = after(state, row_grads)
        arrived.append(rows)
        routed_blocks.append(coming)
        rows = next_rows
    row_weights = [gate_slots[:, step].reshape(peers * capacity, 1) for step in range(columns)]

    row_grads = after(row_grads, arrived[3])
    grad_back = {1: swap(row_grads[1])}
    run_expert(3, arrived[3])
    weighted_mats[1] = block_mat(1)
    grad_back[1], row_grads, gate_dots, weighted_mats = after(
        (grad_back[1], row_grads, gate_dots, weighted_mats)
    )
    grad_back[2] = swap(row_grads[2])
    running = up(collect(grad_back, 1))
    dots = jnp.stack(gate_dots, axis=1)
    dot_parts = exchange_plane(dots, early_steps)
    weighted_mats[2] = block_mat(2)
    running, grad_back[2], dot_parts, weighted_mats = after(
        (running, grad_back[2], dot_parts, weighted_mats)
    )
    grad_back[3] = swap(after(row_grads[3], running))
    running = up(collect(grad_back, 2, running))
    dot_parts.update(exchange_plane(after(dots, grad_back[2]), late_steps))
    weighted_mats[3] = block_mat(3)
    running, grad_back[3], dot_parts, weighted_mats = after(
        (running, grad_back[3], dot_parts, weighted_mats)
    )
    grad_back[0] = swap(after(row_grads[0], running))
    running = up(collect(grad_back, 3, running))
    dots = jnp.take(exchange_columns(joined(dot_parts)), to_ring, axis=1).reshape(experts, capacity)
    running, grad_back[0], dots = after((running, grad_back[0], dots))

    grad_gates = jnp.sum(jnp.where(slots_all, dots[:, :, None], 0.0), axis=1)
    grad_logits = (
        gates * (grad_gates - jnp.sum(gates * grad_gates, axis=0, keepdims=True))
    ).astype(bf16)
    grad_routed = collect(grad_back, 0, running, f32) + lax.dot_general(
        grad_logits, router, (((0,), (1,)), ((), ())), preferred_element_type=f32
    )
    scaled = grad_routed * moe_gain
    grad_hidden = (
        cotangent.astype(f32)
        + scaled * inverse_hidden
        - hidden * (jnp.mean(hidden * scaled, axis=-1, keepdims=True) * inverse_hidden**3)
    )
    grad_moe_gain = jnp.sum(grad_routed * hidden * inverse_hidden, axis=0)
    grad_router = dot_general_t(routed, grad_logits)

    grad_low = grad_hidden.astype(bf16)
    near_gradient = gather_near(grad_low)
    output_back = {1: swap(after(returned[1], grad_back[0]))}
    grad_attended = {0: product(grad_low, full_out)}
    grad_gate_weight, grad_up_weight = weight_gradients(
        after(arrived, grad_low), [gate_grads, up_grads], f32, row_weights
    )
    near_gradient, grad_gate_weight, grad_attended = after(
        (near_gradient, grad_gate_weight, grad_attended)
    )

    far_gradient = gather_far(*near_gradient)
    output_back[2] = swap(after(returned[2], output_back[1], grad_low))
    grad_attended.update({1: product(near_gradient[0], full_out), 3: product(near_gradient[1], full_out)})
    output_part = collect(output_back, 1)
    far_gradient = jnp.concatenate(after(far_gradient, output_part), axis=0)
    router_sums = grad_router.reshape(1, columns, width // columns * experts)
    router_sums = jnp.take(after(router_sums, near_gradient), to_ring, axis=1)
    router_sums = jnp.sum(exchange_columns(router_sums)[0], axis=0)
    far_gradient, grad_attended, output_part, router_sums = after(
        (far_gradient, grad_attended, output_part, router_sums)
    )

    grad_sequence = [grad_low, near_gradient[0], far_gradient, near_gradient[1]]
    running = up(output_part)
    output_back[3] = swap(after(returned[3], output_back[2]))
    grad_attended[2] = product(far_gradient, full_out)
    grad_attended = [grad_attended[s] for s in range(columns)]
    half = heads // 2
    arguments = (col_array, qkv, grad_attended, cosine, sine, query_gain, key_gain, levels)
    dp, exp = lax.axis_size("dp"), lax.axis_size("exp")
    tile = width // (dp * exp)

    def weight_parts(lefts, right):
        mine = lax.axis_index("exp")
        if tile % 128 == 0:
            return split_gradient(lefts, right, jnp.reshape(mine, (1,)).astype(jnp.int32), exp, dp)
        (grads,) = weight_gradients(lefts, [right], bf16)
        grads = grads.reshape(dp, exp, tile, -1).transpose(1, 0, 2, 3).reshape(exp, dp * tile, -1)
        return [
            lax.dynamic_index_in_dim(grads, lax.rem(mine + step, exp), 0, keepdims=False)
            for step in range(exp)
        ]

    def exchange_parts(parts):
        return [
            lax.ppermute(part, "exp", [(i, (i + step) % exp) for i in range(exp)]) if step else part
            for step, part in enumerate(parts)
        ]

    def sum_of(parts):
        return sum(part.astype(f32) for part in parts).astype(bf16)

    def swap_parts(sums):
        parts = sums.reshape(dp, -1, sums.shape[1])
        return lax.all_to_all(parts, "dp", 0, 0, tiled=True)

    out_parts = exchange_parts(weight_parts(grad_sequence, attended))
    first_half = attention_backward(*arguments, 0, half)
    first_half, running, out_parts = after((first_half, running, out_parts))
    out_sums = sum_of(out_parts)
    out_sums = swap_parts(after(out_sums, output_back[3]))
    output_part = collect(output_back, 2, running)
    running = up(output_part)
    *grad_qkv, grad_query_gain, grad_key_gain, _, _ = attention_backward(
        *arguments, half, heads - half, after(first_half, output_part)
    )
    grad_query_gain, grad_key_gain = grad_query_gain[0], grad_key_gain[0]

    grad_qkv, out_sums = after((grad_qkv, out_sums))
    *shares, attn_gain_sums = spread(grad_qkv, full_qkv, units)
    send_up, send_down, free_up, free_down, up_rest, down_rest, own_share = shares
    first_up, first_down = up(send_up), down(send_down)
    output_part = collect(after(output_back, attn_gain_sums), 3, running)
    (grad_down,) = weight_gradients(
        after(acted_rows, attn_gain_sums), [cotangent_rows], f32, row_weights
    )
    free_up, free_down = up(free_up), down(free_down)
    qkv_parts = weight_parts(normed, after(grad_qkv, attn_gain_sums))
    small = jnp.concatenate([attn_gain_sums[0], grad_query_gain, grad_key_gain, grad_moe_gain])
    cuts = [0, width, width + head_size, width + 2 * head_size, 2 * (width + head_size)]
    small = jnp.concatenate([small, router_sums])
    small = swap(after(jnp.broadcast_to(small, (peers, small.shape[0])), out_sums))
    output_back[0] = swap(after(returned[0], small))
    first_up, first_down, free_up, free_down, grad_down, output_part, qkv_parts, small = after(
        (first_up, first_down, free_up, free_down, grad_down, output_part, qkv_parts, small)
    )

    second_up = up(scatter_second(up_rest, first_up))
    second_down = down(scatter_second(down_rest, first_down))
    running = up(output_part)
    reduced_out = jnp.sum(out_sums.astype(f32), axis=0)
    qkv_sums = sum_of(exchange_parts(qkv_parts))

    qkv_parts = swap_parts(after(qkv_sums, output_back[0]))
    reduced_qkv = jnp.sum(qkv_parts.astype(f32), axis=0)
    outputs = (hidden + collect(output_back, 0, running, f32)).astype(bf16)
    small = after(jnp.sum(small, axis=0), qkv_sums)
    small = jnp.stack([small, *[shifted(small, step) for step in range(1, columns)]])
    to_true = lax.rem(col - jnp.arange(columns, dtype=jnp.int32) + columns, columns)
    grad_router = jnp.take(small[:, cuts[-1] :], to_true, axis=0).reshape(width, experts)
    small = jnp.sum(small[:, : cuts[-1]], axis=0)
    shared = [small[i:j] for i, j in zip(cuts, cuts[1:])]

    grad_normed = scatter_own(own_share, second_up, second_down, free_up, free_down)
    input_rows = inputs.astype(f32)
    inverse_own = inverse_rms(input_rows)
    scaled_in = grad_normed * attn_gain
    grad_inputs = (
        grad_hidden
        + scaled_in * inverse_own
        - input_rows * (jnp.mean(input_rows * scaled_in, axis=-1, keepdims=True) * inverse_own**3)
    ).astype(bf16)

    split = heads * head_size
    return (
        outputs,
        grad_inputs,
        shared[0],
        reduced_qkv[:, :split],
        reduced_qkv[:, split : split + head_size],
        reduced_qkv[:, split + head_size :],
        shared[1],
        shared[2],
        reduced_out,
        shared[3],
        grad_router,
        grad_gate_weight[None],
        grad_up_weight[None],
        grad_down[None],
    )


def dot_general_t(a, b):
    contract = (((0,), (1,)), ((), ()))
    return lax.dot_general(a, b, contract, preferred_element_type=f32)


def solution(mesh):
    return jax.shard_map(
        local,
        mesh=mesh,
        in_specs=(
            P(("dp", "exp", "col"), None),
            P(("dp", "exp", "col"), None),
            P(("dp", "exp")),
            P(("dp", "exp", "col"), None),
            P(),
            P("exp", "col"),
            P("exp", "col"),
            P("exp", "col"),
            P(),
            P(),
            P("exp", "col"),
            P(),
            P(),
            P(("dp", "exp", "col"), None, None),
            P(("dp", "exp", "col"), None, None),
            P(("dp", "exp", "col"), None, None),
        ),
        out_specs=(
            P(("dp", "exp", "col"), None),
            P(("dp", "exp", "col"), None),
            P(),
            P(("dp", "exp"), "col"),
            P(("dp", "exp"), "col"),
            P(("dp", "exp"), "col"),
            P(),
            P(),
            P(("dp", "exp"), "col"),
            P(),
            P(),
            P(("dp", "exp", "col"), None, None),
            P(("dp", "exp", "col"), None, None),
            P(("dp", "exp", "col"), None, None),
        ),
        check_vma=False,
    )
```

```python
import functools
import math

import jax
import jax.numpy as jnp
from jax import lax
from jax.experimental import pallas as pl
from jax.experimental.pallas import tpu as pltpu
from jax.sharding import PartitionSpec as P

epsilon = 1e-06
rotary_base = 1000000.0
plane = ("dp", "exp")
everyone = ("dp", "exp", "col")
f32 = jnp.float32
bf16 = jnp.bfloat16


def dot_nn(a, b):
    return lax.dot_general(a, b, (((1,), (0,)), ((), ())), preferred_element_type=f32)


def dot_nt(a, b):
    return lax.dot_general(a, b, (((1,), (1,)), ((), ())), preferred_element_type=f32)


def dot_tn(a, b):
    return lax.dot_general(a, b, (((0,), (0,)), ((), ())), preferred_element_type=f32)


def inverse_rms(rows):
    return lax.rsqrt(jnp.mean(rows * rows, axis=-1, keepdims=True) + epsilon)


def rotary_tables(positions, head_size):
    halves = head_size // 2
    frequency = rotary_base ** (-2.0 * jnp.arange(halves, dtype=f32) / head_size)
    angles = positions.astype(f32)[:, None] * frequency[None, :]
    cosine, sine = jnp.cos(angles), jnp.sin(angles)
    return (
        jnp.concatenate([cosine, cosine], axis=1),
        jnp.concatenate([-sine, sine], axis=1),
    )


def turn(rows, cosine, sine):
    return rows * cosine + pltpu.roll(rows, rows.shape[-1] // 2, 1) * sine


def turn_back(rows, cosine, sine):
    return rows * cosine - pltpu.roll(rows, rows.shape[-1] // 2, 1) * sine


def place_of(col_ref, blocks, tokens, step):
    return pl.multiple_of(lax.rem(col_ref[0] - step + blocks, blocks) * tokens, tokens)


def in_order(col_ref, refs, held):
    tokens = refs[0].shape[0]
    for step, ref in enumerate(refs):
        held[pl.ds(place_of(col_ref, len(refs), tokens, step), tokens), :] = ref[...].astype(held.dtype)


def out_of_order(col_ref, held, refs):
    tokens = refs[0].shape[0]
    for step, ref in enumerate(refs):
        ref[...] = held[pl.ds(place_of(col_ref, len(refs), tokens, step), tokens), :].astype(ref.dtype)


def scores_of(keys, query, first, scale):
    count = query.shape[0]
    scores = dot_nt(keys[pl.ds(0, first + count), :], query) * (scale * math.log2(math.e))
    row = lax.broadcasted_iota(jnp.int32, (count, count), 0)
    column = lax.broadcasted_iota(jnp.int32, (count, count), 1)
    last = jnp.where(row <= column, scores[first:], -1e30)
    return jnp.concatenate([scores[:first], last], axis=0) if first else last


def prepare_keys(col_ref, k_refs, v_refs, cos_ref, sin_ref, kg_ref, raw_rows, keys, values):
    in_order(col_ref, k_refs, raw_rows)
    in_order(col_ref, v_refs, values)
    tokens = k_refs[0].shape[0]
    for block in range(len(k_refs)):
        there = pl.ds(block * tokens, tokens)
        raw = raw_rows[there, :]
        rows = raw * inverse_rms(raw) * kg_ref[...]
        keys[there, :] = turn(rows, cos_ref[there, :], sin_ref[there, :]).astype(bf16)


def forward_kernel(blocks, scale, col_ref, *refs):
    q_refs, k_refs, v_refs = refs[:blocks], refs[blocks : 2 * blocks], refs[2 * blocks : 3 * blocks]
    cos_ref, sin_ref, qg_ref, kg_ref = refs[3 * blocks : 3 * blocks + 4]
    out_refs = refs[3 * blocks + 4 : 4 * blocks + 4]
    level_ref, raw_rows, keys, values, mixed_rows = refs[4 * blocks + 4 :]
    tokens = q_refs[0].shape[0]

    @pl.when(pl.program_id(0) == 0)
    def _():
        prepare_keys(col_ref, k_refs, v_refs, cos_ref, sin_ref, kg_ref, raw_rows, keys, values)

    in_order(col_ref, q_refs, raw_rows)
    for block in range(blocks):
        first = block * tokens
        there = pl.ds(first, tokens)
        raw = raw_rows[there, :]
        rows = raw * inverse_rms(raw) * qg_ref[...]
        query = turn(rows, cos_ref[there, :], sin_ref[there, :]).astype(bf16)
        scores = scores_of(keys, query, first, scale)
        peak = jnp.max(scores, axis=0, keepdims=True)
        probs = jnp.exp2(scores - peak)
        total = jnp.sum(probs, axis=0, keepdims=True)
        level_ref[0, :, there] = peak + jnp.log2(total)
        probs = (probs * (1.0 / total)).astype(bf16)
        mixed_rows[there, :] = dot_tn(probs, values[pl.ds(0, first + tokens), :]).astype(bf16)
    out_of_order(col_ref, mixed_rows, out_refs)


def attention_forward(col, qkv, cosine, sine, query_gain, key_gain, heads):
    blocks, tokens, head_size = len(qkv), qkv[0].shape[0], query_gain.shape[-1]
    seq_len = blocks * tokens
    column = lambda index: [pl.BlockSpec((tokens, head_size), index)] * blocks
    whole = pl.BlockSpec((seq_len, head_size), lambda h, c: (0, 0))
    gain = pl.BlockSpec((1, head_size), lambda h, c: (0, 0))
    return pl.pallas_call(
        functools.partial(forward_kernel, blocks, head_size ** (-0.5)),
        out_shape=[
            *[jax.ShapeDtypeStruct((tokens, heads * head_size), bf16)] * blocks,
            jax.ShapeDtypeStruct((heads, 1, seq_len), f32),
        ],
        grid_spec=pltpu.PrefetchScalarGridSpec(
            num_scalar_prefetch=1,
            grid=(heads,),
            in_specs=[
                *column(lambda h, c: (0, h)),
                *column(lambda h, c: (0, heads)),
                *column(lambda h, c: (0, heads + 1)),
                whole,
                whole,
                gain,
                gain,
            ],
            out_specs=[
                *column(lambda h, c: (0, h)),
                pl.BlockSpec((1, 1, seq_len), lambda h, c: (h, 0, 0)),
            ],
            scratch_shapes=[
                pltpu.VMEM((seq_len, head_size), f32),
                pltpu.VMEM((seq_len, head_size), bf16),
                pltpu.VMEM((seq_len, head_size), bf16),
                pltpu.VMEM((seq_len, head_size), bf16),
            ],
        ),
        compiler_params=pltpu.CompilerParams(vmem_limit_bytes=60 * 2**20),
        cost_estimate=pl.CostEstimate(flops=1000, bytes_accessed=1000, transcendentals=0),
        name="attention_forward",
    )(col, *qkv, *qkv, *qkv, cosine, sine, query_gain, key_gain)


def backward_kernel(blocks, scale, first_head, heads, final, col_ref, *refs):
    q_refs, k_refs, v_refs, g_refs = (refs[i * blocks : (i + 1) * blocks] for i in range(4))
    cos_ref, sin_ref, qg_ref, kg_ref, level_ref = refs[4 * blocks : 4 * blocks + 5]
    refs = refs[4 * blocks + 5 :]
    if first_head:
        refs = refs[blocks:]
        held_refs, refs = refs[:4], refs[4:]
    grad_refs, refs = refs[:blocks], refs[blocks:]
    qgain_ref, kgain_ref, out_keys, out_values = refs[:4]
    raw_rows, mixed_rows, keys, values, grad_rows, grad_keys, grad_values = refs[4:]
    tokens = q_refs[0].shape[0]
    step = pl.program_id(0)

    @pl.when(step == 0)
    def _():
        prepare_keys(col_ref, k_refs, v_refs, cos_ref, sin_ref, kg_ref, raw_rows, keys, values)
        if first_head:
            qgain_ref[...] = held_refs[0][...]
            kgain_ref[...] = held_refs[1][...]
            grad_keys[...] = held_refs[2][...]
            grad_values[...] = held_refs[3][...]
        else:
            grad_keys[...] = jnp.zeros_like(grad_keys)
            grad_values[...] = jnp.zeros_like(grad_values)
            qgain_ref[...] = jnp.zeros_like(qgain_ref)
            kgain_ref[...] = jnp.zeros_like(kgain_ref)

    def through_norm(grad_rot, unit, inverse, there, gain_ref, gain_grad_ref):
        grad_scaled = turn_back(grad_rot, cos_ref[there, :], sin_ref[there, :])
        gain_grad_ref[0:1, :] += jnp.sum(grad_scaled * unit, axis=0, keepdims=True)
        grad_unit = grad_scaled * gain_ref[...]
        return inverse * (grad_unit - unit * jnp.mean(grad_unit * unit, axis=1, keepdims=True))

    @pl.when(step < heads)
    def _():
        in_order(col_ref, q_refs, raw_rows)
        in_order(col_ref, g_refs, mixed_rows)
        for block in range(blocks):
            first = block * tokens
            there = pl.ds(first, tokens)
            raw = raw_rows[there, :]
            inverse = inverse_rms(raw)
            unit = raw * inverse
            query = turn(unit * qg_ref[...], cos_ref[there, :], sin_ref[there, :]).astype(bf16)
            grad_mixed = mixed_rows[there, :]
            upto = pl.ds(0, first + tokens)
            probs = jnp.exp2(scores_of(keys, query, first, scale) - level_ref[0, :, there])
            grad_probs = dot_nt(values[upto, :], grad_mixed)
            inner = jnp.sum(probs * grad_probs, axis=0, keepdims=True)
            grad_scores = (probs * (grad_probs - inner)).astype(bf16)
            grad_values[upto, :] += dot_nn(probs.astype(bf16), grad_mixed)
            grad_keys[upto, :] += dot_nn(grad_scores, query)
            grad_query = dot_tn(grad_scores, keys[upto, :])
            grad_rows[there, :] = through_norm(
                grad_query * scale, unit, inverse, there, qg_ref, qgain_ref
            ).astype(bf16)

    if not final:

        @pl.when(step == heads - 1)
        def _():
            out_keys[...] = grad_keys[...]
            out_values[...] = grad_values[...]

    @pl.when(step == heads)
    def _():
        in_order(col_ref, k_refs, raw_rows)
        for block in range(blocks):
            there = pl.ds(block * tokens, tokens)
            raw = raw_rows[there, :]
            inverse = inverse_rms(raw)
            grad_rows[there, :] = through_norm(
                grad_keys[there, :] * scale, raw * inverse, inverse, there, kg_ref, kgain_ref
            ).astype(bf16)

    @pl.when(step == heads + 1)
    def _():
        grad_rows[...] = grad_values[...].astype(bf16)

    out_of_order(col_ref, grad_rows, grad_refs)


def attention_backward(
    col, qkv, grad_attended, cosine, sine, query_gain, key_gain, levels, first, heads, former=None
):
    blocks, tokens, head_size = len(qkv), qkv[0].shape[0], query_gain.shape[-1]
    seq_len = blocks * tokens
    all_heads = levels.shape[0]
    final = first + heads == all_heads
    column = lambda index: [pl.BlockSpec((tokens, head_size), index)] * blocks
    whole = pl.BlockSpec((seq_len, head_size), lambda h, c: (0, 0))
    gain = pl.BlockSpec((1, head_size), lambda h, c: (0, 0))
    gain_out = pl.BlockSpec((8, head_size), lambda h, c: (0, 0))
    last = all_heads - 1
    held = [] if former is None else former
    return pl.pallas_call(
        functools.partial(backward_kernel, blocks, head_size ** (-0.5), first, heads, final),
        out_shape=[
            *[jax.ShapeDtypeStruct(qkv[0].shape, bf16)] * blocks,
            jax.ShapeDtypeStruct((8, head_size), f32),
            jax.ShapeDtypeStruct((8, head_size), f32),
            jax.ShapeDtypeStruct((seq_len, head_size), f32),
            jax.ShapeDtypeStruct((seq_len, head_size), f32),
        ],
        grid_spec=pltpu.PrefetchScalarGridSpec(
            num_scalar_prefetch=1,
            grid=(heads + 2 if final else heads,),
            in_specs=[
                *column(lambda h, c: (0, jnp.minimum(h + first, last))),
                *column(lambda h, c: (0, all_heads)),
                *column(lambda h, c: (0, all_heads + 1)),
                *column(lambda h, c: (0, jnp.minimum(h + first, last))),
                whole,
                whole,
                gain,
                gain,
                pl.BlockSpec((1, 1, seq_len), lambda h, c: (jnp.minimum(h + first, last), 0, 0)),
                *([] if former is None else [pl.BlockSpec(memory_space=pl.ANY)] * blocks),
                *([] if former is None else [gain_out, gain_out, whole, whole]),
            ],
            out_specs=[*column(lambda h, c: (0, h + first)), gain_out, gain_out, whole, whole],
            scratch_shapes=[
                pltpu.VMEM((seq_len, head_size), f32),
                pltpu.VMEM((seq_len, head_size), bf16),
                pltpu.VMEM((seq_len, head_size), bf16),
                pltpu.VMEM((seq_len, head_size), bf16),
                pltpu.VMEM((seq_len, head_size), bf16),
                pltpu.VMEM((seq_len, head_size), f32),
                pltpu.VMEM((seq_len, head_size), f32),
            ],
        ),
        input_output_aliases={} if former is None else {1 + 4 * blocks + 5 + i: i for i in range(blocks)},
        compiler_params=pltpu.CompilerParams(vmem_limit_bytes=60 * 2**20),
        cost_estimate=pl.CostEstimate(flops=1000, bytes_accessed=1000, transcendentals=0),
        name="attention_backward",
    )(col, *qkv, *qkv, *qkv, *grad_attended, cosine, sine, query_gain, key_gain, levels, *held)


def weight_kernel(blocks, rights, weighted, *refs):
    left_refs, refs = refs[:blocks], refs[blocks:]
    right_refs, refs = refs[: blocks * rights], refs[blocks * rights :]
    if weighted:
        weight_refs, refs = refs[:blocks], refs[blocks:]
        out_refs, held = refs[:rights], refs[rights:]

        @pl.when(pl.program_id(0) == 0)
        def _():
            for index, ref in enumerate(right_refs):
                scaled = ref[...].astype(f32) * weight_refs[index % blocks][...]
                held[index][...] = scaled.astype(bf16)

        right_refs = held
    else:
        out_refs = refs
    for index, out_ref in enumerate(out_refs):
        total = dot_tn(left_refs[0][...], right_refs[index * blocks][...])
        for block in range(1, blocks):
            total = total + dot_tn(left_refs[block][...], right_refs[index * blocks + block][...])
        out_ref[...] = total.astype(out_ref.dtype)


def weight_gradients(lefts, rights, out_type, weights=None, tile=256):
    blocks, rows, tall = len(lefts), lefts[0].shape[0], lefts[0].shape[1]
    flat = [block for right in rights for block in right]
    fixed = lambda array: pl.BlockSpec(array.shape, lambda i: (0, 0))
    return pl.pallas_call(
        functools.partial(weight_kernel, blocks, len(rights), weights is not None),
        out_shape=[jax.ShapeDtypeStruct((tall, right[0].shape[1]), out_type) for right in rights],
        grid=(tall // tile,),
        in_specs=[
            *[pl.BlockSpec((rows, tile), lambda i: (0, i))] * blocks,
            *[fixed(block) for block in flat],
            *([] if weights is None else [fixed(weight) for weight in weights]),
        ],
        out_specs=[
            pl.BlockSpec((tile, right[0].shape[1]), lambda i: (i, 0)) for right in rights
        ],
        scratch_shapes=[] if weights is None else [pltpu.VMEM(block.shape, bf16) for block in flat],
        compiler_params=pltpu.CompilerParams(vmem_limit_bytes=60 * 2**20),
        cost_estimate=pl.CostEstimate(flops=1000, bytes_accessed=1000, transcendentals=0),
        name="weight_gradients",
    )(*lefts, *flat, *([] if weights is None else weights))


def split_kernel(blocks, groups, mine_ref, *refs):
    left_refs, right_refs, out_refs = refs[:blocks], refs[blocks : 2 * blocks], refs[2 * blocks :]
    total = dot_tn(left_refs[0][...], right_refs[0][...])
    for block in range(1, blocks):
        total = total + dot_tn(left_refs[block][...], right_refs[block][...])
    for index, out_ref in enumerate(out_refs):

        @pl.when(pl.program_id(0) // groups == index)
        def _():
            out_ref[...] = total.astype(out_ref.dtype)


def split_gradient(lefts, right, mine, devices, groups):
    blocks, rows, tall = len(lefts), lefts[0].shape[0], lefts[0].shape[1]
    tile, wide = tall // (devices * groups), right[0].shape[1]

    def left_tile(i, mine_ref):
        return (0, i % groups * devices + lax.rem(mine_ref[0] + i // groups, devices))

    def out_tile(index):
        return lambda i, mine_ref: (jnp.clip(i - index * groups, 0, groups - 1), 0)

    return pl.pallas_call(
        functools.partial(split_kernel, blocks, groups),
        out_shape=[jax.ShapeDtypeStruct((groups * tile, wide), bf16)] * devices,
        grid_spec=pltpu.PrefetchScalarGridSpec(
            num_scalar_prefetch=1,
            grid=(devices * groups,),
            in_specs=[
                *[pl.BlockSpec((rows, tile), left_tile)] * blocks,
                *[pl.BlockSpec((rows, wide), lambda i, mine_ref: (0, 0))] * blocks,
            ],
            out_specs=[pl.BlockSpec((tile, wide), out_tile(index)) for index in range(devices)],
        ),
        compiler_params=pltpu.CompilerParams(vmem_limit_bytes=60 * 2**20),
        cost_estimate=pl.CostEstimate(flops=1000, bytes_accessed=1000, transcendentals=0),
        name="split_gradient",
    )(mine, *lefts, *right)


def spread_kernel(with_units, *refs):
    block_refs, weight_ref, refs = refs[:4], refs[4], refs[5:]
    if with_units:
        unit_refs, refs = refs[:4], refs[4:]
    far_up, far_down, free_up, free_down, up_rest, down_rest, own_ref = refs[:7]
    weight = weight_ref[...]
    middle = own_ref.shape[0] // 2
    shares = {}
    for step in (2, 3, 1, 0):
        shares[step] = dot_nt(block_refs[step][...], weight)
    far_up[...] = shares[2][:middle].astype(bf16)
    far_down[...] = shares[2][middle:].astype(bf16)
    free_up[...] = shares[3][middle:].astype(bf16)
    free_down[...] = shares[1][:middle].astype(bf16)
    up_rest[...] = shares[3][:middle]
    down_rest[...] = shares[1][middle:]
    own_ref[...] = shares[0]
    if with_units:
        total = sum(
            jnp.sum(shares[step] * unit_refs[step][...], axis=0, keepdims=True) for step in range(4)
        )
        refs[7][...] = jnp.broadcast_to(total, refs[7].shape)


def spread(blocks, weight, units=None, tile=512):
    tokens, depth = blocks[0].shape
    width = weight.shape[0]
    part = lambda rows: pl.BlockSpec((rows, tile), lambda i: (0, i))
    shape = jax.ShapeDtypeStruct
    return pl.pallas_call(
        functools.partial(spread_kernel, units is not None),
        out_shape=[
            *[shape((tokens // 2, width), bf16)] * 4,
            *[shape((tokens // 2, width), f32)] * 2,
            shape((tokens, width), f32),
            *([] if units is None else [shape((8, width), f32)]),
        ],
        grid=(width // tile,),
        in_specs=[
            *[pl.BlockSpec((tokens, depth), lambda i: (0, 0))] * 4,
            pl.BlockSpec((tile, depth), lambda i: (i, 0)),
            *([] if units is None else [part(tokens)] * 4),
        ],
        out_specs=[
            *[part(tokens // 2)] * 6,
            part(tokens),
            *([] if units is None else [part(8)]),
        ],
        compiler_params=pltpu.CompilerParams(vmem_limit_bytes=60 * 2**20),
        cost_estimate=pl.CostEstimate(flops=1000, bytes_accessed=1000, transcendentals=0),
        name="spread",
    )(*blocks, weight, *([] if units is None else units))


def product_kernel(transposed, left_ref, right_ref, *refs):
    result = (dot_tn if transposed else dot_nn)(left_ref[...], right_ref[...])
    if len(refs) > 1:
        result = result + refs[0][...].astype(f32)
    refs[-1][...] = result.astype(refs[-1].dtype)


def product(left, right, addend=None, out_type=bf16, transposed=False, tile=512):
    rows = left.shape[1 if transposed else 0]
    part = lambda height: pl.BlockSpec((height, tile), lambda i: (0, i))
    return pl.pallas_call(
        functools.partial(product_kernel, transposed),
        out_shape=jax.ShapeDtypeStruct((rows, right.shape[1]), out_type),
        grid=(right.shape[1] // tile,),
        in_specs=[
            pl.BlockSpec(left.shape, lambda i: (0, 0)),
            part(right.shape[0]),
            *([] if addend is None else [part(rows)]),
        ],
        out_specs=part(rows),
        compiler_params=pltpu.CompilerParams(vmem_limit_bytes=60 * 2**20),
        cost_estimate=pl.CostEstimate(flops=1000, bytes_accessed=1000, transcendentals=0),
        name="product",
    )(left, right, *([] if addend is None else [addend]))


def expert_kernel(
    rows_ref, upstream_ref, gate_ref, up_ref, down_ref,
    acted_ref, gate_grad_ref, up_grad_ref, row_grad_ref, returned_ref, dots_ref,
    gates, ups, downs, gate_grads, up_grads, acted_rows,
):
    step = pl.program_id(0)
    tile = gate_ref.shape[1]
    gate_part = dot_nn(rows_ref[...], gate_ref[...])
    up_part = dot_nn(rows_ref[...], up_ref[...])
    drive = dot_nt(upstream_ref[...], down_ref[...])
    sigmoid = jax.nn.sigmoid(gate_part)
    silu = gate_part * sigmoid
    acted = silu * up_part
    acted_low = acted.astype(bf16)
    gate_grad = (drive * up_part * sigmoid * (1.0 + gate_part * (1.0 - sigmoid))).astype(bf16)
    up_grad = (drive * silu).astype(bf16)
    acted_ref[...] = acted_low
    gate_grad_ref[...] = gate_grad
    up_grad_ref[...] = up_grad
    dots = jnp.sum(acted * drive, axis=1, keepdims=True)
    for index in range(gates.shape[1] // tile):

        @pl.when(step == index)
        def _():
            here = pl.ds(index * tile, tile)
            gates[:, here] = gate_ref[...]
            ups[:, here] = up_ref[...]
            downs[here, :] = down_ref[...]
            gate_grads[:, here] = gate_grad
            up_grads[:, here] = up_grad
            acted_rows[:, here] = acted_low

    @pl.when(step == 0)
    def _():
        dots_ref[...] = dots

    @pl.when(step > 0)
    def _():
        dots_ref[...] += dots

    @pl.when(step == pl.num_programs(0) - 1)
    def _():
        for first in range(0, row_grad_ref.shape[1], 512):
            here = pl.ds(first, 512)
            row_grad_ref[:, here] = (
                dot_nt(gate_grads[...], gates[here, :]) + dot_nt(up_grads[...], ups[here, :])
            ).astype(bf16)
            returned_ref[:, here] = dot_nn(acted_rows[...], downs[:, here]).astype(bf16)


def expert_block(rows, upstream_rows, gate_weight, up_weight, down_weight, tile=256):
    count, width = rows.shape
    hidden = gate_weight.shape[1]
    shape = jax.ShapeDtypeStruct
    whole = pl.BlockSpec((count, width), lambda j: (0, 0))
    part = pl.BlockSpec((count, tile), lambda j: (0, j))
    return pl.pallas_call(
        expert_kernel,
        out_shape=[
            shape((count, hidden), bf16),
            shape((count, hidden), bf16),
            shape((count, hidden), bf16),
            shape((count, width), bf16),
            shape((count, width), bf16),
            shape((count, 1), f32),
        ],
        grid=(hidden // tile,),
        in_specs=[
            whole,
            whole,
            pl.BlockSpec((width, tile), lambda j: (0, j)),
            pl.BlockSpec((width, tile), lambda j: (0, j)),
            pl.BlockSpec((tile, width), lambda j: (j, 0)),
        ],
        out_specs=[part, part, part, whole, whole, pl.BlockSpec((count, 1), lambda j: (0, 0))],
        scratch_shapes=[
            pltpu.VMEM((width, hidden), bf16),
            pltpu.VMEM((width, hidden), bf16),
            pltpu.VMEM((hidden, width), bf16),
            pltpu.VMEM((count, hidden), bf16),
            pltpu.VMEM((count, hidden), bf16),
            pltpu.VMEM((count, hidden), bf16),
        ],
        compiler_params=pltpu.CompilerParams(vmem_limit_bytes=60 * 2**20),
        cost_estimate=pl.CostEstimate(flops=1000, bytes_accessed=1000, transcendentals=0),
        name="expert_block",
    )(rows, upstream_rows, gate_weight, up_weight, down_weight)


def local(
    inputs,
    expert_ids,
    positions,
    cotangent,
    attn_gain,
    query_proj,
    key_projection,
    value_projection,
    query_norm_gain,
    key_norm_gain,
    out_proj,
    moe_gain,
    router,
    gate_proj,
    up_proj,
    down_proj,
):
    tokens, width = inputs.shape
    head_size = query_norm_gain.shape[0]
    choices = expert_ids.shape[1]
    experts = router.shape[1]
    capacity = tokens * choices * 5 // (4 * experts)
    columns = lax.axis_size("col")
    peers = lax.axis_size("dp") * lax.axis_size("exp")
    col = lax.axis_index("col")
    here = lax.axis_index("dp") * lax.axis_size("exp") + lax.axis_index("exp")
    col_array = jnp.reshape(col, (1,)).astype(jnp.int32)
    heads = query_proj.shape[1] // head_size
    assert key_projection.shape[1] == head_size and experts == peers * columns
    assert columns == 4 and tokens % 32 == 0
    middle = tokens // 2

    def shifted(block, by):
        return lax.ppermute(block, "col", [(i, (i + by) % columns) for i in range(columns)])

    def up(block):
        return shifted(block, 1)

    def down(block):
        return shifted(block, -1)

    def gather_near(block):
        return up(block), down(block)

    def gather_far(former, latter):
        return up(former[:middle]), down(latter[middle:])

    def scatter_second(rest, far):
        return (rest + far.astype(f32)).astype(bf16)

    def scatter_own(own, second_up, second_down, free_up, free_down):
        return own + jnp.concatenate(
            [
                second_up.astype(f32) + free_down.astype(f32),
                free_up.astype(f32) + second_down.astype(f32),
            ],
            axis=0,
        )

    def swap(rows):
        return lax.all_to_all(
            rows.reshape(peers, rows.shape[0] // peers, *rows.shape[1:]), plane, 0, 0, tiled=True
        ).reshape(rows.shape)

    def swap_all(values):
        return lax.all_to_all(values, everyone, 0, 0, tiled=True)

    def after(value, *others):
        return lax.optimization_barrier((value, others))[0]

    def exchange_plane(values, steps):
        parts = {}
        for step in steps:
            part = lax.dynamic_index_in_dim(values, lax.rem(here + step, peers), 0, keepdims=False)
            pairs = [(i, (i + step) % peers) for i in range(peers)]
            parts[step] = lax.ppermute(part, plane, pairs) if step else part
        return parts

    def joined(parts):
        order = lax.rem(here - jnp.arange(peers, dtype=jnp.int32) + peers, peers)
        return jnp.take(jnp.stack([parts[step] for step in range(peers)]), order, axis=0)

    early_steps, late_steps = range(peers // 2), range(peers // 2, peers)

    def exchange_columns(values):
        parts = [values[:, 0], *[shifted(values[:, s], -s) for s in range(1, columns)]]
        return jnp.stack([parts[0], *parts[:0:-1]], axis=1)

    to_ring = lax.rem(col - jnp.arange(columns, dtype=jnp.int32) + columns, columns)

    earlier = (
        lax.broadcasted_iota(jnp.int32, (tokens, tokens), 0)
        < lax.broadcasted_iota(jnp.int32, (tokens, tokens), 1)
    ).astype(bf16)
    all_experts = jnp.arange(experts, dtype=jnp.int32)
    plane_experts = jnp.arange(peers, dtype=jnp.int32) * columns + col

    def chosen_in(ids, named):
        return jnp.any(ids[None, :, :] == named[:, None, None], axis=1)

    def slots_of(ids, named):
        chosen = chosen_in(ids, named)
        rank = dot_nn(chosen.astype(bf16), earlier)
        code = jnp.where(chosen, rank, -1.0)
        place = lax.broadcasted_iota(jnp.int32, (1, capacity, 1), 1).astype(f32)
        return chosen, code[:, None, :] == place

    def slot_mat(ids):
        return slots_of(ids, plane_experts)[1].astype(bf16).reshape(peers * capacity, tokens)

    def pick(step, block):
        return product(slot_mats[step], block)

    def gates_of(chosen, block):
        logits = jnp.where(chosen, dot_general_t(router, block), -1e30)
        exponent = jnp.exp(logits - jnp.max(logits, axis=0, keepdims=True))
        exponent = jnp.where(chosen, exponent, 0.0)
        return exponent / jnp.sum(exponent, axis=0, keepdims=True)

    def weighted_mat(step, block_gates):
        gates_here = block_gates.reshape(peers, columns, 1, tokens)
        gates_here = lax.dynamic_index_in_dim(gates_here, col, 1, keepdims=False)
        mat = slot_mats[step].reshape(peers, capacity, tokens) * gates_here
        return mat.astype(bf16).reshape(peers * capacity, tokens)

    def collect(back, step, addend=None, out_type=bf16):
        return product(weighted_mats[step], back[step], addend, out_type, transposed=True)

    near_inputs = gather_near(inputs)
    local_qkv = jnp.concatenate([query_proj, key_projection, value_projection], axis=1)
    full_qkv = lax.all_gather(local_qkv, "exp", axis=0, tiled=True)
    full_out = lax.all_gather(out_proj, "exp", axis=0, tiled=True)
    own_ids = expert_ids.T
    slot_mats = [slot_mat(own_ids)]
    cotangent_rows = [swap(pick(0, cotangent)), None, None, None]
    near_inputs, full_qkv = after((near_inputs, full_qkv))

    far_inputs = jnp.concatenate(gather_far(*near_inputs), axis=0)
    def project(block):
        rows = block.astype(f32)
        unit = rows * inverse_rms(rows)
        low = (unit * attn_gain).astype(bf16)
        return unit, low, dot_nn(low, full_qkv)

    projected = [project(inputs), project(near_inputs[0]), None, project(near_inputs[1])]
    cosine, sine = rotary_tables(positions, head_size)
    far_inputs, cotangent_rows[0], cosine, sine = after(
        (far_inputs, cotangent_rows[0], cosine, sine),
        [projected[s][2] for s in (0, 1, 3)],
    )

    near_cotangent = gather_near(after(cotangent, far_inputs))
    later_ids = after(own_ids, far_inputs)
    ids_blocks = [own_ids, *[shifted(later_ids, step) for step in range(1, columns)]]
    projected[2] = project(far_inputs)
    units, normed, qkv = zip(*projected)
    query_gain, key_gain = query_norm_gain[None, :], key_norm_gain[None, :]
    *attended, levels = attention_forward(col_array, qkv, cosine, sine, query_gain, key_gain, heads)
    shares = spread(attended, full_out)
    ids_blocks = after(ids_blocks, attended)
    slot_mats += [slot_mat(ids_blocks[s]) for s in (1, 2, 3)]
    picked = pick(1, after(near_cotangent[0], attended))
    near_cotangent, shares, slot_mats, picked = after((near_cotangent, shares, slot_mats, picked))

    send_up, send_down, free_up, free_down, up_rest, down_rest, own_share = shares
    cotangent_rows[1] = swap(picked)
    first_up, first_down = up(send_up), down(send_down)
    far_up = up(near_cotangent[0][:middle])
    chosen_all, slots_all = slots_of(own_ids, all_experts)
    picked = pick(3, near_cotangent[1])
    late_half = near_cotangent[1][middle:]
    first_up, first_down, far_up, cotangent_rows[1], chosen_all, slots_all, picked, late_half, frees = after(
        (
            first_up, first_down, far_up, cotangent_rows[1], chosen_all, slots_all, picked, late_half,
            (free_up, free_down),
        )
    )
    cotangent_rows[3] = swap(picked)
    far_down = down(late_half)
    second_up = up(scatter_second(up_rest, first_up))
    second_down = down(scatter_second(down_rest, first_down))
    picked = pick(2, jnp.concatenate([far_up, far_down], axis=0))
    second_up, second_down, picked, cotangent_rows[3], frees = after(
        (second_up, second_down, picked, cotangent_rows[3], frees)
    )

    free_up, free_down = up(frees[0]), down(frees[1])
    cotangent_rows[2] = swap(picked)
    gate_weight, up_weight, down_weight = gate_proj[0], up_proj[0], down_proj[0]
    hidden = inputs.astype(f32) + scatter_own(own_share, second_up, second_down, free_up, free_down)
    inverse_hidden = inverse_rms(hidden)
    routed = (hidden * inverse_hidden * moe_gain).astype(bf16)
    own_rows = after(pick(0, routed), cotangent_rows[2])

    acted_rows, gate_grads, up_grads, row_grads, returned, gate_dots = [], [], [], [], [], []

    def run_expert(step, rows):
        results = expert_block(rows, cotangent_rows[step], gate_weight, up_weight, down_weight)
        for held, result in zip((acted_rows, gate_grads, up_grads, row_grads, returned), results):
            held.append(result)
        gate_dots.append(results[5].reshape(peers, capacity))

    def block_mat(step):
        block_gates = gates_of(chosen_in(ids_blocks[step], all_experts), routed_blocks[step])
        return weighted_mat(step, block_gates)

    routed_blocks, arrived, weighted_mats = [routed], [], {}
    rows, next_rows = own_rows, None
    slot_parts = {}
    for step in range(columns):
        rows = swap(rows)
        coming = None
        if step < columns - 1:
            coming = up(routed_blocks[step])
            next_rows = pick(step + 1, coming)
        if step:
            run_expert(step - 1, arrived[step - 1])
        if step == 0:
            gates = gates_of(chosen_all, routed)
            gate_slots = jnp.sum(jnp.where(slots_all, gates[:, None, :], 0.0), axis=2)
            gate_slots = jnp.take(gate_slots.reshape(peers, columns, capacity), to_ring, axis=1)
            weighted_mats[0] = weighted_mat(0, gates)
            slot_parts = exchange_plane(gate_slots, early_steps)
        elif step == 1:
            slot_parts.update(exchange_plane(gate_slots, late_steps))
        elif step == 2:
            gate_slots = exchange_columns(joined(slot_parts))
            slot_parts = {}
        state = (rows, next_rows, coming, gate_slots, weighted_mats, slot_parts)
        rows, next_rows, coming, gate_slots, weighted_mats, slot_parts = after(state, row_grads)
        arrived.append(rows)
        routed_blocks.append(coming)
        rows = next_rows
    row_weights = [gate_slots[:, step].reshape(peers * capacity, 1) for step in range(columns)]

    row_grads = after(row_grads, arrived[3])
    grad_back = {1: swap(row_grads[1])}
    run_expert(3, arrived[3])
    weighted_mats[1] = block_mat(1)
    grad_back[1], row_grads, gate_dots, weighted_mats = after(
        (grad_back[1], row_grads, gate_dots, weighted_mats)
    )
    grad_back[2] = swap(row_grads[2])
    running = up(collect(grad_back, 1))
    dots = jnp.stack(gate_dots, axis=1)
    dot_parts = exchange_plane(dots, early_steps)
    weighted_mats[2] = block_mat(2)
    running, grad_back[2], dot_parts, weighted_mats = after(
        (running, grad_back[2], dot_parts, weighted_mats)
    )
    grad_back[3] = swap(after(row_grads[3], running))
    running = up(collect(grad_back, 2, running))
    dot_parts.update(exchange_plane(after(dots, grad_back[2]), late_steps))
    weighted_mats[3] = block_mat(3)
    running, grad_back[3], dot_parts, weighted_mats = after(
        (running, grad_back[3], dot_parts, weighted_mats)
    )
    grad_back[0] = swap(after(row_grads[0], running))
    running = up(collect(grad_back, 3, running))
    dots = jnp.take(exchange_columns(joined(dot_parts)), to_ring, axis=1).reshape(experts, capacity)
    running, grad_back[0], dots = after((running, grad_back[0], dots))

    grad_gates = jnp.sum(jnp.where(slots_all, dots[:, :, None], 0.0), axis=1)
    grad_logits = (
        gates * (grad_gates - jnp.sum(gates * grad_gates, axis=0, keepdims=True))
    ).astype(bf16)
    grad_routed = collect(grad_back, 0, running, f32) + lax.dot_general(
        grad_logits, router, (((0,), (1,)), ((), ())), preferred_element_type=f32
    )
    scaled = grad_routed * moe_gain
    grad_hidden = (
        cotangent.astype(f32)
        + scaled * inverse_hidden
        - hidden * (jnp.mean(hidden * scaled, axis=-1, keepdims=True) * inverse_hidden**3)
    )
    grad_moe_gain = jnp.sum(grad_routed * hidden * inverse_hidden, axis=0)
    grad_router = dot_general_t(routed, grad_logits)

    grad_low = grad_hidden.astype(bf16)
    near_gradient = gather_near(grad_low)
    output_back = {1: swap(after(returned[1], grad_back[0]))}
    grad_attended = {0: product(grad_low, full_out)}
    grad_gate_weight, grad_up_weight = weight_gradients(
        after(arrived, grad_low), [gate_grads, up_grads], f32, row_weights
    )
    near_gradient, grad_gate_weight, grad_attended = after(
        (near_gradient, grad_gate_weight, grad_attended)
    )

    far_gradient = gather_far(*near_gradient)
    output_back[2] = swap(after(returned[2], output_back[1], grad_low))
    grad_attended.update({1: product(near_gradient[0], full_out), 3: product(near_gradient[1], full_out)})
    output_part = collect(output_back, 1)
    far_gradient = jnp.concatenate(after(far_gradient, output_part), axis=0)
    router_sums = grad_router.reshape(1, columns, width // columns * experts)
    router_sums = jnp.take(after(router_sums, near_gradient), to_ring, axis=1)
    router_sums = jnp.sum(exchange_columns(router_sums)[0], axis=0)
    far_gradient, grad_attended, output_part, router_sums = after(
        (far_gradient, grad_attended, output_part, router_sums)
    )

    grad_sequence = [grad_low, near_gradient[0], far_gradient, near_gradient[1]]
    running = up(output_part)
    output_back[3] = swap(after(returned[3], output_back[2]))
    grad_attended[2] = product(far_gradient, full_out)
    grad_attended = [grad_attended[s] for s in range(columns)]
    half = heads // 2
    arguments = (col_array, qkv, grad_attended, cosine, sine, query_gain, key_gain, levels)
    dp, exp = lax.axis_size("dp"), lax.axis_size("exp")
    tile = width // (dp * exp)

    def weight_parts(lefts, right):
        mine = lax.axis_index("exp")
        if tile % 128 == 0:
            return split_gradient(lefts, right, jnp.reshape(mine, (1,)).astype(jnp.int32), exp, dp)
        (grads,) = weight_gradients(lefts, [right], bf16)
        grads = grads.reshape(dp, exp, tile, -1).transpose(1, 0, 2, 3).reshape(exp, dp * tile, -1)
        return [
            lax.dynamic_index_in_dim(grads, lax.rem(mine + step, exp), 0, keepdims=False)
            for step in range(exp)
        ]

    def exchange_parts(parts):
        return [
            lax.ppermute(part, "exp", [(i, (i + step) % exp) for i in range(exp)]) if step else part
            for step, part in enumerate(parts)
        ]

    def sum_of(parts):
        return sum(part.astype(f32) for part in parts).astype(bf16)

    def swap_parts(sums):
        parts = sums.reshape(dp, -1, sums.shape[1])
        return lax.all_to_all(parts, "dp", 0, 0, tiled=True)

    out_parts = exchange_parts(weight_parts(grad_sequence, attended))
    first_half = attention_backward(*arguments, 0, half)
    first_half, running, out_parts = after((first_half, running, out_parts))
    out_sums = sum_of(out_parts)
    out_sums = swap_parts(after(out_sums, output_back[3]))
    output_part = collect(output_back, 2, running)
    running = up(output_part)
    *grad_qkv, grad_query_gain, grad_key_gain, _, _ = attention_backward(
        *arguments, half, heads - half, after(first_half, output_part)
    )
    grad_query_gain, grad_key_gain = grad_query_gain[0], grad_key_gain[0]

    grad_qkv, out_sums = after((grad_qkv, out_sums))
    *shares, attn_gain_sums = spread(grad_qkv, full_qkv, units)
    send_up, send_down, free_up, free_down, up_rest, down_rest, own_share = shares
    first_up, first_down = up(send_up), down(send_down)
    output_part = collect(after(output_back, attn_gain_sums), 3, running)
    (grad_down,) = weight_gradients(
        after(acted_rows, attn_gain_sums), [cotangent_rows], f32, row_weights
    )
    free_up, free_down = up(free_up), down(free_down)
    qkv_parts = weight_parts(normed, after(grad_qkv, attn_gain_sums))
    small = jnp.concatenate([attn_gain_sums[0], grad_query_gain, grad_key_gain, grad_moe_gain])
    cuts = [0, width, width + head_size, width + 2 * head_size, 2 * (width + head_size)]
    small = jnp.concatenate([small, router_sums])
    small = swap(after(jnp.broadcast_to(small, (peers, small.shape[0])), out_sums, first_up))
    output_back[0] = swap(after(returned[0], small))
    first_up, first_down, free_up, free_down, grad_down, output_part, qkv_parts, small = after(
        (first_up, first_down, free_up, free_down, grad_down, output_part, qkv_parts, small)
    )

    second_up = up(scatter_second(up_rest, first_up))
    second_down = down(scatter_second(down_rest, first_down))
    running = up(output_part)
    reduced_out = jnp.sum(out_sums.astype(f32), axis=0)
    qkv_sums = sum_of(exchange_parts(qkv_parts))

    qkv_parts = swap_parts(after(qkv_sums, output_back[0]))
    reduced_qkv = jnp.sum(qkv_parts.astype(f32), axis=0)
    outputs = (hidden + collect(output_back, 0, after(running, qkv_sums), f32)).astype(bf16)
    small = after(jnp.sum(small, axis=0), qkv_sums)
    small = jnp.stack([small, *[shifted(small, step) for step in range(1, columns)]])
    to_true = lax.rem(col - jnp.arange(columns, dtype=jnp.int32) + columns, columns)
    grad_router = jnp.take(small[:, cuts[-1] :], to_true, axis=0).reshape(width, experts)
    small = jnp.sum(small[:, : cuts[-1]], axis=0)
    shared = [small[i:j] for i, j in zip(cuts, cuts[1:])]

    grad_normed = scatter_own(own_share, second_up, second_down, free_up, free_down)
    input_rows = inputs.astype(f32)
    inverse_own = inverse_rms(input_rows)
    scaled_in = grad_normed * attn_gain
    grad_inputs = (
        grad_hidden
        + scaled_in * inverse_own
        - input_rows * (jnp.mean(input_rows * scaled_in, axis=-1, keepdims=True) * inverse_own**3)
    ).astype(bf16)

    split = heads * head_size
    return (
        outputs,
        grad_inputs,
        shared[0],
        reduced_qkv[:, :split],
        reduced_qkv[:, split : split + head_size],
        reduced_qkv[:, split + head_size :],
        shared[1],
        shared[2],
        reduced_out,
        shared[3],
        grad_router,
        grad_gate_weight[None],
        grad_up_weight[None],
        grad_down[None],
    )


def dot_general_t(a, b):
    contract = (((0,), (1,)), ((), ()))
    return lax.dot_general(a, b, contract, preferred_element_type=f32)


def solution(mesh):
    return jax.shard_map(
        local,
        mesh=mesh,
        in_specs=(
            P(("dp", "exp", "col"), None),
            P(("dp", "exp", "col"), None),
            P(("dp", "exp")),
            P(("dp", "exp", "col"), None),
            P(),
            P("exp", "col"),
            P("exp", "col"),
            P("exp", "col"),
            P(),
            P(),
            P("exp", "col"),
            P(),
            P(),
            P(("dp", "exp", "col"), None, None),
            P(("dp", "exp", "col"), None, None),
            P(("dp", "exp", "col"), None, None),
        ),
        out_specs=(
            P(("dp", "exp", "col"), None),
            P(("dp", "exp", "col"), None),
            P(),
            P(("dp", "exp"), "col"),
            P(("dp", "exp"), "col"),
            P(("dp", "exp"), "col"),
            P(),
            P(),
            P(("dp", "exp"), "col"),
            P(),
            P(),
            P(("dp", "exp", "col"), None, None),
            P(("dp", "exp", "col"), None, None),
            P(("dp", "exp", "col"), None, None),
        ),
        check_vma=False,
    )
```
